256 devices in a mesh: tm: 8 (over z_hi, core), space: 32 (over x, z_lo, y).
Axes of the slice: x: 4, y: 4, z: 8 (z_hi: 4, z_lo: 2; z = z_hi * 2 + z_lo), core: 2. Of those that a mesh axis runs over, the one named last changes fastest.
Arguments:
- dual_state: float32 [800, 16, 4, 1024], P('space', 'tm'), may hold values from -6 to 6
- obs_dual: float32 [800, 16, 4, 1024], P('space', 'tm'), may hold values from -6 to 6
- increment: float32 [800, 16, 4, 1024], P('space', 'tm'), may hold values from -6 to 6
- wind_east: float32 [800, 16, 1024], P('space', 'tm'), may hold values from -0.45 to 0.45
- wind_north: float32 [800, 16, 1024], P('space', 'tm'), may hold values from -0.45 to 0.45
- deviation: float32 [800, 4, 1024], P('space'), may hold values from 0.1 to 1
- merid_filter: float32 [800, 800], replicated, may hold values from -1 to 2
- obs_weight: float32 [800, 16, 4, 1024], P('space', 'tm'), may hold values from 0 to 1
- obs_error: float32 [800, 16, 4, 1024], P('space', 'tm'), may hold values from 0.25 to 2.5
Outputs:
- precond_dual: float32 [800, 16, 4, 1024], P('space', 'tm')
- precond_obs: float32 [800, 16, 4, 1024], P('space', 'tm')
- precond_increment: float32 [800, 16, 4, 1024], P('space', 'tm')
The draws below stay inside these ranges and needn't reach their ends.
All inputs are finite; a program needn't handle non-finite values.
Results may differ from the reference program's by a relative error of at most 0.000075.
Values sent between devices are 32-bit elements; how exact they have to be, the bound alone decides.
No kernel may reach another device: no remote copies, remote signals or barrier semaphores. Data moves between devices by JAX's collectives and lax.ppermute only.
A program may use at most 64 MiB of HBM per device.

```python
import math
import jax
import jax.numpy as jnp
from jax import lax

FIELD_LEVELS = 4
NLON = 1024
NLAT = 800
STEPS = 2
NSUB = 16


def draw_merid_filter(key, part):
    key = jax.random.fold_in(key, 11)
    near_key, far_key = jax.random.split(key)
    index = jnp.arange(NLAT)
    distance = jnp.abs(index[:, None] - index[None, :]).astype(jnp.float32)
    noise = jax.random.uniform(near_key, (NLAT, NLAT), jnp.float32, -1.0, 1.0)
    far_noise = jax.random.uniform(far_key, (NLAT, NLAT), jnp.float32, -1.0, 1.0)
    reach = NLAT / 16.0
    distant = 0.15 * far_noise
    filtered = 2.0 * jnp.eye(NLAT, dtype=jnp.float32) + noise * jnp.exp(-distance / reach) + distant
    return filtered / math.sqrt(4.0 + reach / 3.0 + 0.0075 * NLAT)


def block_levels(key, extent, cuts, low, top_value):
    def one(position, blocks):
        heights = jax.random.uniform(jax.random.fold_in(jax.random.fold_in(key, 6), position), (blocks,), jnp.float32, low / len(cuts), top_value / len(cuts))
        return jnp.repeat(jnp.exp(heights), extent[position] // blocks).reshape((-1,) + (1,) * (len(extent) - position - 1))

    factor_of = one(*cuts[0])
    for cut in cuts[1:]:
        factor_of = factor_of * one(*cut)
    return factor_of


def scatter_about(key, dims, width, bound, cuts=(), kind=jnp.bfloat16):
    result = width * jax.random.normal(key, dims, jnp.float32)
    if cuts:
        result = result * block_levels(key, dims, cuts, -0.22, 0.18)
    return jnp.clip(result, -bound, bound).astype(kind)


def setup_inputs(seed: int = 0) -> dict:
    seeds = jax.random.split(jax.random.key(seed), 10)
    return {
        "dual_state": scatter_about(seeds[0], (NLAT, NSUB, FIELD_LEVELS, NLON), 1.0, 6.0, ((0, 32), (1, 8)), jnp.float32),
        "obs_dual": scatter_about(seeds[1], (NLAT, NSUB, FIELD_LEVELS, NLON), 1.0, 6.0, ((0, 32), (1, 8)), jnp.float32),
        "increment": scatter_about(seeds[2], (NLAT, NSUB, FIELD_LEVELS, NLON), 1.0, 6.0, ((0, 32), (1, 8)), jnp.float32),
        "wind_east": jnp.clip(jax.random.uniform(seeds[3], (NLAT, NSUB, NLON), jnp.float32, -0.45, 0.45) * block_levels(seeds[3], (NLAT, NSUB, NLON), ((0, 32), (1, 8)), -0.4, 0.0), -0.45, 0.45),
        "wind_north": jnp.clip(jax.random.uniform(seeds[4], (NLAT, NSUB, NLON), jnp.float32, -0.45, 0.45) * block_levels(seeds[4], (NLAT, NSUB, NLON), ((0, 32), (1, 8)), -0.4, 0.0), -0.45, 0.45),
        "deviation": jnp.clip(jnp.exp(math.log(1.0) - 2.3025851 * jax.random.uniform(seeds[5], (NLAT, FIELD_LEVELS, NLON), jnp.float32) ** block_levels(seeds[5], (NLAT, FIELD_LEVELS, NLON), ((0, 32),), -0.2, 0.2)), 0.1, 1.0),
        "merid_filter": draw_merid_filter(jax.random.fold_in(seeds[9], 71), 0),
        "obs_weight": jnp.clip(1.0 * jax.random.uniform(seeds[7], (NLAT, NSUB, FIELD_LEVELS, NLON), jnp.float32) ** block_levels(seeds[7], (NLAT, NSUB, FIELD_LEVELS, NLON), ((0, 32), (1, 8)), -0.2, 0.2), 0.0, 1.0),
        "obs_error": jnp.clip(jnp.exp(math.log(2.5) - 2.3025851 * jax.random.uniform(seeds[8], (NLAT, NSUB, FIELD_LEVELS, NLON), jnp.float32) ** block_levels(seeds[8], (NLAT, NSUB, FIELD_LEVELS, NLON), ((0, 32), (1, 8)), -0.2, 0.2)), 0.25, 2.5),
    }


def wind_coefficients(wind_east, wind_north):
    from_west = jnp.maximum(wind_east, 0.0)[:, :, None, :]
    from_east = jnp.maximum(-wind_east, 0.0)[:, :, None, :]
    from_south = jnp.maximum(wind_north, 0.0)[:, :, None, :]
    from_north = jnp.maximum(-wind_north, 0.0)[:, :, None, :]
    staying = 1.0 - from_west - from_east - from_south - from_north
    return staying, from_west, from_east, from_south, from_north


def pad_rows(values):
    return jnp.pad(values, ((1, 1), (0, 0), (0, 0), (0, 0)))


def forward_step(values, coefficients):
    staying, from_west, from_east, from_south, from_north = coefficients
    padded = pad_rows(values)
    return (staying * values + from_west * jnp.roll(values, 1, 3) + from_east * jnp.roll(values, -1, 3)
            + from_south * padded[:-2] + from_north * padded[2:])


def adjoint_step(values, coefficients):
    staying, from_west, from_east, from_south, from_north = coefficients
    return (staying * values + jnp.roll(from_west * values, -1, 3) + jnp.roll(from_east * values, 1, 3)
            + pad_rows(from_south * values)[2:] + pad_rows(from_north * values)[:-2])


def covariance(values, deviation, merid_filter):
    scaled = deviation[:, None] * values
    column_block = scaled.reshape(values.shape[0], -1)
    inner_part = jnp.dot(merid_filter.T, column_block, precision=lax.Precision.HIGHEST, preferred_element_type=jnp.float32)
    outer_part = jnp.dot(merid_filter, inner_part, precision=lax.Precision.HIGHEST, preferred_element_type=jnp.float32)
    return deviation[:, None] * outer_part.reshape(values.shape)


def reference(dual_state, obs_dual, increment, wind_east, wind_north, deviation, merid_filter, obs_weight, obs_error):
    coefficients = wind_coefficients(wind_east, wind_north)
    advanced = increment
    for number in range(STEPS):
        advanced = forward_step(advanced, coefficients)
    preceding = jnp.concatenate([jnp.zeros_like(advanced[:, :1]), advanced[:, :-1]], 1)
    model_error_term = increment - preceding
    returned = jnp.concatenate([dual_state[:, 1:], jnp.zeros_like(dual_state[:, :1])], 1)
    for number in range(STEPS):
        returned = adjoint_step(returned, coefficients)
    adjoint_term = dual_state - returned
    first_block = covariance(dual_state, deviation, merid_filter) + model_error_term
    second_block = obs_error * obs_dual + obs_weight * increment
    third_block = adjoint_term + obs_weight * obs_dual
    precond_dual = jnp.flip(jnp.cumsum(jnp.flip(third_block, 1), 1), 1)
    precond_obs = second_block / obs_error
    remainder = first_block - covariance(precond_dual, deviation, merid_filter)
    precond_increment = jnp.cumsum(remainder, 1)
    return precond_dual, precond_obs, precond_increment
```

```python
import jax
import jax.numpy as jnp
from jax import lax
from jax.experimental import pallas as pl
from jax.experimental.pallas import tpu as pltpu
from jax.sharding import PartitionSpec as P

ROWS, SUBS, FIELDS, LON = 25, 2, 4, 1024
LAT = 800
SPACE = 32
CHIPS = 4
BLOCK = 160
LANES = 128
TILES = LON // LANES
VMEM_LIMIT = 48 * 1024 * 1024

F32 = jnp.float32
BF16 = jnp.bfloat16


def call(kernel, out_shapes, operands, scratch=(), scalars=False, flops=0):
    in_specs = [pl.BlockSpec(memory_space=pltpu.VMEM)] * len(operands)
    if scalars:
        in_specs[0] = pl.BlockSpec(memory_space=pltpu.SMEM)
    size = sum(4 * a.size for a in operands) + sum(4 * s.size for s in out_shapes)
    return pl.pallas_call(
        kernel,
        out_shape=tuple(out_shapes),
        in_specs=in_specs,
        out_specs=tuple(pl.BlockSpec(memory_space=pltpu.VMEM) for _ in out_shapes),
        scratch_shapes=list(scratch),
        compiler_params=pltpu.CompilerParams(vmem_limit_bytes=VMEM_LIMIT),
        cost_estimate=pl.CostEstimate(flops=flops, bytes_accessed=size, transcendentals=0),
    )(*operands)


def field(*shape):
    return jax.ShapeDtypeStruct(shape, F32)


def split(x):
    high = x.astype(BF16)
    return high, (x - high.astype(F32)).astype(BF16)


def dot3(a_high, a_low, b_high, b_low, dims):
    def one(a, b):
        return lax.dot_general(a, b, (dims, ((), ())), preferred_element_type=F32)

    return one(a_high, b_high) + (one(a_high, b_low) + one(a_low, b_high))


def square_kernel(w_ref, high_ref, low_ref, w_high, w_low):
    high, low = split(w_ref[...])
    w_high[...] = high
    w_low[...] = low

    @pl.loop(0, LAT // BLOCK)
    def _(block):
        rows = pl.ds(pl.multiple_of(block * BLOCK, BLOCK), BLOCK)
        product = dot3(w_high[rows, :], w_low[rows, :], w_high[...], w_low[...], ((1,), (1,)))
        product_high, product_low = split(product)
        high_ref[rows, :] = product_high
        low_ref[rows, :] = product_low


def filter_kernel(high_ref, low_ref, x_ref, y_ref, x_high, x_low):
    for part in range(2):
        high, low = split(x_ref[pl.ds(part, LAT, stride=2), :])
        x_high[:, part * LANES : (part + 1) * LANES] = high
        x_low[:, part * LANES : (part + 1) * LANES] = low

    @pl.loop(0, LAT // BLOCK)
    def _(block):
        rows = pl.ds(pl.multiple_of(block * BLOCK, BLOCK), BLOCK)
        product = dot3(high_ref[rows, :], low_ref[rows, :], x_high[...], x_low[...], ((1,), (0,)))
        for part in range(2):
            y_ref[pl.ds(2 * block * BLOCK + part, BLOCK, stride=2), :] = product[
                :, part * LANES : (part + 1) * LANES
            ]


def paired(first, second):
    lower = lax.broadcasted_iota(jnp.int32, (2 * FIELDS, LON), 0) < FIELDS
    shape = (2 * FIELDS, LON)
    return jnp.where(lower, jnp.broadcast_to(first, shape), jnp.broadcast_to(second, shape))


def tangent_row(below, here, above, east, north):
    east_size, north_size = jnp.abs(east), jnp.abs(north)
    along = jnp.where(east > 0, pltpu.roll(here, 1, 1), pltpu.roll(here, LON - 1, 1))
    across = jnp.where(north > 0, below, above)
    return (1.0 - east_size - north_size) * here + east_size * along + north_size * across


def tangent_kernel(inc_ref, low_ref, high_ref, wind_ref, base_ref, total_ref, rows_ref, step_ref):
    rows_ref[0:2] = low_ref[:, 0:8, :]
    rows_ref[27:29] = high_ref[:, 0:8, :]

    def winds(row):
        block = wind_ref[row]
        return paired(block[0:1], block[1:2]), paired(block[2:3], block[3:4])

    @pl.loop(0, ROWS)
    def _(row):
        rows_ref[row + 2] = jnp.concatenate([inc_ref[row, 0], inc_ref[row, 1]], axis=0)

    @pl.loop(1, ROWS + 3)
    def _(row):
        east, north = winds(row)
        step_ref[row] = tangent_row(
            rows_ref[row - 1], rows_ref[row], rows_ref[row + 1], east, north
        )

    @pl.loop(2, ROWS + 2)
    def _(row):
        east, north = winds(row)
        advanced = tangent_row(
            step_ref[row - 1], step_ref[row], step_ref[row + 1], east, north
        )
        first = inc_ref[row - 2, 0]
        second = first + inc_ref[row - 2, 1] - advanced[0:4]
        base_ref[row - 2, 0] = first
        base_ref[row - 2, 1] = second
        total_ref[row - 2] = second - advanced[4:8]


def adjoint_parts(here, east, north):
    along, across = east * here, north * here
    zero = jnp.zeros_like(here)
    kept = (1.0 - jnp.abs(east) - jnp.abs(north)) * here
    kept = kept + pltpu.roll(jnp.where(east > 0, along, zero), LON - 1, 1)
    kept = kept + pltpu.roll(jnp.where(east > 0, zero, -along), 1, 1)
    to_south = jnp.where(north > 0, across, zero)
    to_north = jnp.where(north > 0, zero, -across)
    return kept, to_south, to_north


def adjoint_kernel(
    scalar_ref,
    dual_ref,
    low_ref,
    high_ref,
    wind_ref,
    early_ref,
    obs_ref,
    weight_ref,
    base_ref,
    sums_ref,
    keep_ref,
    send_ref,
    rows_ref,
    step_ref,
    back_ref,
):
    rows_ref[0:2] = low_ref[:, 8:16, :]
    rows_ref[27:29] = high_ref[:, 8:16, :]

    def winds(row):
        early, block = early_ref[row], wind_ref[row]
        return paired(early[0:1], block[0:1]), paired(early[1:2], block[2:3])

    @pl.loop(0, ROWS)
    def _(row):
        rows_ref[row + 2] = jnp.concatenate([dual_ref[row, 0], dual_ref[row, 1]], axis=0)

    def sweep(source, target, begin, end):
        kept, _, to_north = adjoint_parts(source[begin], *winds(begin))

        def step(row, carry):
            pending, from_below = carry
            kept, to_south, to_north = adjoint_parts(source[row], *winds(row))
            target[row - 1] = pending + to_south
            return kept + from_below, to_north

        lax.fori_loop(begin + 1, end, step, (kept, to_north))

    sweep(rows_ref, step_ref, 0, ROWS + 4)
    sweep(step_ref, back_ref, 1, ROWS + 3)

    here = scalar_ref[0]
    inner = scalar_ref[1]
    is_first = scalar_ref[2] < 0.5

    @pl.loop(0, ROWS)
    def _(row):
        returned = back_ref[row + 2]
        before = inner * returned[0:4]
        dual_first, dual_second = dual_ref[row, 0], dual_ref[row, 1]
        third_first = dual_first + weight_ref[row, 0] * obs_ref[row, 0]
        third_second = dual_second + weight_ref[row, 1] * obs_ref[row, 1]
        base = third_first - returned[4:8] + third_second
        base_ref[row, 0] = base
        base_ref[row, 1] = third_second
        sums = dual_first + (2.0 * here) * before - (2.0 * here + 1.0) * base
        total = sums + dual_second - third_second
        sums_ref[row, 0] = sums
        sums_ref[row, 1] = total
        later = base - before
        lower = jnp.concatenate([later[0:2], total[0:2]], axis=0)
        upper = jnp.concatenate([later[2:4], total[2:4]], axis=0)
        keep_ref[row] = jnp.where(is_first, lower, upper)
        send_ref[row] = jnp.where(is_first, upper, lower)


def joined(is_first, own, other):
    return jnp.concatenate(
        [jnp.where(is_first, own, other), jnp.where(is_first, other, own)], axis=0
    )


def spread_kernel(
    scalar_ref, base_ref, sums_ref, deviation_ref, own_ref, other_ref, dual_ref, column_ref
):
    here = scalar_ref[0]
    is_first = scalar_ref[2] < 0.5

    @pl.loop(0, ROWS)
    def _(row):
        own, other = own_ref[row], other_ref[row]
        later = joined(is_first, own[0:2], other[0:2])
        earlier = joined(is_first, own[2:4], other[2:4])
        deviation = deviation_ref[row]
        for sub in range(SUBS):
            dual_ref[row, sub] = base_ref[row, sub] + later
            sums = earlier + sums_ref[row, sub] - (2.0 * here + (1.0 + sub)) * later
            scaled = deviation * sums
            for pair in range(2):
                for tile in range(TILES):
                    column_ref[sub * 16 + pair * 8 + tile, row] = scaled[
                        2 * pair : 2 * pair + 2, tile * LANES : (tile + 1) * LANES
                    ]


def finish_kernel(
    scalar_ref, column_ref, base_ref, deviation_ref, own_ref, other_ref, out_ref
):
    is_first = scalar_ref[2] < 0.5

    @pl.loop(0, ROWS)
    def _(row):
        earlier = joined(is_first, own_ref[row], other_ref[row])
        deviation = deviation_ref[row]
        for sub in range(SUBS):
            filtered = jnp.concatenate(
                [
                    jnp.concatenate(
                        [column_ref[sub * 16 + pair * 8 + tile, row] for tile in range(TILES)],
                        axis=1,
                    )
                    for pair in range(2)
                ],
                axis=0,
            )
            out_ref[row, sub] = deviation * filtered + (base_ref[row, sub] + earlier)


def body(
    dual_state,
    obs_dual,
    increment,
    wind_east,
    wind_north,
    deviation,
    merid_filter,
    obs_weight,
    obs_error,
):
    place = lax.axis_index("tm")
    chip, core = place // 2, place % 2
    size = lax.axis_size("space")
    upward = [(i, i + 1) for i in range(size - 1)]
    downward = [(i + 1, i) for i in range(size - 1)]
    following = [(i, i + 1) for i in range(2 * CHIPS - 1)]
    swap = [(i, i ^ 1) for i in range(2 * CHIPS)]

    def over_chips(pairs):
        return [(2 * a + c, 2 * b + c) for a, b in pairs for c in range(2)]

    rise = [(c, (c + 1) % CHIPS) for c in range(CHIPS)]
    fall = [((c + 1) % CHIPS, c) for c in range(CHIPS)]

    scalars = jnp.stack([place, jnp.minimum(place, 1), core]).astype(F32)

    def edge(rows):
        return jnp.concatenate(
            [
                increment[rows].reshape(2, 8, LON),
                dual_state[rows].reshape(2, 8, LON),
                wind_east[rows],
                wind_north[rows],
            ],
            axis=1,
        )

    low = lax.ppermute(edge(slice(ROWS - 2, ROWS)), "space", upward)
    high = lax.ppermute(edge(slice(0, 2)), "space", downward)

    filter_high, filter_low = call(
        square_kernel,
        [jax.ShapeDtypeStruct((LAT, LAT), BF16)] * 2,
        [merid_filter],
        [pltpu.VMEM((LAT, LAT), BF16)] * 2,
        flops=6 * LAT**3,
    )

    winds = jnp.concatenate(
        [low[:, 16:20], jnp.concatenate([wind_east, wind_north], axis=1), high[:, 16:20]], axis=0
    )
    early = lax.ppermute(
        jnp.concatenate([winds[:, 1:2], winds[:, 3:4]], axis=1), "tm", following
    )

    model_base, model_total = call(
        tangent_kernel,
        [field(ROWS, SUBS, FIELDS, LON), field(ROWS, FIELDS, LON)],
        [increment, low, high, winds],
        [pltpu.VMEM((ROWS + 4, 8, LON), F32)] * 2,
        flops=40 * ROWS * 8 * LON,
    )
    precond_obs = (obs_error * obs_dual + obs_weight * increment) / obs_error

    dual_base, dual_sums, keep, send = call(
        adjoint_kernel,
        [field(ROWS, SUBS, FIELDS, LON)] * 2 + [field(ROWS, FIELDS, LON)] * 2,
        [scalars, dual_state, low, high, winds, early, obs_dual, obs_weight],
        [pltpu.VMEM((ROWS + 4, 8, LON), F32)] * 3,
        scalars=True,
        flops=60 * ROWS * 8 * LON,
    )

    received = lax.ppermute(send, "tm", swap)
    chip_total = keep + received
    later, earlier = chip_total[:, 0:2], chip_total[:, 2:4]
    falling = lax.ppermute(jnp.where(chip == 0, earlier, later), "tm", over_chips(fall))
    rising = lax.ppermute(jnp.where(chip == CHIPS - 1, later, earlier), "tm", over_chips(rise))
    falling_on = lax.ppermute(falling, "tm", over_chips([(2, 1), (1, 0)]))
    rising_on = lax.ppermute(rising, "tm", over_chips([(1, 2), (2, 3)]))
    zero = jnp.zeros_like(falling)
    from_later = (
        jnp.where(chip < 3, falling, zero) + jnp.where(chip == 0, rising, zero) + falling_on
    )
    from_earlier = (
        jnp.where(chip > 0, rising, zero) + jnp.where(chip == 3, falling, zero) + rising_on
    )
    first = core == 0
    own = jnp.concatenate(
        [
            from_later + jnp.where(first, received[:, 0:2], zero),
            from_earlier + jnp.where(first, zero, received[:, 2:4]),
        ],
        axis=1,
    )
    other = lax.ppermute(
        jnp.concatenate(
            [
                from_later + jnp.where(first, zero, keep[:, 0:2]),
                from_earlier + jnp.where(first, keep[:, 2:4], zero),
            ],
            axis=1,
        ),
        "tm",
        swap,
    )

    precond_dual, columns = call(
        spread_kernel,
        [field(ROWS, SUBS, FIELDS, LON), field(SPACE, ROWS, 2, LANES)],
        [scalars, dual_base, dual_sums, deviation, own, other],
        scalars=True,
        flops=10 * ROWS * 8 * LON,
    )

    model_keep = jnp.where(first, model_total[:, 0:2], model_total[:, 2:4])
    model_send = jnp.where(first, model_total[:, 2:4], model_total[:, 0:2])
    model_received = lax.ppermute(model_send, "tm", swap)
    model_chip = model_keep + model_received
    model_up = lax.ppermute(model_chip, "tm", over_chips([(0, 1), (1, 2), (2, 3)]))
    model_wrap = lax.ppermute(model_chip, "tm", over_chips([(0, 3)]))

    columns = lax.all_to_all(columns, "space", split_axis=0, concat_axis=0, tiled=True)
    (columns,) = call(
        filter_kernel,
        [field(2 * LAT, LANES)],
        [filter_high, filter_low, columns.reshape(2 * LAT, LANES)],
        [pltpu.VMEM((LAT, 2 * LANES), BF16)] * 2,
        flops=6 * LAT * LAT * 2 * LANES,
    )
    columns = lax.all_to_all(
        columns.reshape(SPACE, ROWS, 2, LANES), "space", split_axis=0, concat_axis=0, tiled=True
    )

    model_on = lax.ppermute(model_up, "tm", over_chips([(1, 2), (2, 3)]))
    model_earlier = model_up + model_wrap + model_on
    model_own = model_earlier + jnp.where(first, zero, model_received)
    model_other = lax.ppermute(
        model_earlier + jnp.where(first, model_keep, zero), "tm", swap
    )

    (precond_increment,) = call(
        finish_kernel,
        [field(ROWS, SUBS, FIELDS, LON)],
        [scalars, columns, model_base, deviation, model_own, model_other],
        scalars=True,
        flops=4 * ROWS * 8 * LON,
    )
    return (precond_dual, precond_obs, precond_increment)


def solution(mesh):
    banded = P("space", "tm", None, None)
    placed = (
        banded,
        banded,
        banded,
        P("space", "tm", None),
        P("space", "tm", None),
        P("space", None, None),
        P(),
        banded,
        banded,
    )
    return jax.shard_map(
        body,
        mesh=mesh,
        in_specs=placed,
        out_specs=(banded, banded, banded),
        check_vma=False,
    )
```

```python
import jax
import jax.numpy as jnp
from jax import lax
from jax.experimental import pallas as pl
from jax.experimental.pallas import tpu as pltpu
from jax.sharding import PartitionSpec as P

ROWS, SUBS, FIELDS, LON = 25, 2, 4, 1024
LAT = 800
SPACE = 32
CHIPS = 4
BLOCK = 160
LANES = 128
TILES = LON // LANES
VMEM_LIMIT = 12 * 1024 * 1024

F32 = jnp.float32
BF16 = jnp.bfloat16
TOKEN = jax.ShapeDtypeStruct((8, LANES), F32)


def call(kernel, out_shapes, operands, scratch=(), scalars=False, flops=0):
    in_specs = [pl.BlockSpec(memory_space=pltpu.VMEM)] * len(operands)
    if scalars:
        in_specs[0] = pl.BlockSpec(memory_space=pltpu.SMEM)
    size = sum(4 * a.size for a in operands) + sum(4 * s.size for s in out_shapes)
    return pl.pallas_call(
        kernel,
        out_shape=tuple(out_shapes),
        in_specs=in_specs,
        out_specs=tuple(pl.BlockSpec(memory_space=pltpu.VMEM) for _ in out_shapes),
        scratch_shapes=list(scratch),
        compiler_params=pltpu.CompilerParams(vmem_limit_bytes=VMEM_LIMIT),
        cost_estimate=pl.CostEstimate(flops=flops, bytes_accessed=size, transcendentals=0),
    )(*operands)


def rows_loop(begin, end, unroll, each):
    @pl.loop(0, (end - begin) // unroll)
    def _(group):
        for k in range(unroll):
            each(begin + group * unroll + k)

    for row in range(end - (end - begin) % unroll, end):
        each(row)


def field(*shape):
    return jax.ShapeDtypeStruct(shape, F32)


def split(x):
    high = x.astype(BF16)
    return high, (x - high.astype(F32)).astype(BF16)


def dot3(a_high, a_low, b_high, b_low, dims):
    def one(a, b):
        return lax.dot_general(a, b, (dims, ((), ())), preferred_element_type=F32)

    return one(a_high, b_high) + (one(a_high, b_low) + one(a_low, b_high))


def edge_kernel(*refs):
    fields, (east_ref, north_ref) = refs[:8], refs[8:10]
    up_ref, down_ref, wind_ref, ahead_ref, token_ref = refs[10:]
    for target, rows, first in ((down_ref, (0, 1), 0), (up_ref, (ROWS - 2, ROWS - 1), 2)):
        for k in range(2):
            for part in range(2):
                source = fields[4 * part + first + k]
                for sub in range(SUBS):
                    start = 8 * part + FIELDS * sub
                    target[k, start : start + FIELDS, :] = source[0, sub]
            for sub in range(SUBS):
                target[k, 16 + 2 * sub : 17 + 2 * sub, :] = east_ref[rows[k], sub : sub + 1]
                target[k, 17 + 2 * sub : 18 + 2 * sub, :] = north_ref[rows[k], sub : sub + 1]

    def each(row):
        east, north = east_ref[row], north_ref[row]
        wind_ref[row, 0:1] = east[0:1]
        wind_ref[row, 1:2] = north[0:1]
        wind_ref[row, 2:3] = east[1:2]
        wind_ref[row, 3:4] = north[1:2]
        ahead_ref[row, 0:1] = east[1:2]
        ahead_ref[row, 1:2] = north[1:2]

    rows_loop(0, ROWS, 5, each)
    token_ref[...] = jnp.zeros_like(token_ref)


def edges(increment, dual_state, wind_east, wind_north):
    def row_spec(row):
        return pl.BlockSpec((1, SUBS, FIELDS, LON), lambda i: (row, 0, 0, 0))

    whole = pl.BlockSpec((ROWS, SUBS, LON), lambda i: (0, 0, 0))
    picked = [row_spec(row) for row in (0, 1, ROWS - 2, ROWS - 1)]
    shapes = [field(2, 20, LON)] * 2 + [field(ROWS, 4, LON), field(ROWS, 2, LON), TOKEN]
    return pl.pallas_call(
        edge_kernel,
        grid=(1,),
        out_shape=tuple(shapes),
        in_specs=picked + picked + [whole, whole],
        out_specs=tuple(pl.BlockSpec(memory_space=pltpu.VMEM) for _ in shapes),
        compiler_params=pltpu.CompilerParams(vmem_limit_bytes=VMEM_LIMIT),
        cost_estimate=pl.CostEstimate(flops=0, bytes_accessed=1500000, transcendentals=0),
    )(*[increment] * 4, *[dual_state] * 4, wind_east, wind_north)


def square_kernel(w_ref, after_ref, high_ref, low_ref, token_ref, w_high, w_low):
    token_ref[...] = jnp.zeros_like(token_ref)
    high, low = split(w_ref[...])
    w_high[...] = high
    w_low[...] = low

    @pl.loop(0, LAT // BLOCK)
    def _(block):
        rows = pl.ds(pl.multiple_of(block * BLOCK, BLOCK), BLOCK)
        product = dot3(w_high[rows, :], w_low[rows, :], w_high[...], w_low[...], ((1,), (1,)))
        product_high, product_low = split(product)
        high_ref[rows, :] = product_high
        low_ref[rows, :] = product_low


def filter_kernel(high_ref, low_ref, x_ref, after_ref, y_ref, token_ref, x_high, x_low):
    token_ref[...] = jnp.zeros_like(token_ref)
    for part in range(2):
        high, low = split(x_ref[pl.ds(part, LAT, stride=2), :])
        x_high[:, part * LANES : (part + 1) * LANES] = high
        x_low[:, part * LANES : (part + 1) * LANES] = low

    @pl.loop(0, LAT // BLOCK)
    def _(block):
        rows = pl.ds(pl.multiple_of(block * BLOCK, BLOCK), BLOCK)
        product = dot3(high_ref[rows, :], low_ref[rows, :], x_high[...], x_low[...], ((1,), (0,)))
        for part in range(2):
            y_ref[pl.ds(2 * block * BLOCK + part, BLOCK, stride=2), :] = product[
                :, part * LANES : (part + 1) * LANES
            ]


def paired(first, second):
    lower = lax.broadcasted_iota(jnp.int32, (2 * FIELDS, LON), 0) < FIELDS
    shape = (2 * FIELDS, LON)
    return jnp.where(lower, jnp.broadcast_to(first, shape), jnp.broadcast_to(second, shape))


def tangent_row(below, here, above, east, north):
    east_size, north_size = jnp.abs(east), jnp.abs(north)
    along = jnp.where(east > 0, pltpu.roll(here, 1, 1), pltpu.roll(here, LON - 1, 1))
    across = jnp.where(north > 0, below, above)
    return (1.0 - east_size - north_size) * here + east_size * along + north_size * across


def halo_rows(target, source, low, high, begin):
    target[0:2] = low[:, begin : begin + 8, :]
    target[ROWS + 2 : ROWS + 4] = high[:, begin : begin + 8, :]

    def each(row):
        target[row + 2] = jnp.concatenate([source[row, 0], source[row, 1]], axis=0)

    rows_loop(0, ROWS, 5, each)


def tangent_kernel(
    scalar_ref,
    inc_ref,
    low_ref,
    high_ref,
    wind_ref,
    after_ref,
    base_ref,
    keep_ref,
    send_ref,
    token_ref,
    rows_ref,
    step_ref,
    east_ref,
    north_ref,
):
    token_ref[...] = jnp.zeros_like(token_ref)
    halo_rows(rows_ref, inc_ref, low_ref, high_ref, 0)
    is_first = scalar_ref[2] < 0.5

    def spread(row, block):
        east_ref[row] = paired(block[0:1], block[2:3])
        north_ref[row] = paired(block[1:2], block[3:4])

    spread(1, low_ref[1, 16:20, :])
    spread(ROWS + 2, high_ref[0, 16:20, :])
    rows_loop(0, ROWS, 5, lambda row: spread(row + 2, wind_ref[row]))

    def first_step(row):
        step_ref[row] = tangent_row(
            rows_ref[row - 1], rows_ref[row], rows_ref[row + 1], east_ref[row], north_ref[row]
        )

    rows_loop(1, ROWS + 3, 3, first_step)

    def second_step(row):
        advanced = tangent_row(
            step_ref[row + 1], step_ref[row + 2], step_ref[row + 3],
            east_ref[row + 2], north_ref[row + 2],
        )
        first = inc_ref[row, 0]
        second = first + inc_ref[row, 1] - advanced[0:4]
        base_ref[row, 0] = first
        base_ref[row, 1] = second
        total = second - advanced[4:8]
        keep_ref[row] = jnp.where(is_first, total[0:2], total[2:4])
        send_ref[row] = jnp.where(is_first, total[2:4], total[0:2])

    rows_loop(0, ROWS, 5, second_step)


def adjoint_parts(here, east, north):
    along, across = east * here, north * here
    zero = jnp.zeros_like(here)
    kept = (1.0 - jnp.abs(east) - jnp.abs(north)) * here
    kept = kept + pltpu.roll(jnp.where(east > 0, along, zero), LON - 1, 1)
    kept = kept + pltpu.roll(jnp.where(east > 0, zero, -along), 1, 1)
    to_south = jnp.where(north > 0, across, zero)
    to_north = jnp.where(north > 0, zero, -across)
    return kept, to_south, to_north


def adjoint_kernel(
    scalar_ref,
    dual_ref,
    low_ref,
    high_ref,
    wind_ref,
    ahead_ref,
    rim_ref,
    obs_ref,
    weight_ref,
    after_ref,
    base_ref,
    sums_ref,
    keep_ref,
    send_ref,
    rows_ref,
    step_ref,
    back_ref,
    east_ref,
    north_ref,
):
    halo_rows(rows_ref, dual_ref, low_ref, high_ref, 8)

    def spread(row, early, block):
        east_ref[row] = paired(early[0:1], block[0:1])
        north_ref[row] = paired(early[1:2], block[1:2])

    for k in range(2):
        spread(k, rim_ref[k], low_ref[k, 16:18, :])
        spread(ROWS + 2 + k, rim_ref[2 + k], high_ref[k, 16:18, :])
    rows_loop(0, ROWS, 5, lambda row: spread(row + 2, ahead_ref[row], wind_ref[row]))

    def sweep(source, target, begin, end, unroll):
        def parts(row):
            return adjoint_parts(source[row], east_ref[row], north_ref[row])

        def step(group, carry):
            pending, from_below = carry
            for k in range(unroll):
                row = begin + 1 + group * unroll + k
                kept, to_south, to_north = parts(row)
                target[row - 1] = pending + to_south
                pending, from_below = kept + from_below, to_north
            return pending, from_below

        kept, _, to_north = parts(begin)
        lax.fori_loop(0, (end - begin - 1) // unroll, step, (kept, to_north))

    sweep(rows_ref, step_ref, 0, ROWS + 4, 4)
    sweep(step_ref, back_ref, 1, ROWS + 3, 2)

    here = scalar_ref[0]
    inner = scalar_ref[1]
    is_first = scalar_ref[2] < 0.5

    def each(row):
        returned = back_ref[row + 2]
        before = inner * returned[0:4]
        dual_first, dual_second = dual_ref[row, 0], dual_ref[row, 1]
        third_first = dual_first + weight_ref[row, 0] * obs_ref[row, 0]
        third_second = dual_second + weight_ref[row, 1] * obs_ref[row, 1]
        base = third_first - returned[4:8] + third_second
        base_ref[row, 0] = base
        base_ref[row, 1] = third_second
        sums = dual_first + (2.0 * here) * before - (2.0 * here + 1.0) * base
        total = sums + dual_second - third_second
        sums_ref[row, 0] = sums
        sums_ref[row, 1] = total
        later = base - before
        lower = jnp.concatenate([later[0:2], total[0:2]], axis=0)
        upper = jnp.concatenate([later[2:4], total[2:4]], axis=0)
        keep_ref[row] = jnp.where(is_first, lower, upper)
        send_ref[row] = jnp.where(is_first, upper, lower)

    rows_loop(0, ROWS, 5, each)


def joined(is_first, own, other):
    return jnp.concatenate(
        [jnp.where(is_first, own, other), jnp.where(is_first, other, own)], axis=0
    )


def spread_kernel(
    scalar_ref,
    base_ref,
    sums_ref,
    deviation_ref,
    own_ref,
    other_ref,
    model_keep_ref,
    model_received_ref,
    dual_ref,
    column_ref,
    model_ref,
    token_ref,
):
    token_ref[...] = jnp.zeros_like(token_ref)
    here = scalar_ref[0]
    is_first = scalar_ref[2] < 0.5

    def each(row):
        own, other = own_ref[row], other_ref[row]
        later = joined(is_first, own[0:2], other[0:2])
        earlier = joined(is_first, own[2:4], other[2:4])
        deviation = deviation_ref[row]
        for sub in range(SUBS):
            dual_ref[row, sub] = base_ref[row, sub] + later
            sums = earlier + sums_ref[row, sub] - (2.0 * here + (1.0 + sub)) * later
            scaled = deviation * sums
            for pair in range(2):
                for tile in range(TILES):
                    column_ref[sub * 16 + pair * 8 + tile, row] = scaled[
                        2 * pair : 2 * pair + 2, tile * LANES : (tile + 1) * LANES
                    ]
        model_ref[row] = model_keep_ref[row] + model_received_ref[row]

    rows_loop(0, ROWS, 5, each)


def obs_kernel(obs_ref, inc_ref, weight_ref, error_ref, after_ref, out_ref, token_ref):
    token_ref[...] = jnp.zeros_like(token_ref)

    def each(row):
        error = error_ref[row]
        out_ref[row] = (error * obs_ref[row] + weight_ref[row] * inc_ref[row]) / error

    rows_loop(0, ROWS, 5, each)


def model_kernel(
    scalar_ref, up_ref, far_ref, wrap_ref, keep_ref, received_ref, after_ref, own_ref, send_ref
):
    is_first = scalar_ref[2] < 0.5

    def each(row):
        earlier = up_ref[row] + far_ref[row] + wrap_ref[row]
        zero = jnp.zeros_like(earlier)
        own_ref[row] = earlier + jnp.where(is_first, zero, received_ref[row])
        send_ref[row] = earlier + jnp.where(is_first, keep_ref[row], zero)

    rows_loop(0, ROWS, 5, each)


def finish_kernel(
    scalar_ref, column_ref, base_ref, deviation_ref, own_ref, other_ref, out_ref
):
    is_first = scalar_ref[2] < 0.5

    def each(row):
        earlier = joined(is_first, own_ref[row], other_ref[row])
        deviation = deviation_ref[row]
        for sub in range(SUBS):
            filtered = jnp.concatenate(
                [
                    jnp.concatenate(
                        [column_ref[sub * 16 + pair * 8 + tile, row] for tile in range(TILES)],
                        axis=1,
                    )
                    for pair in range(2)
                ],
                axis=0,
            )
            out_ref[row, sub] = deviation * filtered + (base_ref[row, sub] + earlier)

    rows_loop(0, ROWS, 5, each)


def body(
    dual_state,
    obs_dual,
    increment,
    wind_east,
    wind_north,
    deviation,
    merid_filter,
    obs_weight,
    obs_error,
):
    place = lax.axis_index("tm")
    chip, core = place // 2, place % 2
    size = lax.axis_size("space")
    upward = [(i, i + 1) for i in range(size - 1)]
    downward = [(i + 1, i) for i in range(size - 1)]
    following = [(i, i + 1) for i in range(2 * CHIPS - 1)]
    swap = [(i, i ^ 1) for i in range(2 * CHIPS)]

    def over_chips(pairs):
        return [(2 * a + c, 2 * b + c) for a, b in pairs for c in range(2)]

    rise = [(c, (c + 1) % CHIPS) for c in range(CHIPS)]
    fall = [((c + 1) % CHIPS, c) for c in range(CHIPS)]

    scalars = jnp.stack([place, jnp.minimum(place, 1), core]).astype(F32)

    to_north, to_south, winds, ahead, token = edges(
        increment, dual_state, wind_east, wind_north
    )
    low = lax.ppermute(to_north, "space", upward)
    high = lax.ppermute(to_south, "space", downward)
    ahead = lax.ppermute(ahead, "tm", following)

    filter_high, filter_low, token = call(
        square_kernel,
        [jax.ShapeDtypeStruct((LAT, LAT), BF16)] * 2 + [TOKEN],
        [merid_filter, token],
        [pltpu.VMEM((LAT, LAT), BF16)] * 2,
        flops=6 * LAT**3,
    )

    rim = lax.ppermute(
        jnp.concatenate([low[:, 18:20], high[:, 18:20]], axis=0), "tm", following
    )
    extended = pltpu.VMEM((ROWS + 4, 8, LON), F32)
    model_base, model_keep, model_send, token = call(
        tangent_kernel,
        [field(ROWS, SUBS, FIELDS, LON)] + [field(ROWS, 2, LON)] * 2 + [TOKEN],
        [scalars, increment, low, high, winds, token],
        [extended] * 4,
        scalars=True,
        flops=40 * ROWS * 8 * LON,
    )
    model_received = lax.ppermute(model_send, "tm", swap)

    dual_base, dual_sums, keep, send = call(
        adjoint_kernel,
        [field(ROWS, SUBS, FIELDS, LON)] * 2 + [field(ROWS, FIELDS, LON)] * 2,
        [scalars, dual_state, low, high, winds, ahead, rim, obs_dual, obs_weight, token],
        [extended] * 5,
        scalars=True,
        flops=60 * ROWS * 8 * LON,
    )

    received = lax.ppermute(send, "tm", swap)
    chip_total = keep + received
    later, earlier = chip_total[:, 0:2], chip_total[:, 2:4]
    falling = lax.ppermute(jnp.where(chip == 0, earlier, later), "tm", over_chips(fall))
    rising = lax.ppermute(jnp.where(chip == CHIPS - 1, later, earlier), "tm", over_chips(rise))
    falling_on = lax.ppermute(falling, "tm", over_chips([(2, 1), (1, 0)]))
    rising_on = lax.ppermute(rising, "tm", over_chips([(1, 2), (2, 3)]))
    zero = jnp.zeros_like(falling)
    from_later = (
        jnp.where(chip < 3, falling, zero) + jnp.where(chip == 0, rising, zero) + falling_on
    )
    from_earlier = (
        jnp.where(chip > 0, rising, zero) + jnp.where(chip == 3, falling, zero) + rising_on
    )
    first = core == 0
    own = jnp.concatenate(
        [
            from_later + jnp.where(first, received[:, 0:2], zero),
            from_earlier + jnp.where(first, zero, received[:, 2:4]),
        ],
        axis=1,
    )
    other = lax.ppermute(
        jnp.concatenate(
            [
                from_later + jnp.where(first, zero, keep[:, 0:2]),
                from_earlier + jnp.where(first, keep[:, 2:4], zero),
            ],
            axis=1,
        ),
        "tm",
        swap,
    )

    precond_dual, columns, model_chip, token = call(
        spread_kernel,
        [
            field(ROWS, SUBS, FIELDS, LON),
            field(SPACE, ROWS, 2, LANES),
            field(ROWS, 2, LON),
            TOKEN,
        ],
        [scalars, dual_base, dual_sums, deviation, own, other, model_keep, model_received],
        scalars=True,
        flops=10 * ROWS * 8 * LON,
    )

    columns = lax.all_to_all(columns, "space", split_axis=0, concat_axis=0, tiled=True)
    model_up = lax.ppermute(model_chip, "tm", over_chips([(0, 1), (1, 2), (2, 3)]))
    model_far = lax.ppermute(model_chip, "tm", over_chips([(0, 2), (1, 3)]))
    model_wrap = lax.ppermute(model_chip, "tm", over_chips([(0, 3)]))

    precond_obs, token = call(
        obs_kernel,
        [field(ROWS, SUBS, FIELDS, LON), TOKEN],
        [obs_dual, increment, obs_weight, obs_error, token],
        flops=10 * ROWS * 8 * LON,
    )

    columns, token = call(
        filter_kernel,
        [field(2 * LAT, LANES), TOKEN],
        [filter_high, filter_low, columns.reshape(2 * LAT, LANES), token],
        [pltpu.VMEM((LAT, 2 * LANES), BF16)] * 2,
        flops=6 * LAT * LAT * 2 * LANES,
    )
    columns = lax.all_to_all(
        columns.reshape(SPACE, ROWS, 2, LANES), "space", split_axis=0, concat_axis=0, tiled=True
    )

    model_own, model_send = call(
        model_kernel,
        [field(ROWS, 2, LON)] * 2,
        [scalars, model_up, model_far, model_wrap, model_keep, model_received, token],
        scalars=True,
        flops=10 * ROWS * 2 * LON,
    )
    model_other = lax.ppermute(model_send, "tm", swap)

    (precond_increment,) = call(
        finish_kernel,
        [field(ROWS, SUBS, FIELDS, LON)],
        [scalars, columns, model_base, deviation, model_own, model_other],
        scalars=True,
        flops=4 * ROWS * 8 * LON,
    )
    return (precond_dual, precond_obs, precond_increment)


def solution(mesh):
    banded = P("space", "tm", None, None)
    placed = (
        banded,
        banded,
        banded,
        P("space", "tm", None),
        P("space", "tm", None),
        P("space", None, None),
        P(),
        banded,
        banded,
    )
    return jax.shard_map(
        body,
        mesh=mesh,
        in_specs=placed,
        out_specs=(banded, banded, banded),
        check_vma=False,
    )
```

```python
import jax
import jax.numpy as jnp
from jax import lax
from jax.experimental import pallas as pl
from jax.experimental.pallas import tpu as pltpu
from jax.sharding import PartitionSpec as P

ROWS, SUBS, FIELDS, LON = 25, 2, 4, 1024
LAT = 800
SPACE = 32
CHIPS = 4
BLOCK = 160
LANES = 128
TILES = LON // LANES
VMEM_LIMIT = 12 * 1024 * 1024

F32 = jnp.float32
BF16 = jnp.bfloat16
TOKEN = jax.ShapeDtypeStruct((8, LANES), F32)


def call(kernel, out_shapes, operands, scratch=(), after=(), flops=0):
    count = len(operands)

    def run(*refs):
        kernel(*refs[:count], *refs[count + len(after) :])

    size = sum(4 * a.size for a in operands) + sum(4 * s.size for s in out_shapes)
    return pl.pallas_call(
        run,
        out_shape=tuple(out_shapes),
        in_specs=[pl.BlockSpec(memory_space=pltpu.VMEM)] * count
        + [pl.BlockSpec(memory_space=pl.ANY)] * len(after),
        out_specs=tuple(pl.BlockSpec(memory_space=pltpu.VMEM) for _ in out_shapes),
        scratch_shapes=list(scratch),
        compiler_params=pltpu.CompilerParams(vmem_limit_bytes=VMEM_LIMIT),
        cost_estimate=pl.CostEstimate(flops=flops, bytes_accessed=size, transcendentals=0),
    )(*operands, *after)


def hold(arrays, after):
    def run(*refs):
        pass

    count = len(arrays)
    anywhere = [pl.BlockSpec(memory_space=pl.ANY)] * (count + len(after))
    return pl.pallas_call(
        run,
        out_shape=tuple(field(*a.shape) for a in arrays),
        in_specs=anywhere,
        out_specs=tuple(anywhere[:count]),
        input_output_aliases={k: k for k in range(count)},
        cost_estimate=pl.CostEstimate(flops=0, bytes_accessed=0, transcendentals=0),
    )(*arrays, *after)


def place():
    return lax.axis_index("tm")


def rows_loop(begin, end, unroll, each):
    @pl.loop(0, (end - begin) // unroll)
    def _(group):
        for k in range(unroll):
            each(begin + group * unroll + k)

    for row in range(end - (end - begin) % unroll, end):
        each(row)


def field(*shape):
    return jax.ShapeDtypeStruct(shape, F32)


def split(x):
    high = x.astype(BF16)
    return high, (x - high.astype(F32)).astype(BF16)


def dot3(a_high, a_low, b_high, b_low, dims):
    def one(a, b):
        return lax.dot_general(a, b, (dims, ((), ())), preferred_element_type=F32)

    return one(a_high, b_high) + (one(a_high, b_low) + one(a_low, b_high))


def edge_kernel(
    inc_ref,
    dual_ref,
    east_ref,
    north_ref,
    up_ref,
    down_ref,
    wind_ref,
    ahead_ref,
    ahead_up_ref,
    ahead_down_ref,
    token_ref,
    inc_rows,
    dual_rows,
    east_rows,
    north_rows,
    done,
):
    token_ref[...] = jnp.zeros_like(token_ref)
    ends = (pl.ds(0, 2), pl.ds(ROWS - 2, 2))
    copies = [
        pltpu.make_async_copy(east_ref, east_rows, done.at[0]),
        pltpu.make_async_copy(north_ref, north_rows, done.at[1]),
    ]
    for k in range(2):
        copies += [
            pltpu.make_async_copy(inc_ref.at[ends[k]], inc_rows.at[k], done.at[2 + k]),
            pltpu.make_async_copy(dual_ref.at[ends[k]], dual_rows.at[k], done.at[4 + k]),
        ]
    for copy in copies:
        copy.start()
    for copy in copies:
        copy.wait()

    for target, ahead, begin, side in (
        (down_ref, ahead_down_ref, 0, 0),
        (up_ref, ahead_up_ref, ROWS - 2, 1),
    ):
        for k in range(2):
            for sub in range(SUBS):
                start = FIELDS * sub
                target[k, start : start + FIELDS, :] = inc_rows[side, k, sub]
                target[k, 8 + start : 8 + start + FIELDS, :] = dual_rows[side, k, sub]
                east = east_rows[begin + k, sub : sub + 1]
                north = north_rows[begin + k, sub : sub + 1]
                target[k, 16 + 2 * sub : 17 + 2 * sub, :] = east
                target[k, 17 + 2 * sub : 18 + 2 * sub, :] = north
            ahead[k, 0:1] = east
            ahead[k, 1:2] = north

    def each(row):
        east, north = east_rows[row], north_rows[row]
        wind_ref[row, 0:1] = east[0:1]
        wind_ref[row, 1:2] = north[0:1]
        wind_ref[row, 2:3] = east[1:2]
        wind_ref[row, 3:4] = north[1:2]
        ahead_ref[row, 0:1] = east[1:2]
        ahead_ref[row, 1:2] = north[1:2]

    rows_loop(0, ROWS, 5, each)


def edges(increment, dual_state, wind_east, wind_north):
    shapes = [field(2, 20, LON)] * 2 + [field(ROWS, 4, LON), field(ROWS, 2, LON)]
    shapes += [field(2, 2, LON)] * 2 + [TOKEN]
    ends = pltpu.VMEM((2, 2, SUBS, FIELDS, LON), F32)
    wind = pltpu.VMEM((ROWS, SUBS, LON), F32)
    return pl.pallas_call(
        edge_kernel,
        out_shape=tuple(shapes),
        in_specs=[pl.BlockSpec(memory_space=pltpu.HBM)] * 4,
        out_specs=tuple(pl.BlockSpec(memory_space=pltpu.VMEM) for _ in shapes),
        scratch_shapes=[ends, ends, wind, wind, pltpu.SemaphoreType.DMA((6,))],
        compiler_params=pltpu.CompilerParams(vmem_limit_bytes=61 * 1024 * 1024),
        cost_estimate=pl.CostEstimate(flops=0, bytes_accessed=1500000, transcendentals=0),
    )(increment, dual_state, wind_east, wind_north)


def square_kernel(w_ref, high_ref, low_ref, token_ref, w_high, w_low):
    token_ref[...] = jnp.zeros_like(token_ref)
    high, low = split(w_ref[...])
    w_high[...] = high
    w_low[...] = low

    @pl.loop(0, LAT // BLOCK)
    def _(block):
        rows = pl.ds(pl.multiple_of(block * BLOCK, BLOCK), BLOCK)
        product = dot3(w_high[rows, :], w_low[rows, :], w_high[...], w_low[...], ((1,), (1,)))
        product_high, product_low = split(product)
        high_ref[rows, :] = product_high
        low_ref[rows, :] = product_low


def filter_kernel(high_ref, low_ref, x_ref, y_ref, token_ref, x_high, x_low):
    token_ref[...] = jnp.zeros_like(token_ref)
    for part in range(2):
        high, low = split(x_ref[pl.ds(part, LAT, stride=2), :])
        x_high[:, part * LANES : (part + 1) * LANES] = high
        x_low[:, part * LANES : (part + 1) * LANES] = low

    @pl.loop(0, LAT // BLOCK)
    def _(block):
        rows = pl.ds(pl.multiple_of(block * BLOCK, BLOCK), BLOCK)
        product = dot3(high_ref[rows, :], low_ref[rows, :], x_high[...], x_low[...], ((1,), (0,)))
        for part in range(2):
            y_ref[pl.ds(2 * block * BLOCK + part, BLOCK, stride=2), :] = product[
                :, part * LANES : (part + 1) * LANES
            ]


def paired(first, second):
    lower = lax.broadcasted_iota(jnp.int32, (2 * FIELDS, LON), 0) < FIELDS
    shape = (2 * FIELDS, LON)
    return jnp.where(lower, jnp.broadcast_to(first, shape), jnp.broadcast_to(second, shape))


def tangent_row(below, here, above, east, north):
    east_size, north_size = jnp.abs(east), jnp.abs(north)
    along = jnp.where(east > 0, pltpu.roll(here, 1, 1), pltpu.roll(here, LON - 1, 1))
    across = jnp.where(north > 0, below, above)
    return (1.0 - east_size - north_size) * here + east_size * along + north_size * across


def halo_rows(target, source, low, high, begin):
    target[0:2] = low[:, begin : begin + 8, :]
    target[ROWS + 2 : ROWS + 4] = high[:, begin : begin + 8, :]

    def each(row):
        target[row + 2] = jnp.concatenate([source[row, 0], source[row, 1]], axis=0)

    rows_loop(0, ROWS, 5, each)


def tangent_kernel(
    inc_ref,
    low_ref,
    high_ref,
    wind_ref,
    base_ref,
    keep_ref,
    send_ref,
    token_ref,
    rows_ref,
    step_ref,
    east_ref,
    north_ref,
):
    token_ref[...] = jnp.zeros_like(token_ref)
    halo_rows(rows_ref, inc_ref, low_ref, high_ref, 0)
    is_first = place() % 2 == 0

    def spread(row, block):
        east_ref[row] = paired(block[0:1], block[2:3])
        north_ref[row] = paired(block[1:2], block[3:4])

    spread(1, low_ref[1, 16:20, :])
    spread(ROWS + 2, high_ref[0, 16:20, :])
    rows_loop(0, ROWS, 5, lambda row: spread(row + 2, wind_ref[row]))

    def first_step(row):
        step_ref[row] = tangent_row(
            rows_ref[row - 1], rows_ref[row], rows_ref[row + 1], east_ref[row], north_ref[row]
        )

    rows_loop(1, ROWS + 3, 3, first_step)

    def second_step(row):
        advanced = tangent_row(
            step_ref[row + 1], step_ref[row + 2], step_ref[row + 3],
            east_ref[row + 2], north_ref[row + 2],
        )
        first = inc_ref[row, 0]
        second = first + inc_ref[row, 1] - advanced[0:4]
        base_ref[row, 0] = first
        base_ref[row, 1] = second
        total = second - advanced[4:8]
        keep_ref[row] = jnp.where(is_first, total[0:2], total[2:4])
        send_ref[row] = jnp.where(is_first, total[2:4], total[0:2])

    rows_loop(0, ROWS, 5, second_step)


def adjoint_parts(here, east, north):
    along, across = east * here, north * here
    zero = jnp.zeros_like(here)
    kept = (1.0 - jnp.abs(east) - jnp.abs(north)) * here
    kept = kept + pltpu.roll(jnp.where(east > 0, along, zero), LON - 1, 1)
    kept = kept + pltpu.roll(jnp.where(east > 0, zero, -along), 1, 1)
    to_south = jnp.where(north > 0, across, zero)
    to_north = jnp.where(north > 0, zero, -across)
    return kept, to_south, to_north


def adjoint_kernel(
    dual_ref,
    low_ref,
    high_ref,
    wind_ref,
    ahead_ref,
    rim_low_ref,
    rim_high_ref,
    obs_ref,
    weight_ref,
    base_ref,
    sums_ref,
    keep_ref,
    send_ref,
    rows_ref,
    step_ref,
    back_ref,
    east_ref,
    north_ref,
):
    halo_rows(rows_ref, dual_ref, low_ref, high_ref, 8)

    def spread(row, early, block):
        east_ref[row] = paired(early[0:1], block[0:1])
        north_ref[row] = paired(early[1:2], block[1:2])

    for k in range(2):
        spread(k, rim_low_ref[k], low_ref[k, 16:18, :])
        spread(ROWS + 2 + k, rim_high_ref[k], high_ref[k, 16:18, :])
    rows_loop(0, ROWS, 5, lambda row: spread(row + 2, ahead_ref[row], wind_ref[row]))

    def sweep(source, target, begin, end, unroll):
        def parts(row):
            return adjoint_parts(source[row], east_ref[row], north_ref[row])

        def step(group, carry):
            pending, from_below = carry
            for k in range(unroll):
                row = begin + 1 + group * unroll + k
                kept, to_south, to_north = parts(row)
                target[row - 1] = pending + to_south
                pending, from_below = kept + from_below, to_north
            return pending, from_below

        kept, _, to_north = parts(begin)
        lax.fori_loop(0, (end - begin - 1) // unroll, step, (kept, to_north))

    sweep(rows_ref, step_ref, 0, ROWS + 4, 4)
    sweep(step_ref, back_ref, 1, ROWS + 3, 2)

    here = place().astype(F32)
    inner = jnp.minimum(here, 1.0)
    is_first = place() % 2 == 0

    def each(row):
        returned = back_ref[row + 2]
        before = inner * returned[0:4]
        dual_first, dual_second = dual_ref[row, 0], dual_ref[row, 1]
        third_first = dual_first + weight_ref[row, 0] * obs_ref[row, 0]
        third_second = dual_second + weight_ref[row, 1] * obs_ref[row, 1]
        base = third_first - returned[4:8] + third_second
        base_ref[row, 0] = base
        base_ref[row, 1] = third_second
        sums = dual_first + (2.0 * here) * before - (2.0 * here + 1.0) * base
        total = sums + dual_second - third_second
        sums_ref[row, 0] = sums
        sums_ref[row, 1] = total
        later = base - before
        lower = jnp.concatenate([later[0:2], total[0:2]], axis=0)
        upper = jnp.concatenate([later[2:4], total[2:4]], axis=0)
        keep_ref[row] = jnp.where(is_first, lower, upper)
        send_ref[row] = jnp.where(is_first, upper, lower)

    rows_loop(0, ROWS, 5, each)


def joined(is_first, own, other):
    return jnp.concatenate(
        [jnp.where(is_first, own, other), jnp.where(is_first, other, own)], axis=0
    )


def spread_kernel(
    base_ref,
    sums_ref,
    deviation_ref,
    own_ref,
    other_ref,
    model_keep_ref,
    model_received_ref,
    dual_ref,
    column_ref,
    model_ref,
    token_ref,
):
    token_ref[...] = jnp.zeros_like(token_ref)
    here = place().astype(F32)
    is_first = place() % 2 == 0

    def each(row):
        own, other = own_ref[row], other_ref[row]
        later = joined(is_first, own[0:2], other[0:2])
        earlier = joined(is_first, own[2:4], other[2:4])
        deviation = deviation_ref[row]
        for sub in range(SUBS):
            dual_ref[row, sub] = base_ref[row, sub] + later
            sums = earlier + sums_ref[row, sub] - (2.0 * here + (1.0 + sub)) * later
            scaled = deviation * sums
            for pair in range(2):
                for tile in range(TILES):
                    column_ref[sub * 16 + pair * 8 + tile, row] = scaled[
                        2 * pair : 2 * pair + 2, tile * LANES : (tile + 1) * LANES
                    ]
        model_ref[row] = model_keep_ref[row] + model_received_ref[row]

    rows_loop(0, ROWS, 5, each)


def obs_kernel(obs_ref, inc_ref, weight_ref, error_ref, out_ref, token_ref):
    token_ref[...] = jnp.zeros_like(token_ref)

    def each(row):
        error = error_ref[row]
        out_ref[row] = (error * obs_ref[row] + weight_ref[row] * inc_ref[row]) / error

    rows_loop(0, ROWS, 5, each)


def ready_kernel(keep_ref, received_ref, falling_ref, rising_ref, token_ref):
    token_ref[...] = jnp.zeros_like(token_ref)
    chip = place() // 2

    def each(row):
        total = keep_ref[row] + received_ref[row]
        later, earlier = total[0:2], total[2:4]
        falling_ref[row] = jnp.where(chip == 0, earlier, later)
        rising_ref[row] = jnp.where(chip == CHIPS - 1, later, earlier)

    rows_loop(0, ROWS, 5, each)


def carry_kernel(
    falling_ref, rising_ref, falling_on_ref, rising_on_ref, keep_ref, received_ref, own_ref, send_ref
):
    chip, is_first = place() // 2, place() % 2 == 0

    def each(row):
        falling, rising = falling_ref[row], rising_ref[row]
        keep, received = keep_ref[row], received_ref[row]
        zero = jnp.zeros_like(falling)
        later = jnp.where(chip < CHIPS - 1, falling, zero) + jnp.where(chip == 0, rising, zero)
        later = later + falling_on_ref[row]
        earlier = jnp.where(chip > 0, rising, zero) + jnp.where(chip == CHIPS - 1, falling, zero)
        earlier = earlier + rising_on_ref[row]
        own_ref[row, 0:2] = later + jnp.where(is_first, received[0:2], zero)
        own_ref[row, 2:4] = earlier + jnp.where(is_first, zero, received[2:4])
        send_ref[row, 0:2] = later + jnp.where(is_first, zero, keep[0:2])
        send_ref[row, 2:4] = earlier + jnp.where(is_first, keep[2:4], zero)

    rows_loop(0, ROWS, 5, each)


def model_kernel(up_ref, wrap_ref, on_ref, keep_ref, received_ref, own_ref, send_ref):
    is_first = place() % 2 == 0

    def each(row):
        earlier = up_ref[row] + wrap_ref[row] + on_ref[row]
        zero = jnp.zeros_like(earlier)
        own_ref[row] = earlier + jnp.where(is_first, zero, received_ref[row])
        send_ref[row] = earlier + jnp.where(is_first, keep_ref[row], zero)

    rows_loop(0, ROWS, 5, each)


def finish_kernel(column_ref, base_ref, deviation_ref, own_ref, other_ref, out_ref):
    is_first = place() % 2 == 0

    def each(row):
        earlier = joined(is_first, own_ref[row], other_ref[row])
        deviation = deviation_ref[row]
        for sub in range(SUBS):
            filtered = jnp.concatenate(
                [
                    jnp.concatenate(
                        [column_ref[sub * 16 + pair * 8 + tile, row] for tile in range(TILES)],
                        axis=1,
                    )
                    for pair in range(2)
                ],
                axis=0,
            )
            out_ref[row, sub] = deviation * filtered + (base_ref[row, sub] + earlier)

    rows_loop(0, ROWS, 5, each)


def body(
    dual_state,
    obs_dual,
    increment,
    wind_east,
    wind_north,
    deviation,
    merid_filter,
    obs_weight,
    obs_error,
):
    size = lax.axis_size("space")
    upward = [(i, i + 1) for i in range(size - 1)]
    downward = [(i + 1, i) for i in range(size - 1)]
    following = [(i, i + 1) for i in range(2 * CHIPS - 1)]
    swap = [(i, i ^ 1) for i in range(2 * CHIPS)]

    def aslant(pairs):
        return [(a * size + i, b * size + j) for a, b in following for i, j in pairs]

    def over_chips(pairs):
        return [(2 * a + c, 2 * b + c) for a, b in pairs for c in range(2)]

    rise = over_chips([(c, (c + 1) % CHIPS) for c in range(CHIPS)])
    fall = over_chips([((c + 1) % CHIPS, c) for c in range(CHIPS)])

    to_north, to_south, winds, ahead, ahead_north, ahead_south, token = edges(
        increment, dual_state, wind_east, wind_north
    )
    ahead = lax.ppermute(ahead, "tm", following)
    low = lax.ppermute(to_north, "space", upward)
    high = lax.ppermute(to_south, "space", downward)
    rim_low = lax.ppermute(ahead_north, ("tm", "space"), aslant(upward))
    rim_high = lax.ppermute(ahead_south, ("tm", "space"), aslant(downward))

    extended = pltpu.VMEM((ROWS + 4, 8, LON), F32)
    dual_base, dual_sums, keep, send = call(
        adjoint_kernel,
        [field(ROWS, SUBS, FIELDS, LON)] * 2 + [field(ROWS, FIELDS, LON)] * 2,
        [dual_state, low, high, winds, ahead, rim_low, rim_high, obs_dual, obs_weight],
        [extended] * 5,
        flops=60 * ROWS * 8 * LON,
    )

    received = lax.ppermute(send, "tm", swap)
    falling, rising, token = call(
        ready_kernel,
        [field(ROWS, 2, LON)] * 2 + [TOKEN],
        [keep, received],
        flops=4 * ROWS * 4 * LON,
    )
    falling = lax.ppermute(falling, "tm", fall)
    rising = lax.ppermute(rising, "tm", rise)

    filter_high, filter_low, token = call(
        square_kernel,
        [jax.ShapeDtypeStruct((LAT, LAT), BF16)] * 2 + [TOKEN],
        [merid_filter],
        [pltpu.VMEM((LAT, LAT), BF16)] * 2,
        after=[token],
        flops=6 * LAT**3,
    )
    falling, rising, token = hold([falling, rising, token], [filter_high])
    model_base, model_keep, model_send, token = call(
        tangent_kernel,
        [field(ROWS, SUBS, FIELDS, LON)] + [field(ROWS, 2, LON)] * 2 + [TOKEN],
        [increment, low, high, winds],
        [extended] * 4,
        after=[token],
        flops=40 * ROWS * 8 * LON,
    )
    model_received = lax.ppermute(model_send, "tm", swap)

    falling_on = lax.ppermute(falling, "tm", over_chips([(2, 1), (1, 0)]))
    rising_on = lax.ppermute(rising, "tm", over_chips([(1, 2), (2, 3)]))
    own, send = call(
        carry_kernel,
        [field(ROWS, FIELDS, LON)] * 2,
        [falling, rising, falling_on, rising_on, keep, received],
        after=[token],
        flops=10 * ROWS * 4 * LON,
    )
    other = lax.ppermute(send, "tm", swap)

    precond_dual, columns, model_chip, token = call(
        spread_kernel,
        [
            field(ROWS, SUBS, FIELDS, LON),
            field(SPACE, ROWS, 2, LANES),
            field(ROWS, 2, LON),
            TOKEN,
        ],
        [dual_base, dual_sums, deviation, own, other, model_keep, model_received],
        flops=10 * ROWS * 8 * LON,
    )

    columns = lax.all_to_all(columns, "space", split_axis=0, concat_axis=0, tiled=True)
    model_up = lax.ppermute(model_chip, "tm", over_chips([(0, 1), (1, 2), (2, 3)]))
    model_wrap = lax.ppermute(model_chip, "tm", over_chips([(0, 3)]))

    precond_obs, token = call(
        obs_kernel,
        [field(ROWS, SUBS, FIELDS, LON), TOKEN],
        [obs_dual, increment, obs_weight, obs_error],
        after=[token],
        flops=10 * ROWS * 8 * LON,
    )

    columns, token = call(
        filter_kernel,
        [field(2 * LAT, LANES), TOKEN],
        [filter_high, filter_low, columns.reshape(2 * LAT, LANES)],
        [pltpu.VMEM((LAT, 2 * LANES), BF16)] * 2,
        after=[token, model_up, model_wrap],
        flops=6 * LAT * LAT * 2 * LANES,
    )
    columns = lax.all_to_all(
        columns.reshape(SPACE, ROWS, 2, LANES), "space", split_axis=0, concat_axis=0, tiled=True
    )

    model_on = lax.ppermute(model_up, "tm", over_chips([(1, 2), (2, 3)]))
    model_own, model_send = call(
        model_kernel,
        [field(ROWS, 2, LON)] * 2,
        [model_up, model_wrap, model_on, model_keep, model_received],
        after=[token],
        flops=10 * ROWS * 2 * LON,
    )
    model_other = lax.ppermute(model_send, "tm", swap)

    (precond_increment,) = call(
        finish_kernel,
        [field(ROWS, SUBS, FIELDS, LON)],
        [columns, model_base, deviation, model_own, model_other],
        flops=4 * ROWS * 8 * LON,
    )
    return (precond_dual, precond_obs, precond_increment)


def solution(mesh):
    banded = P("space", "tm", None, None)
    placed = (
        banded,
        banded,
        banded,
        P("space", "tm", None),
        P("space", "tm", None),
        P("space", None, None),
        P(),
        banded,
        banded,
    )
    return jax.shard_map(
        body,
        mesh=mesh,
        in_specs=placed,
        out_specs=(banded, banded, banded),
        check_vma=False,
    )
```

```python
import jax
import jax.numpy as jnp
from jax import lax
from jax.experimental import pallas as pl
from jax.experimental.pallas import tpu as pltpu
from jax.sharding import PartitionSpec as P

ROWS, SUBS, FIELDS, LON = 25, 2, 4, 1024
LAT = 800
SPACE = 32
CHIPS = 4
BLOCK = 400
LANES = 128
TILES = LON // LANES
VMEM_LIMIT = 16 * 1024 * 1024
WHOLE_VMEM = 61 * 1024 * 1024
OBS_FLOPS = 10**11
SUM_FLOPS = 10**11

F32 = jnp.float32
BF16 = jnp.bfloat16
TOKEN = jax.ShapeDtypeStruct((8, LANES), F32)


HBM = pl.BlockSpec(memory_space=pltpu.HBM)
VMEM = pl.BlockSpec(memory_space=pltpu.VMEM)


def call(
    kernel, outs, operands, scratch=(), after=(), flops=0, far_ins=(), far_outs=(),
    limit=VMEM_LIMIT,
):
    count, made = len(operands), len(outs)

    def run(*refs):
        begin = count + len(after)
        kernel(*refs[:count], *refs[begin : begin + made], *refs[begin + made + 1 :])

    size = sum(4 * a.size for a in operands) + sum(4 * o.size for o in outs)
    return pl.pallas_call(
        run,
        out_shape=(*outs, TOKEN),
        in_specs=[HBM if k in far_ins else VMEM for k in range(count)] + [HBM] * len(after),
        out_specs=(*(HBM if k in far_outs else VMEM for k in range(made)), HBM),
        scratch_shapes=list(scratch),
        compiler_params=pltpu.CompilerParams(vmem_limit_bytes=limit),
        cost_estimate=pl.CostEstimate(flops=flops, bytes_accessed=size, transcendentals=0),
    )(*operands, *after)


def hold(array, after=(), flops=0):
    def run(*refs):
        pass

    return pl.pallas_call(
        run,
        out_shape=field(*array.shape),
        in_specs=[pl.BlockSpec(memory_space=pl.ANY)] * (1 + len(after)),
        out_specs=pl.BlockSpec(memory_space=pl.ANY),
        input_output_aliases={0: 0},
        compiler_params=pltpu.CompilerParams(vmem_limit_bytes=1024 * 1024),
        cost_estimate=pl.CostEstimate(flops=flops, bytes_accessed=0, transcendentals=0),
    )(array, *after)


def place():
    return lax.axis_index("tm")


def rows_loop(begin, end, unroll, each, then=None):
    @pl.loop(0, (end - begin) // unroll)
    def _(group):
        for k in range(unroll):
            each(begin + group * unroll + k)
        if then is not None:
            then(group)

    for row in range(end - (end - begin) % unroll, end):
        each(row)


GROUP = 5
GROUPS = ROWS // GROUP


def group_rows(group):
    return pl.ds(group * GROUP, GROUP)


def field(*shape):
    return jax.ShapeDtypeStruct(shape, F32)


def split(x):
    high = x.astype(BF16)
    return high, (x - high.astype(F32)).astype(BF16)


def dot3(a_high, a_low, b_high, b_low, dims):
    def one(a, b):
        return lax.dot_general(a, b, (dims, ((), ())), preferred_element_type=F32)

    return one(a_high, b_high) + (one(a_high, b_low) + one(a_low, b_high))


def edge_kernel(
    inc_ref,
    dual_ref,
    east_ref,
    north_ref,
    up_ref,
    down_ref,
    wind_ref,
    inc_rows,
    dual_rows,
    east_rows,
    north_rows,
    done,
):
    copies = [
        pltpu.make_async_copy(east_ref, east_rows, done.at[2, 0]),
        pltpu.make_async_copy(north_ref, north_rows, done.at[2, 1]),
    ]
    for k, rows in enumerate((pl.ds(0, 2), pl.ds(ROWS - 2, 2))):
        copies += [
            pltpu.make_async_copy(inc_ref.at[rows], inc_rows.at[k], done.at[k, 0]),
            pltpu.make_async_copy(dual_ref.at[rows], dual_rows.at[k], done.at[k, 1]),
        ]
    for copy in copies:
        copy.start()
    for copy in copies:
        copy.wait()

    for side, (target, begin) in enumerate(((down_ref, 0), (up_ref, ROWS - 2))):
        for k in range(2):
            for sub in range(SUBS):
                start = FIELDS * sub
                target[k, start : start + FIELDS, :] = inc_rows[side, k, sub]
                target[k, 8 + start : 8 + start + FIELDS, :] = dual_rows[side, k, sub]
                east = east_rows[begin + k, sub : sub + 1]
                north = north_rows[begin + k, sub : sub + 1]
                target[k, 16 + 2 * sub : 17 + 2 * sub, :] = east
                target[k, 17 + 2 * sub : 18 + 2 * sub, :] = north

    def each(row):
        east, north = east_rows[row], north_rows[row]
        wind_ref[row, 0:1] = east[0:1]
        wind_ref[row, 1:2] = north[0:1]
        wind_ref[row, 2:3] = east[1:2]
        wind_ref[row, 3:4] = north[1:2]

    rows_loop(0, ROWS, GROUP, each)


def edges(increment, dual_state, wind_east, wind_north):
    ends = pltpu.VMEM((2, 2, SUBS, FIELDS, LON), F32)
    wind = pltpu.VMEM((ROWS, SUBS, LON), F32)
    return call(
        edge_kernel,
        [field(2, 20, LON)] * 2 + [field(ROWS, 4, LON)],
        [increment, dual_state, wind_east, wind_north],
        [ends, ends, wind, wind, pltpu.SemaphoreType.DMA((3, 2))],
        far_ins=(0, 1, 2, 3),
        limit=WHOLE_VMEM,
    )


def ahead_kernel(low_ref, high_ref, wind_ref, ahead_ref):
    ahead_ref[0:2] = low_ref[:, 18:20, :]
    ahead_ref[ROWS + 2 : ROWS + 4] = high_ref[:, 18:20, :]

    def each(row):
        ahead_ref[row + 2] = wind_ref[row, 2:4]

    rows_loop(0, ROWS, GROUP, each)


def square_kernel(w_ref, high_ref, low_ref, w_high, w_low, out_high, out_low, done):
    high, low = split(w_ref[...])
    w_high[...] = high
    w_low[...] = low

    def copies(block):
        rows = pl.ds(pl.multiple_of(block * BLOCK, BLOCK), BLOCK)
        return (
            pltpu.make_async_copy(out_high.at[rows], high_ref.at[rows], done.at[0, block]),
            pltpu.make_async_copy(out_low.at[rows], low_ref.at[rows], done.at[1, block]),
        )

    @pl.loop(0, LAT // BLOCK)
    def _(block):
        rows = pl.ds(pl.multiple_of(block * BLOCK, BLOCK), BLOCK)
        product = dot3(w_high[rows, :], w_low[rows, :], w_high[...], w_low[...], ((1,), (1,)))
        product_high, product_low = split(product)
        out_high[rows, :] = product_high
        out_low[rows, :] = product_low
        for copy in copies(block):
            copy.start()

    @pl.loop(0, LAT // BLOCK)
    def _(block):
        for copy in copies(block):
            copy.wait()


def filter_kernel(
    high_ref, low_ref, x_ref, y_ref, high, low, x_high, x_low, y_rows, done, sent
):
    def pick(block):
        return pl.ds(pl.multiple_of(block * BLOCK, BLOCK), BLOCK)

    def copies(block):
        rows = pick(block)
        return (
            pltpu.make_async_copy(high_ref.at[rows], high.at[rows], done.at[0, block]),
            pltpu.make_async_copy(low_ref.at[rows], low.at[rows], done.at[1, block]),
        )

    def sending(block):
        rows = pl.ds(pl.multiple_of(2 * block * BLOCK, 2 * BLOCK), 2 * BLOCK)
        return pltpu.make_async_copy(y_rows.at[rows], y_ref.at[rows], sent.at[block])

    for block in range(LAT // BLOCK):
        for copy in copies(block):
            copy.start()
    for part in range(2):
        part_high, part_low = split(x_ref[pl.ds(part, LAT, stride=2), :])
        x_high[:, part * LANES : (part + 1) * LANES] = part_high
        x_low[:, part * LANES : (part + 1) * LANES] = part_low

    @pl.loop(0, LAT // BLOCK)
    def _(block):
        for copy in copies(block):
            copy.wait()
        rows = pick(block)
        product = dot3(high[rows, :], low[rows, :], x_high[...], x_low[...], ((1,), (0,)))
        for part in range(2):
            y_rows[pl.ds(2 * block * BLOCK + part, BLOCK, stride=2), :] = product[
                :, part * LANES : (part + 1) * LANES
            ]
        sending(block).start()

    @pl.loop(0, LAT // BLOCK)
    def _(block):
        sending(block).wait()


def paired(first, second):
    lower = lax.broadcasted_iota(jnp.int32, (2 * FIELDS, LON), 0) < FIELDS
    shape = (2 * FIELDS, LON)
    return jnp.where(lower, jnp.broadcast_to(first, shape), jnp.broadcast_to(second, shape))


def tangent_row(below, here, above, east, north):
    east_size, north_size = jnp.abs(east), jnp.abs(north)
    along = jnp.where(east > 0, pltpu.roll(here, 1, 1), pltpu.roll(here, LON - 1, 1))
    across = jnp.where(north > 0, below, above)
    return (1.0 - east_size - north_size) * here + east_size * along + north_size * across


def halo_rows(target, source, low, high, begin):
    target[0:2] = low[:, begin : begin + 8, :]
    target[ROWS + 2 : ROWS + 4] = high[:, begin : begin + 8, :]

    def each(row):
        target[row + 2] = jnp.concatenate([source[row, 0], source[row, 1]], axis=0)

    rows_loop(0, ROWS, 5, each)


def tangent_kernel(
    inc_ref,
    low_ref,
    high_ref,
    wind_ref,
    base_ref,
    total_ref,
    rows_ref,
    step_ref,
    east_ref,
    north_ref,
):
    halo_rows(rows_ref, inc_ref, low_ref, high_ref, 0)

    def spread(row, block):
        east_ref[row] = paired(block[0:1], block[2:3])
        north_ref[row] = paired(block[1:2], block[3:4])

    spread(1, low_ref[1, 16:20, :])
    spread(ROWS + 2, high_ref[0, 16:20, :])
    rows_loop(0, ROWS, 5, lambda row: spread(row + 2, wind_ref[row]))

    def first_step(row):
        step_ref[row] = tangent_row(
            rows_ref[row - 1], rows_ref[row], rows_ref[row + 1], east_ref[row], north_ref[row]
        )

    rows_loop(1, ROWS + 3, 3, first_step)

    def second_step(row):
        advanced = tangent_row(
            step_ref[row + 1], step_ref[row + 2], step_ref[row + 3],
            east_ref[row + 2], north_ref[row + 2],
        )
        first = inc_ref[row, 0]
        second = first + inc_ref[row, 1] - advanced[0:4]
        base_ref[row, 0] = first
        base_ref[row, 1] = second
        total_ref[row] = second - advanced[4:8]

    rows_loop(0, ROWS, 5, second_step)


def adjoint_parts(here, east, north):
    along, across = east * here, north * here
    zero = jnp.zeros_like(here)
    kept = (1.0 - jnp.abs(east) - jnp.abs(north)) * here
    kept = kept + pltpu.roll(jnp.where(east > 0, along, zero), LON - 1, 1)
    kept = kept + pltpu.roll(jnp.where(east > 0, zero, -along), 1, 1)
    to_south = jnp.where(north > 0, across, zero)
    to_north = jnp.where(north > 0, zero, -across)
    return kept, to_south, to_north


def adjoint_kernel(
    dual_ref,
    wind_ref,
    obs_ref,
    weight_ref,
    low_ref,
    high_ref,
    ahead_ref,
    base_ref,
    sums_ref,
    keep_ref,
    send_ref,
    rows_ref,
    step_ref,
    back_ref,
    east_ref,
    north_ref,
):
    halo_rows(rows_ref, dual_ref, low_ref, high_ref, 8)

    def spread(row, early, block):
        east_ref[row] = paired(early[0:1], block[0:1])
        north_ref[row] = paired(early[1:2], block[1:2])

    for k in range(2):
        spread(k, ahead_ref[k], low_ref[k, 16:18, :])
        spread(ROWS + 2 + k, ahead_ref[ROWS + 2 + k], high_ref[k, 16:18, :])
    rows_loop(0, ROWS, 5, lambda row: spread(row + 2, ahead_ref[row + 2], wind_ref[row]))

    def sweep(source, target, begin, end, unroll):
        def parts(row):
            return adjoint_parts(source[row], east_ref[row], north_ref[row])

        def step(group, carry):
            pending, from_below = carry
            for k in range(unroll):
                row = begin + 1 + group * unroll + k
                kept, to_south, to_north = parts(row)
                target[row - 1] = pending + to_south
                pending, from_below = kept + from_below, to_north
            return pending, from_below

        kept, _, to_north = parts(begin)
        lax.fori_loop(0, (end - begin - 1) // unroll, step, (kept, to_north))

    sweep(rows_ref, step_ref, 0, ROWS + 4, 4)
    sweep(step_ref, back_ref, 1, ROWS + 3, 2)

    here = place().astype(F32)
    inner = jnp.minimum(here, 1.0)
    is_first = place() % 2 == 0

    def each(row):
        returned = back_ref[row + 2]
        before = inner * returned[0:4]
        dual_first, dual_second = dual_ref[row, 0], dual_ref[row, 1]
        third_first = dual_first + weight_ref[row, 0] * obs_ref[row, 0]
        third_second = dual_second + weight_ref[row, 1] * obs_ref[row, 1]
        base = third_first - returned[4:8] + third_second
        base_ref[row, 0] = base
        base_ref[row, 1] = third_second
        sums = dual_first + (2.0 * here) * before - (2.0 * here + 1.0) * base
        total = sums + dual_second - third_second
        sums_ref[row, 0] = sums
        sums_ref[row, 1] = total
        later = base - before
        keep_ref[row] = jnp.where(is_first, later, total)
        send_ref[row] = jnp.where(is_first, total, later)

    rows_loop(0, ROWS, 5, each)


def spread_kernel(
    base_ref,
    sums_ref,
    deviation_ref,
    carry_ref,
    received_ref,
    other_ref,
    total_ref,
    total_received_ref,
    dual_ref,
    column_ref,
    model_ref,
):
    here = place().astype(F32)
    is_first = place() % 2 == 0

    def each(row):
        own, other = carry_ref[row] + received_ref[row], other_ref[row]
        later = jnp.where(is_first, own, other)
        earlier = jnp.where(is_first, other, own)
        deviation = deviation_ref[row]
        for sub in range(SUBS):
            dual_ref[row, sub] = base_ref[row, sub] + later
            sums = earlier + sums_ref[row, sub] - (2.0 * here + (1.0 + sub)) * later
            scaled = deviation * sums
            for pair in range(2):
                for tile in range(TILES):
                    column_ref[sub * 16 + pair * 8 + tile, row] = scaled[
                        2 * pair : 2 * pair + 2, tile * LANES : (tile + 1) * LANES
                    ]
        model_ref[row] = total_ref[row] + total_received_ref[row]

    rows_loop(0, ROWS, GROUP, each)


def obs_kernel(
    obs_far, inc_far, weight_far, error_far, out_far, obs, inc, weight, error, out, done, sent
):
    def copies(group):
        rows = group_rows(group)
        return [
            pltpu.make_async_copy(far.at[rows], near.at[rows], done.at[k, group])
            for k, (far, near) in enumerate(
                ((obs_far, obs), (inc_far, inc), (weight_far, weight), (error_far, error))
            )
        ]

    def sending(group):
        rows = group_rows(group)
        return pltpu.make_async_copy(out.at[rows], out_far.at[rows], sent.at[group])

    for group in range(GROUPS):
        for copy in copies(group):
            copy.start()

    @pl.loop(0, GROUPS)
    def _(group):
        for copy in copies(group):
            copy.wait()
        for k in range(GROUP):
            row = group * GROUP + k
            scale = error[row]
            out[row] = (scale * obs[row] + weight[row] * inc[row]) / scale
        sending(group).start()

    @pl.loop(0, GROUPS)
    def _(group):
        sending(group).wait()


def sum_kernel(*refs):
    def each(row):
        total = refs[0][row]
        for ref in refs[1:-1]:
            total = total + ref[row]
        refs[-1][row] = total

    rows_loop(0, ROWS, GROUP, each)


def finish_kernel(
    column_ref,
    base_ref,
    deviation_ref,
    own_ref,
    other_ref,
    received_ref,
    out_ref,
    out_rows,
    done,
):
    is_first = place() % 2 == 0

    def each(row):
        received = received_ref[row]
        earlier = own_ref[row] + other_ref[row]
        earlier = earlier + jnp.where(is_first, jnp.zeros_like(received), received)
        deviation = deviation_ref[row]
        for sub in range(SUBS):
            filtered = jnp.concatenate(
                [
                    jnp.concatenate(
                        [column_ref[sub * 16 + pair * 8 + tile, row] for tile in range(TILES)],
                        axis=1,
                    )
                    for pair in range(2)
                ],
                axis=0,
            )
            out_rows[row, sub] = deviation * filtered + (base_ref[row, sub] + earlier)

    def copy(group):
        rows = group_rows(group)
        return pltpu.make_async_copy(out_rows.at[rows], out_ref.at[rows], done.at[group])

    rows_loop(0, ROWS, GROUP, each, lambda group: copy(group).start())

    @pl.loop(0, GROUPS)
    def _(group):
        copy(group).wait()


def body(
    dual_state,
    obs_dual,
    increment,
    wind_east,
    wind_north,
    deviation,
    merid_filter,
    obs_weight,
    obs_error,
):
    size = lax.axis_size("space")
    upward = [(i, i + 1) for i in range(size - 1)]
    downward = [(i + 1, i) for i in range(size - 1)]
    following = [(i, i + 1) for i in range(2 * CHIPS - 1)]
    swap = [(i, i ^ 1) for i in range(2 * CHIPS)]

    def by_core(first, second):
        return [(2 * a, 2 * b) for a, b in first] + [(2 * a + 1, 2 * b + 1) for a, b in second]

    rise = [(c, c + 1) for c in range(CHIPS - 1)]
    fall = [(c + 1, c) for c in range(CHIPS - 1)]
    ends = (0, CHIPS - 1)
    whole, half = field(ROWS, SUBS, FIELDS, LON), field(ROWS, FIELDS, LON)

    to_north, to_south, winds, _ = edges(increment, dual_state, wind_east, wind_north)
    low = lax.ppermute(to_north, "space", upward)
    high = lax.ppermute(to_south, "space", downward)
    ahead, _ = call(ahead_kernel, [field(ROWS + 4, 2, LON)], [low, high, winds])
    ahead = lax.ppermute(ahead, "tm", following)

    extended = pltpu.VMEM((ROWS + 4, 8, LON), F32)
    whole_rows = pltpu.VMEM((ROWS, SUBS, FIELDS, LON), F32)
    model_base, model_total, token = call(
        tangent_kernel,
        [whole, half],
        [increment, low, high, winds],
        [extended] * 4,
        flops=40 * ROWS * 8 * LON,
    )
    dual_base, dual_sums, keep, send, _ = call(
        adjoint_kernel,
        [whole, whole, half, half],
        [dual_state, winds, obs_dual, obs_weight, low, high, ahead],
        [extended] * 5,
        after=[token],
        flops=60 * ROWS * 8 * LON,
    )

    received = lax.ppermute(send, "tm", swap)
    chip_total, token = call(sum_kernel, [half], [keep, received], flops=ROWS * 4 * LON)
    near = lax.ppermute(chip_total, "tm", by_core(fall, rise))
    wrapped = lax.ppermute(chip_total, "tm", by_core([ends[::-1]], [ends]))

    blocks = pltpu.SemaphoreType.DMA((2, LAT // BLOCK))
    square = pltpu.VMEM((LAT, LAT), BF16)
    filter_high, filter_low, token = call(
        square_kernel,
        [jax.ShapeDtypeStruct((LAT, LAT), BF16)] * 2,
        [merid_filter],
        [square] * 4 + [blocks],
        after=[token],
        flops=6 * LAT**3,
        far_outs=(0, 1),
    )
    near = hold(near, [token])
    on = lax.ppermute(near, "tm", by_core(fall[:2], rise[1:]))
    model_received = lax.ppermute(model_total, "tm", swap)

    carry, _ = call(sum_kernel, [half], [near, wrapped, on], flops=2 * ROWS * 4 * LON)
    other = lax.ppermute(carry, "tm", swap)

    precond_dual, columns, model_chip, token = call(
        spread_kernel,
        [whole, field(SPACE, ROWS, 2, LANES), half],
        [
            dual_base,
            dual_sums,
            deviation,
            carry,
            received,
            other,
            model_total,
            model_received,
        ],
        flops=10 * ROWS * 8 * LON,
    )

    columns = lax.all_to_all(columns, "space", split_axis=0, concat_axis=0, tiled=True)
    model_near = lax.ppermute(model_chip, "tm", by_core([ends], rise))

    precond_obs, token = call(
        obs_kernel,
        [whole],
        [obs_dual, increment, obs_weight, obs_error],
        [whole_rows] * 5
        + [pltpu.SemaphoreType.DMA((4, GROUPS)), pltpu.SemaphoreType.DMA((GROUPS,))],
        after=[precond_dual],
        flops=OBS_FLOPS,
        far_ins=(0, 1, 2, 3),
        far_outs=(0,),
        limit=WHOLE_VMEM,
    )

    columns, token = call(
        filter_kernel,
        [field(2 * LAT, LANES)],
        [filter_high, filter_low, columns.reshape(2 * LAT, LANES)],
        [square] * 2
        + [pltpu.VMEM((LAT, 2 * LANES), BF16)] * 2
        + [pltpu.VMEM((2 * LAT, LANES), F32), blocks]
        + [pltpu.SemaphoreType.DMA((LAT // BLOCK,))],
        after=[token, model_near],
        flops=6 * LAT * LAT * 2 * LANES,
        far_ins=(0, 1),
        far_outs=(0,),
        limit=63 * 1024 * 1024,
    )
    columns = lax.all_to_all(
        columns.reshape(SPACE, ROWS, 2, LANES), "space", split_axis=0, concat_axis=0, tiled=True
    )

    model_on = lax.ppermute(model_near, "tm", by_core([], rise[1:]))
    model_carry, _ = call(
        sum_kernel, [half], [model_near, model_on], after=[token], flops=SUM_FLOPS
    )
    model_other = lax.ppermute(model_carry, "tm", swap)

    precond_increment, _ = call(
        finish_kernel,
        [whole],
        [columns, model_base, deviation, model_carry, model_other, model_received],
        [whole_rows, pltpu.SemaphoreType.DMA((GROUPS,))],
        flops=4 * ROWS * 8 * LON,
        far_outs=(0,),
    )
    return (precond_dual, precond_obs, precond_increment)


def solution(mesh):
    banded = P("space", "tm", None, None)
    placed = (
        banded,
        banded,
        banded,
        P("space", "tm", None),
        P("space", "tm", None),
        P("space", None, None),
        P(),
        banded,
        banded,
    )
    return jax.shard_map(
        body,
        mesh=mesh,
        in_specs=placed,
        out_specs=(banded, banded, banded),
        check_vma=False,
    )
```

```python
import functools

import jax
import jax.numpy as jnp
from jax import lax
from jax.experimental import pallas as pl
from jax.experimental.pallas import tpu as pltpu
from jax.sharding import PartitionSpec as P

ROWS, SUBS, FIELDS, LON = 25, 2, 4, 1024
LAT = 800
SPACE = 32
CHIPS = 4
BLOCK = 400
LANES = 128
TILES = LON // LANES
VMEM_LIMIT = 16 * 1024 * 1024
WHOLE_VMEM = 61 * 1024 * 1024
THIRD_VMEM = 50 * 1024 * 1024
OBS_FLOPS = 10**11
SUM_FLOPS = 10**11

F32 = jnp.float32
BF16 = jnp.bfloat16
TOKEN = jax.ShapeDtypeStruct((8, LANES), F32)


HBM = pl.BlockSpec(memory_space=pltpu.HBM)
VMEM = pl.BlockSpec(memory_space=pltpu.VMEM)


def call(
    kernel, outs, operands, scratch=(), after=(), flops=0, far_ins=(), far_outs=(),
    limit=VMEM_LIMIT,
):
    count, made = len(operands), len(outs)

    def run(*refs):
        begin = count + len(after)
        kernel(*refs[:count], *refs[begin : begin + made], *refs[begin + made + 1 :])

    size = sum(4 * a.size for a in operands) + sum(4 * o.size for o in outs)
    return pl.pallas_call(
        run,
        out_shape=(*outs, TOKEN),
        in_specs=[HBM if k in far_ins else VMEM for k in range(count)] + [HBM] * len(after),
        out_specs=(*(HBM if k in far_outs else VMEM for k in range(made)), HBM),
        scratch_shapes=list(scratch),
        compiler_params=pltpu.CompilerParams(vmem_limit_bytes=limit),
        cost_estimate=pl.CostEstimate(flops=flops, bytes_accessed=size, transcendentals=0),
    )(*operands, *after)


def hold(array, after=(), flops=0):
    def run(*refs):
        pass

    return pl.pallas_call(
        run,
        out_shape=field(*array.shape),
        in_specs=[pl.BlockSpec(memory_space=pl.ANY)] * (1 + len(after)),
        out_specs=pl.BlockSpec(memory_space=pl.ANY),
        input_output_aliases={0: 0},
        compiler_params=pltpu.CompilerParams(vmem_limit_bytes=1024 * 1024),
        cost_estimate=pl.CostEstimate(flops=flops, bytes_accessed=0, transcendentals=0),
    )(array, *after)


def place():
    return lax.axis_index("tm")


def rows_loop(begin, end, unroll, each, then=None):
    @pl.loop(0, (end - begin) // unroll)
    def _(group):
        for k in range(unroll):
            each(begin + group * unroll + k)
        if then is not None:
            then(group)

    for row in range(end - (end - begin) % unroll, end):
        each(row)


GROUP = 5
GROUPS = ROWS // GROUP


def group_rows(group):
    return pl.ds(group * GROUP, GROUP)


def field(*shape):
    return jax.ShapeDtypeStruct(shape, F32)


def split(x):
    high = x.astype(BF16)
    return high, (x - high.astype(F32)).astype(BF16)


def dot3(a_high, a_low, b_high, b_low, dims):
    def one(a, b):
        return lax.dot_general(a, b, (dims, ((), ())), preferred_element_type=F32)

    return one(a_high, b_high) + (one(a_high, b_low) + one(a_low, b_high))


def edge_kernel(
    inc_ref,
    dual_ref,
    east_ref,
    north_ref,
    up_ref,
    down_ref,
    inc_up_ref,
    inc_down_ref,
    wind_ref,
    ahead_ref,
    inc_rows,
    dual_rows,
    east_rows,
    north_rows,
    done,
):
    copies = [
        pltpu.make_async_copy(east_ref, east_rows, done.at[2, 0]),
        pltpu.make_async_copy(north_ref, north_rows, done.at[2, 1]),
    ]
    for k, rows in enumerate((pl.ds(0, 2), pl.ds(ROWS - 2, 2))):
        copies += [
            pltpu.make_async_copy(inc_ref.at[rows], inc_rows.at[k], done.at[k, 0]),
            pltpu.make_async_copy(dual_ref.at[rows], dual_rows.at[k], done.at[k, 1]),
        ]
    for copy in copies:
        copy.start()
    for copy in copies:
        copy.wait()

    for side, (target, inc_target, begin) in enumerate(
        ((down_ref, inc_down_ref, 0), (up_ref, inc_up_ref, ROWS - 2))
    ):
        for k in range(2):
            for sub in range(SUBS):
                start = 8 * k + FIELDS * sub
                target[start : start + FIELDS, :] = dual_rows[side, k, sub]
                inc_target[start : start + FIELDS, :] = inc_rows[side, k, sub]
                at = 16 + 4 * k + 2 * sub
                target[at : at + 1, :] = east_rows[begin + k, sub : sub + 1]
                target[at + 1 : at + 2, :] = north_rows[begin + k, sub : sub + 1]

    def each(row):
        east, north = east_rows[row], north_rows[row]
        wind_ref[row, 0:1] = east[0:1]
        wind_ref[row, 1:2] = north[0:1]
        wind_ref[row, 2:3] = east[1:2]
        wind_ref[row, 3:4] = north[1:2]
        ahead_ref[row, 0:1] = east[1:2]
        ahead_ref[row, 1:2] = north[1:2]

    rows_loop(0, ROWS, GROUP, each)


def edges(increment, dual_state, wind_east, wind_north):
    ends = pltpu.VMEM((2, 2, SUBS, FIELDS, LON), F32)
    wind = pltpu.VMEM((ROWS, SUBS, LON), F32)
    return call(
        edge_kernel,
        [field(24, LON)] * 2
        + [field(16, LON)] * 2
        + [field(ROWS, 4, LON), field(ROWS, 2, LON)],
        [increment, dual_state, wind_east, wind_north],
        [ends, ends, wind, wind, pltpu.SemaphoreType.DMA((3, 2))],
        far_ins=(0, 1, 2, 3),
        limit=WHOLE_VMEM,
    )


def rim_kernel(low_ref, high_ref, rim_ref):
    for k in range(2):
        rim_ref[2 * k : 2 * k + 2, :] = low_ref[18 + 4 * k : 20 + 4 * k, :]
        rim_ref[4 + 2 * k : 6 + 2 * k, :] = high_ref[18 + 4 * k : 20 + 4 * k, :]


def square_kernel(begin, w_ref, high_ref, low_ref, w_high, w_low):
    high, low = split(w_ref[...])
    w_high[...] = high
    w_low[...] = low
    rows = slice(begin, begin + BLOCK)
    product = dot3(w_high[rows, :], w_low[rows, :], w_high[...], w_low[...], ((1,), (1,)))
    product_high, product_low = split(product)
    high_ref[...] = product_high
    low_ref[...] = product_low


def filter_kernel(
    first_high, first_low, second_high, second_low, x_ref, y_ref, high, low, x_high, x_low, y_rows,
    done, sent,
):
    copies = [
        [
            pltpu.make_async_copy(source, target.at[block], done.at[k, block])
            for k, (source, target) in enumerate(((block_high, high), (block_low, low)))
        ]
        for block, (block_high, block_low) in enumerate(
            ((first_high, first_low), (second_high, second_low))
        )
    ]
    for pair in copies:
        for copy in pair:
            copy.start()
    for part in range(2):
        part_high, part_low = split(x_ref[pl.ds(part, LAT, stride=2), :])
        x_high[:, part * LANES : (part + 1) * LANES] = part_high
        x_low[:, part * LANES : (part + 1) * LANES] = part_low

    sending = []
    for block in range(LAT // BLOCK):
        for copy in copies[block]:
            copy.wait()
        product = dot3(high[block], low[block], x_high[...], x_low[...], ((1,), (0,)))
        for part in range(2):
            y_rows[pl.ds(2 * block * BLOCK + part, BLOCK, stride=2), :] = product[
                :, part * LANES : (part + 1) * LANES
            ]
        rows = pl.ds(2 * block * BLOCK, 2 * BLOCK)
        sending.append(pltpu.make_async_copy(y_rows.at[rows], y_ref.at[rows], sent.at[block]))
        sending[-1].start()
    for copy in sending:
        copy.wait()


def paired(first, second):
    lower = lax.broadcasted_iota(jnp.int32, (2 * FIELDS, LON), 0) < FIELDS
    shape = (2 * FIELDS, LON)
    return jnp.where(lower, jnp.broadcast_to(first, shape), jnp.broadcast_to(second, shape))


def tangent_row(below, here, above, east, north):
    east_size, north_size = jnp.abs(east), jnp.abs(north)
    along = jnp.where(east > 0, pltpu.roll(here, 1, 1), pltpu.roll(here, LON - 1, 1))
    across = jnp.where(north > 0, below, above)
    return (1.0 - east_size - north_size) * here + east_size * along + north_size * across


def halo_rows(target, source, low, high):
    for k in range(2):
        target[k] = low[8 * k : 8 * k + 8, :]
        target[ROWS + 2 + k] = high[8 * k : 8 * k + 8, :]

    def each(row):
        target[row + 2] = jnp.concatenate([source[row, 0], source[row, 1]], axis=0)

    rows_loop(0, ROWS, 5, each)


def tangent_kernel(
    inc_ref,
    inc_low_ref,
    inc_high_ref,
    low_ref,
    high_ref,
    wind_ref,
    base_ref,
    total_ref,
    rows_ref,
    step_ref,
    east_ref,
    north_ref,
):
    halo_rows(rows_ref, inc_ref, inc_low_ref, inc_high_ref)

    def spread(row, block):
        east_ref[row] = paired(block[0:1], block[2:3])
        north_ref[row] = paired(block[1:2], block[3:4])

    spread(1, low_ref[20:24, :])
    spread(ROWS + 2, high_ref[16:20, :])
    rows_loop(0, ROWS, 5, lambda row: spread(row + 2, wind_ref[row]))

    def first_step(row):
        step_ref[row] = tangent_row(
            rows_ref[row - 1], rows_ref[row], rows_ref[row + 1], east_ref[row], north_ref[row]
        )

    rows_loop(1, ROWS + 3, 3, first_step)

    def second_step(row):
        advanced = tangent_row(
            step_ref[row + 1], step_ref[row + 2], step_ref[row + 3],
            east_ref[row + 2], north_ref[row + 2],
        )
        first = inc_ref[row, 0]
        second = first + inc_ref[row, 1] - advanced[0:4]
        base_ref[row, 0] = first
        base_ref[row, 1] = second
        total_ref[row] = second - advanced[4:8]

    rows_loop(0, ROWS, 5, second_step)


def adjoint_parts(here, east, north):
    along, across = east * here, north * here
    zero = jnp.zeros_like(here)
    kept = (1.0 - jnp.abs(east) - jnp.abs(north)) * here
    kept = kept + pltpu.roll(jnp.where(east > 0, along, zero), LON - 1, 1)
    kept = kept + pltpu.roll(jnp.where(east > 0, zero, -along), 1, 1)
    to_south = jnp.where(north > 0, across, zero)
    to_north = jnp.where(north > 0, zero, -across)
    return kept, to_south, to_north


def third_kernel(
    dual_far, obs_far, weight_far, wind_far, rows_ref, third_ref, wind_ref, dual, obs, weight, done
):
    def copies(group):
        rows = group_rows(group)
        return [
            pltpu.make_async_copy(far.at[rows], near.at[rows], done.at[k, group])
            for k, (far, near) in enumerate(
                ((dual_far, dual), (obs_far, obs), (weight_far, weight), (wind_far, wind_ref))
            )
        ]

    for group in range(GROUPS):
        for copy in copies(group):
            copy.start()

    @pl.loop(0, GROUPS)
    def _(group):
        for copy in copies(group):
            copy.wait()
        for k in range(GROUP):
            row = group * GROUP + k
            first, second = dual[row, 0], dual[row, 1]
            rows_ref[row] = jnp.concatenate([first, second], axis=0)
            third_ref[row, 0] = first + weight[row, 0] * obs[row, 0]
            third_ref[row, 1] = second + weight[row, 1] * obs[row, 1]


def adjoint_kernel(
    own_ref,
    third_ref,
    wind_ref,
    low_ref,
    high_ref,
    ahead_ref,
    rim_ref,
    base_ref,
    sums_ref,
    keep_ref,
    send_ref,
    rows_ref,
    step_ref,
    back_ref,
    east_ref,
    north_ref,
):
    def spread(row, early, block):
        east_ref[row] = paired(early[0:1], block[0:1])
        north_ref[row] = paired(early[1:2], block[1:2])

    for k in range(2):
        at = 16 + 4 * k
        spread(k, rim_ref[2 * k : 2 * k + 2, :], low_ref[at : at + 2, :])
        spread(ROWS + 2 + k, rim_ref[4 + 2 * k : 6 + 2 * k, :], high_ref[at : at + 2, :])
    rows_loop(0, ROWS, 5, lambda row: spread(row + 2, ahead_ref[row], wind_ref[row]))
    rows_ref[2 : ROWS + 2] = own_ref[...]
    for k in range(2):
        rows_ref[k] = low_ref[8 * k : 8 * k + 8, :]
        rows_ref[ROWS + 2 + k] = high_ref[8 * k : 8 * k + 8, :]

    def sweep(source, target, begin, end, unroll):
        def parts(row):
            return adjoint_parts(source[row], east_ref[row], north_ref[row])

        def step(group, carry):
            pending, from_below = carry
            for k in range(unroll):
                row = begin + 1 + group * unroll + k
                kept, to_south, to_north = parts(row)
                target[row - 1] = pending + to_south
                pending, from_below = kept + from_below, to_north
            return pending, from_below

        kept, _, to_north = parts(begin)
        lax.fori_loop(0, (end - begin - 1) // unroll, step, (kept, to_north))

    sweep(rows_ref, step_ref, 0, ROWS + 4, 4)
    sweep(step_ref, back_ref, 1, ROWS + 3, 2)

    here = place().astype(F32)
    inner = jnp.minimum(here, 1.0)
    is_first = place() % 2 == 0

    def each(row):
        returned = back_ref[row + 2]
        before = inner * returned[0:4]
        dual_first, dual_second = own_ref[row, 0:4], own_ref[row, 4:8]
        third_first, third_second = third_ref[row, 0], third_ref[row, 1]
        base = third_first - returned[4:8] + third_second
        base_ref[row, 0] = base
        base_ref[row, 1] = third_second
        sums = dual_first + (2.0 * here) * before - (2.0 * here + 1.0) * base
        total = sums + dual_second - third_second
        sums_ref[row, 0] = sums
        sums_ref[row, 1] = total
        later = base - before
        keep_ref[row] = jnp.where(is_first, later, total)
        send_ref[row] = jnp.where(is_first, total, later)

    rows_loop(0, ROWS, GROUP, each)


def spread_kernel(
    base_ref,
    sums_ref,
    deviation_ref,
    carry_ref,
    received_ref,
    other_ref,
    total_ref,
    total_received_ref,
    dual_ref,
    column_ref,
    model_ref,
):
    here = place().astype(F32)
    is_first = place() % 2 == 0

    def each(row):
        own, other = carry_ref[row] + received_ref[row], other_ref[row]
        later = jnp.where(is_first, own, other)
        earlier = jnp.where(is_first, other, own)
        deviation = deviation_ref[row]
        for sub in range(SUBS):
            dual_ref[row, sub] = base_ref[row, sub] + later
            sums = earlier + sums_ref[row, sub] - (2.0 * here + (1.0 + sub)) * later
            scaled = deviation * sums
            for pair in range(2):
                for tile in range(TILES):
                    column_ref[sub * 16 + pair * 8 + tile, row] = scaled[
                        2 * pair : 2 * pair + 2, tile * LANES : (tile + 1) * LANES
                    ]
        model_ref[row] = total_ref[row] + total_received_ref[row]

    rows_loop(0, ROWS, GROUP, each)


def obs_kernel(
    obs_far, inc_far, weight_far, error_far, out_far, obs, inc, weight, error, out, done, sent
):
    def copies(group):
        rows = group_rows(group)
        return [
            pltpu.make_async_copy(far.at[rows], near.at[rows], done.at[k, group])
            for k, (far, near) in enumerate(
                ((obs_far, obs), (inc_far, inc), (weight_far, weight), (error_far, error))
            )
        ]

    def sending(group):
        rows = group_rows(group)
        return pltpu.make_async_copy(out.at[rows], out_far.at[rows], sent.at[group])

    for group in range(GROUPS):
        for copy in copies(group):
            copy.start()

    @pl.loop(0, GROUPS)
    def _(group):
        for copy in copies(group):
            copy.wait()
        for k in range(GROUP):
            row = group * GROUP + k
            scale = error[row]
            out[row] = (scale * obs[row] + weight[row] * inc[row]) / scale
        sending(group).start()

    @pl.loop(0, GROUPS)
    def _(group):
        sending(group).wait()


def sum_kernel(*refs):
    def each(row):
        total = refs[0][row]
        for ref in refs[1:-1]:
            total = total + ref[row]
        refs[-1][row] = total

    rows_loop(0, ROWS, GROUP, each)


def finish_kernel(
    column_ref,
    base_ref,
    deviation_ref,
    own_ref,
    other_ref,
    received_ref,
    out_ref,
    out_rows,
    done,
):
    is_first = place() % 2 == 0

    def each(row):
        received = received_ref[row]
        earlier = own_ref[row] + other_ref[row]
        earlier = earlier + jnp.where(is_first, jnp.zeros_like(received), received)
        deviation = deviation_ref[row]
        for sub in range(SUBS):
            filtered = jnp.concatenate(
                [
                    jnp.concatenate(
                        [column_ref[sub * 16 + pair * 8 + tile, row] for tile in range(TILES)],
                        axis=1,
                    )
                    for pair in range(2)
                ],
                axis=0,
            )
            out_rows[row, sub] = deviation * filtered + (base_ref[row, sub] + earlier)

    def copy(group):
        rows = group_rows(group)
        return pltpu.make_async_copy(out_rows.at[rows], out_ref.at[rows], done.at[group])

    rows_loop(0, ROWS, GROUP, each, lambda group: copy(group).start())

    @pl.loop(0, GROUPS)
    def _(group):
        copy(group).wait()


def body(
    dual_state,
    obs_dual,
    increment,
    wind_east,
    wind_north,
    deviation,
    merid_filter,
    obs_weight,
    obs_error,
):
    size = lax.axis_size("space")
    upward = [(i, i + 1) for i in range(size - 1)]
    downward = [(i + 1, i) for i in range(size - 1)]
    following = [(i, i + 1) for i in range(2 * CHIPS - 1)]
    swap = [(i, i ^ 1) for i in range(2 * CHIPS)]

    def by_core(first, second):
        return [(2 * a, 2 * b) for a, b in first] + [(2 * a + 1, 2 * b + 1) for a, b in second]

    rise = [(c, c + 1) for c in range(CHIPS - 1)]
    fall = [(c + 1, c) for c in range(CHIPS - 1)]
    ends = (0, CHIPS - 1)
    whole, half = field(ROWS, SUBS, FIELDS, LON), field(ROWS, FIELDS, LON)

    to_north, to_south, inc_north, inc_south, winds, ahead, _ = edges(
        increment, dual_state, wind_east, wind_north
    )
    low = lax.ppermute(to_north, "space", upward)
    high = lax.ppermute(to_south, "space", downward)
    ahead = lax.ppermute(ahead, "tm", following)
    inc_low = lax.ppermute(inc_north, "space", upward)
    inc_high = lax.ppermute(inc_south, "space", downward)
    rim, _ = call(rim_kernel, [field(8, LON)], [low, high])
    rim = lax.ppermute(rim, "tm", following)

    extended = pltpu.VMEM((ROWS + 4, 8, LON), F32)
    whole_rows = pltpu.VMEM((ROWS, SUBS, FIELDS, LON), F32)
    own_rows, third, near_winds, _ = call(
        third_kernel,
        [field(ROWS, 8, LON), whole, half],
        [dual_state, obs_dual, obs_weight, winds],
        [whole_rows] * 3 + [pltpu.SemaphoreType.DMA((4, GROUPS))],
        flops=4 * ROWS * 8 * LON,
        far_ins=(0, 1, 2, 3),
        limit=THIRD_VMEM,
    )
    dual_base, dual_sums, keep, send, _ = call(
        adjoint_kernel,
        [whole, whole, half, half],
        [own_rows, third, near_winds, low, high, ahead, rim],
        [extended] * 5,
        flops=60 * ROWS * 8 * LON,
    )

    received = lax.ppermute(send, "tm", swap)
    chip_total, token = call(sum_kernel, [half], [keep, received], flops=ROWS * 4 * LON)
    near = lax.ppermute(chip_total, "tm", by_core(fall, rise))
    wrapped = lax.ppermute(chip_total, "tm", by_core([ends[::-1]], [ends]))

    square = pltpu.VMEM((LAT, LAT), BF16)

    def square_half(begin, after):
        return call(
            functools.partial(square_kernel, begin),
            [jax.ShapeDtypeStruct((BLOCK, LAT), BF16)] * 2,
            [merid_filter],
            [square] * 2,
            after=after,
            flops=3 * LAT**3,
        )

    first_high, first_low, token = square_half(0, [token])
    near = hold(near, [token])
    on = lax.ppermute(near, "tm", by_core(fall[:2], rise[1:]))
    second_high, second_low, token = square_half(BLOCK, [near])
    model_base, model_total, token = call(
        tangent_kernel,
        [whole, half],
        [increment, inc_low, inc_high, low, high, winds],
        [extended] * 4,
        after=[token],
        flops=40 * ROWS * 8 * LON,
    )
    model_received = lax.ppermute(model_total, "tm", swap)

    carry, _ = call(
        sum_kernel, [half], [near, wrapped, on], after=[token], flops=2 * ROWS * 4 * LON
    )
    other = lax.ppermute(carry, "tm", swap)

    precond_dual, columns, model_chip, token = call(
        spread_kernel,
        [whole, field(SPACE, ROWS, 2, LANES), half],
        [
            dual_base,
            dual_sums,
            deviation,
            carry,
            received,
            other,
            model_total,
            model_received,
        ],
        flops=10 * ROWS * 8 * LON,
    )

    columns = lax.all_to_all(columns, "space", split_axis=0, concat_axis=0, tiled=True)
    model_near = lax.ppermute(model_chip, "tm", by_core([ends], rise))

    precond_obs, token = call(
        obs_kernel,
        [whole],
        [obs_dual, increment, obs_weight, obs_error],
        [whole_rows] * 5
        + [pltpu.SemaphoreType.DMA((4, GROUPS)), pltpu.SemaphoreType.DMA((GROUPS,))],
        after=[precond_dual],
        flops=OBS_FLOPS,
        far_ins=(0, 1, 2, 3),
        far_outs=(0,),
        limit=WHOLE_VMEM,
    )

    columns, token = call(
        filter_kernel,
        [field(2 * LAT, LANES)],
        [first_high, first_low, second_high, second_low, columns.reshape(2 * LAT, LANES)],
        [pltpu.VMEM((LAT // BLOCK, BLOCK, LAT), BF16)] * 2
        + [pltpu.VMEM((LAT, 2 * LANES), BF16)] * 2
        + [pltpu.VMEM((2 * LAT, LANES), F32), pltpu.SemaphoreType.DMA((2, LAT // BLOCK))]
        + [pltpu.SemaphoreType.DMA((LAT // BLOCK,))],
        after=[token, model_near],
        flops=6 * LAT * LAT * 2 * LANES,
        far_ins=(0, 1, 2, 3),
        far_outs=(0,),
        limit=63 * 1024 * 1024,
    )
    columns = lax.all_to_all(
        columns.reshape(SPACE, ROWS, 2, LANES), "space", split_axis=0, concat_axis=0, tiled=True
    )

    model_on = lax.ppermute(model_near, "tm", by_core([], rise[1:]))
    model_carry, _ = call(
        sum_kernel, [half], [model_near, model_on], after=[token], flops=SUM_FLOPS
    )
    model_other = lax.ppermute(model_carry, "tm", swap)

    precond_increment, _ = call(
        finish_kernel,
        [whole],
        [columns, model_base, deviation, model_carry, model_other, model_received],
        [whole_rows, pltpu.SemaphoreType.DMA((GROUPS,))],
        flops=4 * ROWS * 8 * LON,
        far_outs=(0,),
    )
    return (precond_dual, precond_obs, precond_increment)


def solution(mesh):
    banded = P("space", "tm", None, None)
    placed = (
        banded,
        banded,
        banded,
        P("space", "tm", None),
        P("space", "tm", None),
        P("space", None, None),
        P(),
        banded,
        banded,
    )
    return jax.shard_map(
        body,
        mesh=mesh,
        in_specs=placed,
        out_specs=(banded, banded, banded),
        check_vma=False,
    )
```

```python
import functools

import jax
import jax.numpy as jnp
from jax import lax
from jax.experimental import pallas as pl
from jax.experimental.pallas import tpu as pltpu
from jax.sharding import PartitionSpec as P

ROWS, SUBS, FIELDS, LON = 25, 2, 4, 1024
LAT = 800
SPACE = 32
CHIPS = 4
BLOCK = 400
LANES = 128
TILES = LON // LANES
VMEM_LIMIT = 16 * 1024 * 1024
WHOLE_VMEM = 61 * 1024 * 1024
OBS_FLOPS = 10**11
SUM_FLOPS = 10**11

F32 = jnp.float32
BF16 = jnp.bfloat16
TOKEN = jax.ShapeDtypeStruct((8, LANES), F32)


HBM = pl.BlockSpec(memory_space=pltpu.HBM)
VMEM = pl.BlockSpec(memory_space=pltpu.VMEM)


def call(
    kernel, outs, operands, scratch=(), after=(), flops=0, far_ins=(), far_outs=(),
    limit=VMEM_LIMIT,
):
    count, made = len(operands), len(outs)

    def run(*refs):
        begin = count + len(after)
        kernel(*refs[:count], *refs[begin : begin + made], *refs[begin + made + 1 :])

    size = sum(4 * a.size for a in operands) + sum(4 * o.size for o in outs)
    return pl.pallas_call(
        run,
        out_shape=(*outs, TOKEN),
        in_specs=[HBM if k in far_ins else VMEM for k in range(count)] + [HBM] * len(after),
        out_specs=(*(HBM if k in far_outs else VMEM for k in range(made)), HBM),
        scratch_shapes=list(scratch),
        compiler_params=pltpu.CompilerParams(vmem_limit_bytes=limit),
        cost_estimate=pl.CostEstimate(flops=flops, bytes_accessed=size, transcendentals=0),
    )(*operands, *after)


def hold(array, after=(), flops=0):
    def run(*refs):
        pass

    return pl.pallas_call(
        run,
        out_shape=field(*array.shape),
        in_specs=[pl.BlockSpec(memory_space=pl.ANY)] * (1 + len(after)),
        out_specs=pl.BlockSpec(memory_space=pl.ANY),
        input_output_aliases={0: 0},
        compiler_params=pltpu.CompilerParams(vmem_limit_bytes=1024 * 1024),
        cost_estimate=pl.CostEstimate(flops=flops, bytes_accessed=0, transcendentals=0),
    )(array, *after)


def place():
    return lax.axis_index("tm")


def rows_loop(begin, end, unroll, each, then=None):
    @pl.loop(0, (end - begin) // unroll)
    def _(group):
        for k in range(unroll):
            each(begin + group * unroll + k)
        if then is not None:
            then(group)

    for row in range(end - (end - begin) % unroll, end):
        each(row)


GROUP = 5
GROUPS = ROWS // GROUP


def group_rows(group):
    return pl.ds(group * GROUP, GROUP)


def field(*shape):
    return jax.ShapeDtypeStruct(shape, F32)


def split(x):
    high = x.astype(BF16)
    return high, (x - high.astype(F32)).astype(BF16)


def dot3(a_high, a_low, b_high, b_low, dims):
    def one(a, b):
        return lax.dot_general(a, b, (dims, ((), ())), preferred_element_type=F32)

    return one(a_high, b_high) + (one(a_high, b_low) + one(a_low, b_high))


def edge_kernel(
    inc_ref,
    dual_ref,
    east_ref,
    north_ref,
    up_ref,
    down_ref,
    wind_ref,
    ahead_ref,
    inc_rows,
    dual_rows,
    east_rows,
    north_rows,
    done,
):
    copies = [
        pltpu.make_async_copy(east_ref, east_rows, done.at[2, 0]),
        pltpu.make_async_copy(north_ref, north_rows, done.at[2, 1]),
    ]
    for k, rows in enumerate((pl.ds(0, 2), pl.ds(ROWS - 2, 2))):
        copies += [
            pltpu.make_async_copy(inc_ref.at[rows], inc_rows.at[k], done.at[k, 0]),
            pltpu.make_async_copy(dual_ref.at[rows], dual_rows.at[k], done.at[k, 1]),
        ]
    for copy in copies:
        copy.start()
    for copy in copies:
        copy.wait()

    for side, (target, begin) in enumerate(((down_ref, 0), (up_ref, ROWS - 2))):
        for k in range(2):
            for sub in range(SUBS):
                start = 8 * k + FIELDS * sub
                target[start : start + FIELDS, :] = dual_rows[side, k, sub]
                target[24 + start : 24 + start + FIELDS, :] = inc_rows[side, k, sub]
                at = 16 + 4 * k + 2 * sub
                target[at : at + 1, :] = east_rows[begin + k, sub : sub + 1]
                target[at + 1 : at + 2, :] = north_rows[begin + k, sub : sub + 1]

    def each(row):
        east, north = east_rows[row], north_rows[row]
        wind_ref[row, 0:1] = east[0:1]
        wind_ref[row, 1:2] = north[0:1]
        wind_ref[row, 2:3] = east[1:2]
        wind_ref[row, 3:4] = north[1:2]
        ahead_ref[row, 0:1] = east[1:2]
        ahead_ref[row, 1:2] = north[1:2]

    rows_loop(0, ROWS, GROUP, each)


def edges(increment, dual_state, wind_east, wind_north):
    ends = pltpu.VMEM((2, 2, SUBS, FIELDS, LON), F32)
    wind = pltpu.VMEM((ROWS, SUBS, LON), F32)
    return call(
        edge_kernel,
        [field(40, LON)] * 2 + [field(ROWS, 4, LON), field(ROWS, 2, LON)],
        [increment, dual_state, wind_east, wind_north],
        [ends, ends, wind, wind, pltpu.SemaphoreType.DMA((3, 2))],
        far_ins=(0, 1, 2, 3),
        limit=WHOLE_VMEM,
    )


def rim_kernel(low_ref, high_ref, rim_ref):
    for k in range(2):
        rim_ref[2 * k : 2 * k + 2, :] = low_ref[18 + 4 * k : 20 + 4 * k, :]
        rim_ref[4 + 2 * k : 6 + 2 * k, :] = high_ref[18 + 4 * k : 20 + 4 * k, :]


def square_kernel(begin, w_ref, high_ref, low_ref, w_high, w_low):
    high, low = split(w_ref[...])
    w_high[...] = high
    w_low[...] = low
    rows = slice(begin, begin + BLOCK)
    product = dot3(w_high[rows, :], w_low[rows, :], w_high[...], w_low[...], ((1,), (1,)))
    product_high, product_low = split(product)
    high_ref[...] = product_high
    low_ref[...] = product_low


def filter_kernel(
    first_high, first_low, second_high, second_low, x_ref, y_ref, high, low, x_high, x_low, y_rows,
    done, sent,
):
    copies = [
        pltpu.make_async_copy(source, target.at[pl.ds(block * BLOCK, BLOCK)], done.at[k, block])
        for block, pair in enumerate(((first_high, first_low), (second_high, second_low)))
        for k, (source, target) in enumerate(zip(pair, (high, low)))
    ]
    for copy in copies:
        copy.start()
    for part in range(2):
        part_high, part_low = split(x_ref[pl.ds(part, LAT, stride=2), :])
        x_high[:, part * LANES : (part + 1) * LANES] = part_high
        x_low[:, part * LANES : (part + 1) * LANES] = part_low
    for copy in copies:
        copy.wait()

    def sending(block):
        rows = pl.ds(pl.multiple_of(2 * block * BLOCK, 2 * BLOCK), 2 * BLOCK)
        return pltpu.make_async_copy(y_rows.at[rows], y_ref.at[rows], sent.at[block])

    @pl.loop(0, LAT // BLOCK)
    def _(block):
        rows = pl.ds(pl.multiple_of(block * BLOCK, BLOCK), BLOCK)
        product = dot3(high[rows, :], low[rows, :], x_high[...], x_low[...], ((1,), (0,)))
        for part in range(2):
            y_rows[pl.ds(2 * block * BLOCK + part, BLOCK, stride=2), :] = product[
                :, part * LANES : (part + 1) * LANES
            ]
        sending(block).start()

    @pl.loop(0, LAT // BLOCK)
    def _(block):
        sending(block).wait()


def paired(first, second):
    lower = lax.broadcasted_iota(jnp.int32, (2 * FIELDS, LON), 0) < FIELDS
    shape = (2 * FIELDS, LON)
    return jnp.where(lower, jnp.broadcast_to(first, shape), jnp.broadcast_to(second, shape))


def tangent_row(below, here, above, east, north):
    east_size, north_size = jnp.abs(east), jnp.abs(north)
    along = jnp.where(east > 0, pltpu.roll(here, 1, 1), pltpu.roll(here, LON - 1, 1))
    across = jnp.where(north > 0, below, above)
    return (1.0 - east_size - north_size) * here + east_size * along + north_size * across


def halo_rows(target, source, low, high):
    for k in range(2):
        target[k] = low[24 + 8 * k : 32 + 8 * k, :]
        target[ROWS + 2 + k] = high[24 + 8 * k : 32 + 8 * k, :]

    def each(row):
        target[row + 2] = jnp.concatenate([source[row, 0], source[row, 1]], axis=0)

    rows_loop(0, ROWS, 5, each)


def tangent_kernel(
    inc_ref,
    low_ref,
    high_ref,
    wind_ref,
    base_ref,
    total_ref,
    rows_ref,
    step_ref,
    east_ref,
    north_ref,
):
    halo_rows(rows_ref, inc_ref, low_ref, high_ref)

    def spread(row, block):
        east_ref[row] = paired(block[0:1], block[2:3])
        north_ref[row] = paired(block[1:2], block[3:4])

    spread(1, low_ref[20:24, :])
    spread(ROWS + 2, high_ref[16:20, :])
    rows_loop(0, ROWS, 5, lambda row: spread(row + 2, wind_ref[row]))

    def first_step(row):
        step_ref[row] = tangent_row(
            rows_ref[row - 1], rows_ref[row], rows_ref[row + 1], east_ref[row], north_ref[row]
        )

    rows_loop(1, ROWS + 3, 3, first_step)

    def second_step(row):
        advanced = tangent_row(
            step_ref[row + 1], step_ref[row + 2], step_ref[row + 3],
            east_ref[row + 2], north_ref[row + 2],
        )
        first = inc_ref[row, 0]
        second = first + inc_ref[row, 1] - advanced[0:4]
        base_ref[row, 0] = first
        base_ref[row, 1] = second
        total_ref[row] = second - advanced[4:8]

    rows_loop(0, ROWS, 5, second_step)


def adjoint_parts(here, east, north):
    along, across = east * here, north * here
    zero = jnp.zeros_like(here)
    kept = (1.0 - jnp.abs(east) - jnp.abs(north)) * here
    kept = kept + pltpu.roll(jnp.where(east > 0, along, zero), LON - 1, 1)
    kept = kept + pltpu.roll(jnp.where(east > 0, zero, -along), 1, 1)
    to_south = jnp.where(north > 0, across, zero)
    to_north = jnp.where(north > 0, zero, -across)
    return kept, to_south, to_north


def third_kernel(dual_ref, obs_ref, weight_ref, rows_ref, third_ref):
    def each(row):
        first, second = dual_ref[row, 0], dual_ref[row, 1]
        rows_ref[row] = jnp.concatenate([first, second], axis=0)
        third_ref[row, 0] = first + weight_ref[row, 0] * obs_ref[row, 0]
        third_ref[row, 1] = second + weight_ref[row, 1] * obs_ref[row, 1]

    rows_loop(0, ROWS, GROUP, each)


def adjoint_kernel(
    own_ref,
    third_ref,
    wind_ref,
    low_ref,
    high_ref,
    ahead_ref,
    rim_ref,
    base_ref,
    sums_ref,
    keep_ref,
    send_ref,
    rows_ref,
    step_ref,
    back_ref,
    east_ref,
    north_ref,
):
    def spread(row, early, block):
        east_ref[row] = paired(early[0:1], block[0:1])
        north_ref[row] = paired(early[1:2], block[1:2])

    for k in range(2):
        at = 16 + 4 * k
        spread(k, rim_ref[2 * k : 2 * k + 2, :], low_ref[at : at + 2, :])
        spread(ROWS + 2 + k, rim_ref[4 + 2 * k : 6 + 2 * k, :], high_ref[at : at + 2, :])
    rows_loop(0, ROWS, 5, lambda row: spread(row + 2, ahead_ref[row], wind_ref[row]))
    rows_ref[2 : ROWS + 2] = own_ref[...]
    for k in range(2):
        rows_ref[k] = low_ref[8 * k : 8 * k + 8, :]
        rows_ref[ROWS + 2 + k] = high_ref[8 * k : 8 * k + 8, :]

    def sweep(source, target, begin, end, unroll):
        def parts(row):
            return adjoint_parts(source[row], east_ref[row], north_ref[row])

        def step(group, carry):
            pending, from_below = carry
            for k in range(unroll):
                row = begin + 1 + group * unroll + k
                kept, to_south, to_north = parts(row)
                target[row - 1] = pending + to_south
                pending, from_below = kept + from_below, to_north
            return pending, from_below

        kept, _, to_north = parts(begin)
        lax.fori_loop(0, (end - begin - 1) // unroll, step, (kept, to_north))

    sweep(rows_ref, step_ref, 0, ROWS + 4, 4)
    sweep(step_ref, back_ref, 1, ROWS + 3, 2)

    here = place().astype(F32)
    inner = jnp.minimum(here, 1.0)
    is_first = place() % 2 == 0

    def each(row):
        returned = back_ref[row + 2]
        before = inner * returned[0:4]
        dual_first, dual_second = own_ref[row, 0:4], own_ref[row, 4:8]
        third_first, third_second = third_ref[row, 0], third_ref[row, 1]
        base = third_first - returned[4:8] + third_second
        base_ref[row, 0] = base
        base_ref[row, 1] = third_second
        sums = dual_first + (2.0 * here) * before - (2.0 * here + 1.0) * base
        total = sums + dual_second - third_second
        sums_ref[row, 0] = sums
        sums_ref[row, 1] = total
        later = base - before
        keep_ref[row] = jnp.where(is_first, later, total)
        send_ref[row] = jnp.where(is_first, total, later)

    rows_loop(0, ROWS, GROUP, each)


def spread_kernel(
    base_ref,
    sums_ref,
    deviation_ref,
    carry_ref,
    received_ref,
    other_ref,
    total_ref,
    total_received_ref,
    dual_ref,
    column_ref,
    model_ref,
):
    here = place().astype(F32)
    is_first = place() % 2 == 0

    def each(row):
        own, other = carry_ref[row] + received_ref[row], other_ref[row]
        later = jnp.where(is_first, own, other)
        earlier = jnp.where(is_first, other, own)
        deviation = deviation_ref[row]
        for sub in range(SUBS):
            dual_ref[row, sub] = base_ref[row, sub] + later
            sums = earlier + sums_ref[row, sub] - (2.0 * here + (1.0 + sub)) * later
            scaled = deviation * sums
            for pair in range(2):
                for tile in range(TILES):
                    column_ref[sub * 16 + pair * 8 + tile, row] = scaled[
                        2 * pair : 2 * pair + 2, tile * LANES : (tile + 1) * LANES
                    ]
        model_ref[row] = total_ref[row] + total_received_ref[row]

    rows_loop(0, ROWS, GROUP, each)


def obs_kernel(
    obs_far, inc_far, weight_far, error_far, out_far, obs, inc, weight, error, out, done, sent
):
    def copies(group):
        rows = group_rows(group)
        return [
            pltpu.make_async_copy(far.at[rows], near.at[rows], done.at[k, group])
            for k, (far, near) in enumerate(
                ((obs_far, obs), (inc_far, inc), (weight_far, weight), (error_far, error))
            )
        ]

    def sending(group):
        rows = group_rows(group)
        return pltpu.make_async_copy(out.at[rows], out_far.at[rows], sent.at[group])

    for group in range(GROUPS):
        for copy in copies(group):
            copy.start()

    @pl.loop(0, GROUPS)
    def _(group):
        for copy in copies(group):
            copy.wait()
        for k in range(GROUP):
            row = group * GROUP + k
            scale = error[row]
            out[row] = (scale * obs[row] + weight[row] * inc[row]) / scale
        sending(group).start()

    @pl.loop(0, GROUPS)
    def _(group):
        sending(group).wait()


def sum_kernel(*refs):
    def each(row):
        total = refs[0][row]
        for ref in refs[1:-1]:
            total = total + ref[row]
        refs[-1][row] = total

    rows_loop(0, ROWS, GROUP, each)


def finish_kernel(
    column_ref,
    base_ref,
    deviation_ref,
    own_ref,
    other_ref,
    received_ref,
    out_ref,
    out_rows,
    done,
):
    is_first = place() % 2 == 0

    def each(row):
        received = received_ref[row]
        earlier = own_ref[row] + other_ref[row]
        earlier = earlier + jnp.where(is_first, jnp.zeros_like(received), received)
        deviation = deviation_ref[row]
        for sub in range(SUBS):
            filtered = jnp.concatenate(
                [
                    jnp.concatenate(
                        [column_ref[sub * 16 + pair * 8 + tile, row] for tile in range(TILES)],
                        axis=1,
                    )
                    for pair in range(2)
                ],
                axis=0,
            )
            out_rows[row, sub] = deviation * filtered + (base_ref[row, sub] + earlier)

    def copy(group):
        rows = group_rows(group)
        return pltpu.make_async_copy(out_rows.at[rows], out_ref.at[rows], done.at[group])

    rows_loop(0, ROWS, GROUP, each, lambda group: copy(group).start())

    @pl.loop(0, GROUPS)
    def _(group):
        copy(group).wait()


def body(
    dual_state,
    obs_dual,
    increment,
    wind_east,
    wind_north,
    deviation,
    merid_filter,
    obs_weight,
    obs_error,
):
    size = lax.axis_size("space")
    upward = [(i, i + 1) for i in range(size - 1)]
    downward = [(i + 1, i) for i in range(size - 1)]
    following = [(i, i + 1) for i in range(2 * CHIPS - 1)]
    swap = [(i, i ^ 1) for i in range(2 * CHIPS)]

    def by_core(first, second):
        return [(2 * a, 2 * b) for a, b in first] + [(2 * a + 1, 2 * b + 1) for a, b in second]

    rise = [(c, c + 1) for c in range(CHIPS - 1)]
    fall = [(c + 1, c) for c in range(CHIPS - 1)]
    ends = (0, CHIPS - 1)
    whole, half = field(ROWS, SUBS, FIELDS, LON), field(ROWS, FIELDS, LON)

    to_north, to_south, winds, ahead, _ = edges(increment, dual_state, wind_east, wind_north)
    low = lax.ppermute(to_north, "space", upward)
    high = lax.ppermute(to_south, "space", downward)
    ahead = lax.ppermute(ahead, "tm", following)
    extended = pltpu.VMEM((ROWS + 4, 8, LON), F32)
    whole_rows = pltpu.VMEM((ROWS, SUBS, FIELDS, LON), F32)
    own_rows, third, token = call(
        third_kernel,
        [field(ROWS, 8, LON), whole],
        [dual_state, obs_dual, obs_weight],
        flops=4 * ROWS * 8 * LON,
    )
    rim, _ = call(rim_kernel, [field(8, LON)], [low, high], after=[token])
    rim = lax.ppermute(rim, "tm", following)
    model_base, model_total, token = call(
        tangent_kernel,
        [whole, half],
        [increment, low, high, winds],
        [extended] * 4,
        flops=40 * ROWS * 8 * LON,
    )
    dual_base, dual_sums, keep, send, _ = call(
        adjoint_kernel,
        [whole, whole, half, half],
        [own_rows, third, winds, low, high, ahead, rim],
        [extended] * 5,
        after=[token],
        flops=60 * ROWS * 8 * LON,
    )

    received = lax.ppermute(send, "tm", swap)
    chip_total, token = call(sum_kernel, [half], [keep, received], flops=ROWS * 4 * LON)
    near = lax.ppermute(chip_total, "tm", by_core(fall, rise))
    wrapped = lax.ppermute(chip_total, "tm", by_core([ends[::-1]], [ends]))

    square = pltpu.VMEM((LAT, LAT), BF16)

    def square_half(begin, after):
        return call(
            functools.partial(square_kernel, begin),
            [jax.ShapeDtypeStruct((BLOCK, LAT), BF16)] * 2,
            [merid_filter],
            [square] * 2,
            after=after,
            flops=3 * LAT**3,
        )

    first_high, first_low, token = square_half(0, [token])
    near = hold(near, [token])
    on = lax.ppermute(near, "tm", by_core(fall[:2], rise[1:]))
    second_high, second_low, token = square_half(BLOCK, [near])
    model_received = lax.ppermute(model_total, "tm", swap)

    carry, _ = call(
        sum_kernel, [half], [near, wrapped, on], after=[token], flops=2 * ROWS * 4 * LON
    )
    other = lax.ppermute(carry, "tm", swap)

    precond_dual, columns, model_chip, token = call(
        spread_kernel,
        [whole, field(SPACE, ROWS, 2, LANES), half],
        [
            dual_base,
            dual_sums,
            deviation,
            carry,
            received,
            other,
            model_total,
            model_received,
        ],
        flops=10 * ROWS * 8 * LON,
    )

    columns = lax.all_to_all(columns, "space", split_axis=0, concat_axis=0, tiled=True)
    model_near = lax.ppermute(model_chip, "tm", by_core([ends], rise))

    precond_obs, token = call(
        obs_kernel,
        [whole],
        [obs_dual, increment, obs_weight, obs_error],
        [whole_rows] * 5
        + [pltpu.SemaphoreType.DMA((4, GROUPS)), pltpu.SemaphoreType.DMA((GROUPS,))],
        after=[precond_dual],
        flops=OBS_FLOPS,
        far_ins=(0, 1, 2, 3),
        far_outs=(0,),
        limit=WHOLE_VMEM,
    )

    columns, token = call(
        filter_kernel,
        [field(2 * LAT, LANES)],
        [first_high, first_low, second_high, second_low, columns.reshape(2 * LAT, LANES)],
        [square] * 2
        + [pltpu.VMEM((LAT, 2 * LANES), BF16)] * 2
        + [pltpu.VMEM((2 * LAT, LANES), F32), pltpu.SemaphoreType.DMA((2, LAT // BLOCK))]
        + [pltpu.SemaphoreType.DMA((LAT // BLOCK,))],
        after=[token, model_near],
        flops=6 * LAT * LAT * 2 * LANES,
        far_ins=(0, 1, 2, 3),
        far_outs=(0,),
        limit=63 * 1024 * 1024,
    )
    columns = lax.all_to_all(
        columns.reshape(SPACE, ROWS, 2, LANES), "space", split_axis=0, concat_axis=0, tiled=True
    )

    model_on = lax.ppermute(model_near, "tm", by_core([], rise[1:]))
    model_carry, _ = call(
        sum_kernel, [half], [model_near, model_on], after=[token], flops=SUM_FLOPS
    )
    model_other = lax.ppermute(model_carry, "tm", swap)

    precond_increment, _ = call(
        finish_kernel,
        [whole],
        [columns, model_base, deviation, model_carry, model_other, model_received],
        [whole_rows, pltpu.SemaphoreType.DMA((GROUPS,))],
        flops=4 * ROWS * 8 * LON,
        far_outs=(0,),
    )
    return (precond_dual, precond_obs, precond_increment)


def solution(mesh):
    banded = P("space", "tm", None, None)
    placed = (
        banded,
        banded,
        banded,
        P("space", "tm", None),
        P("space", "tm", None),
        P("space", None, None),
        P(),
        banded,
        banded,
    )
    return jax.shard_map(
        body,
        mesh=mesh,
        in_specs=placed,
        out_specs=(banded, banded, banded),
        check_vma=False,
    )
```

```python
import functools

import jax
import jax.numpy as jnp
from jax import lax
from jax.experimental import pallas as pl
from jax.experimental.pallas import tpu as pltpu
from jax.sharding import PartitionSpec as P

ROWS, SUBS, FIELDS, LON = 25, 2, 4, 1024
LAT = 800
SPACE = 32
CHIPS = 4
BLOCK = 400
LANES = 128
TILES = LON // LANES
VMEM_LIMIT = 16 * 1024 * 1024
WHOLE_VMEM = 61 * 1024 * 1024
OBS_FLOPS = 10**6
SUM_FLOPS = 10**11

F32 = jnp.float32
BF16 = jnp.bfloat16
TOKEN = jax.ShapeDtypeStruct((8, LANES), F32)


HBM = pl.BlockSpec(memory_space=pltpu.HBM)
VMEM = pl.BlockSpec(memory_space=pltpu.VMEM)


def call(
    kernel, outs, operands, scratch=(), after=(), flops=0, far_ins=(), far_outs=(),
    limit=VMEM_LIMIT,
):
    count, made = len(operands), len(outs)

    def run(*refs):
        begin = count + len(after)
        kernel(*refs[:count], *refs[begin : begin + made], *refs[begin + made + 1 :])

    size = sum(4 * a.size for a in operands) + sum(4 * o.size for o in outs)
    return pl.pallas_call(
        run,
        out_shape=(*outs, TOKEN),
        in_specs=[HBM if k in far_ins else VMEM for k in range(count)] + [HBM] * len(after),
        out_specs=(*(HBM if k in far_outs else VMEM for k in range(made)), HBM),
        scratch_shapes=list(scratch),
        compiler_params=pltpu.CompilerParams(vmem_limit_bytes=limit),
        cost_estimate=pl.CostEstimate(flops=flops, bytes_accessed=size, transcendentals=0),
    )(*operands, *after)


def hold(array, after=(), flops=0):
    def run(*refs):
        pass

    return pl.pallas_call(
        run,
        out_shape=field(*array.shape),
        in_specs=[pl.BlockSpec(memory_space=pl.ANY)] * (1 + len(after)),
        out_specs=pl.BlockSpec(memory_space=pl.ANY),
        input_output_aliases={0: 0},
        compiler_params=pltpu.CompilerParams(vmem_limit_bytes=1024 * 1024),
        cost_estimate=pl.CostEstimate(flops=flops, bytes_accessed=0, transcendentals=0),
    )(array, *after)


def place():
    return lax.axis_index("tm")


def rows_loop(begin, end, unroll, each, then=None):
    @pl.loop(0, (end - begin) // unroll)
    def _(group):
        for k in range(unroll):
            each(begin + group * unroll + k)
        if then is not None:
            then(group)

    for row in range(end - (end - begin) % unroll, end):
        each(row)


GROUP = 5
GROUPS = ROWS // GROUP


def group_rows(group):
    return pl.ds(group * GROUP, GROUP)


def field(*shape):
    return jax.ShapeDtypeStruct(shape, F32)


def split(x):
    high = x.astype(BF16)
    return high, (x - high.astype(F32)).astype(BF16)


def dot3(a_high, a_low, b_high, b_low, dims):
    def one(a, b):
        return lax.dot_general(a, b, (dims, ((), ())), preferred_element_type=F32)

    return one(a_high, b_high) + (one(a_high, b_low) + one(a_low, b_high))


def edge_kernel(
    inc_ref,
    dual_ref,
    east_ref,
    north_ref,
    up_ref,
    down_ref,
    wind_ref,
    ahead_ref,
    inc_rows,
    dual_rows,
    east_rows,
    north_rows,
    done,
):
    copies = [
        pltpu.make_async_copy(east_ref, east_rows, done.at[2, 0]),
        pltpu.make_async_copy(north_ref, north_rows, done.at[2, 1]),
    ]
    for k, rows in enumerate((pl.ds(0, 2), pl.ds(ROWS - 2, 2))):
        copies += [
            pltpu.make_async_copy(inc_ref.at[rows], inc_rows.at[k], done.at[k, 0]),
            pltpu.make_async_copy(dual_ref.at[rows], dual_rows.at[k], done.at[k, 1]),
        ]
    for copy in copies:
        copy.start()
    for copy in copies:
        copy.wait()

    for side, (target, begin) in enumerate(((down_ref, 0), (up_ref, ROWS - 2))):
        for k in range(2):
            for sub in range(SUBS):
                start = 8 * k + FIELDS * sub
                target[start : start + FIELDS, :] = dual_rows[side, k, sub]
                target[24 + start : 24 + start + FIELDS, :] = inc_rows[side, k, sub]
                at = 16 + 4 * k + 2 * sub
                target[at : at + 1, :] = east_rows[begin + k, sub : sub + 1]
                target[at + 1 : at + 2, :] = north_rows[begin + k, sub : sub + 1]

    def each(row):
        east, north = east_rows[row], north_rows[row]
        wind_ref[row, 0:1] = east[0:1]
        wind_ref[row, 1:2] = north[0:1]
        wind_ref[row, 2:3] = east[1:2]
        wind_ref[row, 3:4] = north[1:2]
        ahead_ref[row, 0:1] = east[1:2]
        ahead_ref[row, 1:2] = north[1:2]

    rows_loop(0, ROWS, GROUP, each)


def edges(increment, dual_state, wind_east, wind_north):
    ends = pltpu.VMEM((2, 2, SUBS, FIELDS, LON), F32)
    wind = pltpu.VMEM((ROWS, SUBS, LON), F32)
    return call(
        edge_kernel,
        [field(40, LON)] * 2 + [field(ROWS, 4, LON), field(ROWS, 2, LON)],
        [increment, dual_state, wind_east, wind_north],
        [ends, ends, wind, wind, pltpu.SemaphoreType.DMA((3, 2))],
        far_ins=(0, 1, 2, 3),
        limit=WHOLE_VMEM,
    )


def rim_kernel(low_ref, high_ref, rim_ref):
    for k in range(2):
        rim_ref[2 * k : 2 * k + 2, :] = low_ref[18 + 4 * k : 20 + 4 * k, :]
        rim_ref[4 + 2 * k : 6 + 2 * k, :] = high_ref[18 + 4 * k : 20 + 4 * k, :]


def square_kernel(begin, w_ref, high_ref, low_ref, w_high, w_low):
    high, low = split(w_ref[...])
    w_high[...] = high
    w_low[...] = low
    rows = slice(begin, begin + BLOCK)
    product = dot3(w_high[rows, :], w_low[rows, :], w_high[...], w_low[...], ((1,), (1,)))
    product_high, product_low = split(product)
    high_ref[...] = product_high
    low_ref[...] = product_low


def filter_kernel(
    first_high, first_low, second_high, second_low, x_ref, y_ref, high, low, x_rows, x_high,
    x_low, y_rows, done, sent,
):
    copies = [
        pltpu.make_async_copy(source, target.at[pl.ds(block * BLOCK, BLOCK)], done.at[k, block])
        for block, pair in enumerate(((first_high, first_low), (second_high, second_low)))
        for k, (source, target) in enumerate(zip(pair, (high, low)))
    ]
    arrival = pltpu.make_async_copy(x_ref, x_rows, done.at[2, 0])
    arrival.start()
    for copy in copies:
        copy.start()
    arrival.wait()
    for part in range(2):
        part_high, part_low = split(x_rows[pl.ds(part, LAT, stride=2), :])
        x_high[:, part * LANES : (part + 1) * LANES] = part_high
        x_low[:, part * LANES : (part + 1) * LANES] = part_low
    for copy in copies:
        copy.wait()

    def sending(block):
        rows = pl.ds(pl.multiple_of(2 * block * BLOCK, 2 * BLOCK), 2 * BLOCK)
        return pltpu.make_async_copy(y_rows.at[rows], y_ref.at[rows], sent.at[block])

    @pl.loop(0, LAT // BLOCK)
    def _(block):
        rows = pl.ds(pl.multiple_of(block * BLOCK, BLOCK), BLOCK)
        product = dot3(high[rows, :], low[rows, :], x_high[...], x_low[...], ((1,), (0,)))
        for part in range(2):
            y_rows[pl.ds(2 * block * BLOCK + part, BLOCK, stride=2), :] = product[
                :, part * LANES : (part + 1) * LANES
            ]
        sending(block).start()

    @pl.loop(0, LAT // BLOCK)
    def _(block):
        sending(block).wait()


def paired(first, second):
    lower = lax.broadcasted_iota(jnp.int32, (2 * FIELDS, LON), 0) < FIELDS
    shape = (2 * FIELDS, LON)
    return jnp.where(lower, jnp.broadcast_to(first, shape), jnp.broadcast_to(second, shape))


def tangent_row(below, here, above, east, north):
    east_size, north_size = jnp.abs(east), jnp.abs(north)
    along = jnp.where(east > 0, pltpu.roll(here, 1, 1), pltpu.roll(here, LON - 1, 1))
    across = jnp.where(north > 0, below, above)
    return (1.0 - east_size - north_size) * here + east_size * along + north_size * across


def halo_rows(target, source, low, high):
    for k in range(2):
        target[k] = low[24 + 8 * k : 32 + 8 * k, :]
        target[ROWS + 2 + k] = high[24 + 8 * k : 32 + 8 * k, :]

    def each(row):
        target[row + 2] = jnp.concatenate([source[row, 0], source[row, 1]], axis=0)

    rows_loop(0, ROWS, 5, each)


def tangent_kernel(
    inc_ref,
    low_ref,
    high_ref,
    wind_ref,
    base_ref,
    total_ref,
    rows_ref,
    step_ref,
    east_ref,
    north_ref,
):
    halo_rows(rows_ref, inc_ref, low_ref, high_ref)

    def spread(row, block):
        east_ref[row] = paired(block[0:1], block[2:3])
        north_ref[row] = paired(block[1:2], block[3:4])

    spread(1, low_ref[20:24, :])
    spread(ROWS + 2, high_ref[16:20, :])
    rows_loop(0, ROWS, 5, lambda row: spread(row + 2, wind_ref[row]))

    def first_step(row):
        step_ref[row] = tangent_row(
            rows_ref[row - 1], rows_ref[row], rows_ref[row + 1], east_ref[row], north_ref[row]
        )

    rows_loop(1, ROWS + 3, 3, first_step)

    def second_step(row):
        advanced = tangent_row(
            step_ref[row + 1], step_ref[row + 2], step_ref[row + 3],
            east_ref[row + 2], north_ref[row + 2],
        )
        first = inc_ref[row, 0]
        second = first + inc_ref[row, 1] - advanced[0:4]
        base_ref[row, 0] = first
        base_ref[row, 1] = second
        total_ref[row] = second - advanced[4:8]

    rows_loop(0, ROWS, 5, second_step)


def adjoint_parts(here, east, north):
    along, across = east * here, north * here
    zero = jnp.zeros_like(here)
    kept = (1.0 - jnp.abs(east) - jnp.abs(north)) * here
    kept = kept + pltpu.roll(jnp.where(east > 0, along, zero), LON - 1, 1)
    kept = kept + pltpu.roll(jnp.where(east > 0, zero, -along), 1, 1)
    to_south = jnp.where(north > 0, across, zero)
    to_north = jnp.where(north > 0, zero, -across)
    return kept, to_south, to_north


def third_kernel(dual_ref, obs_ref, weight_ref, rows_ref, third_ref):
    def each(row):
        first, second = dual_ref[row, 0], dual_ref[row, 1]
        rows_ref[row] = jnp.concatenate([first, second], axis=0)
        third_ref[row, 0] = first + weight_ref[row, 0] * obs_ref[row, 0]
        third_ref[row, 1] = second + weight_ref[row, 1] * obs_ref[row, 1]

    rows_loop(0, ROWS, GROUP, each)


def adjoint_kernel(
    own_ref,
    third_ref,
    wind_ref,
    low_ref,
    high_ref,
    ahead_ref,
    rim_ref,
    base_ref,
    sums_ref,
    keep_ref,
    send_ref,
    rows_ref,
    step_ref,
    back_ref,
    east_ref,
    north_ref,
):
    def spread(row, early, block):
        east_ref[row] = paired(early[0:1], block[0:1])
        north_ref[row] = paired(early[1:2], block[1:2])

    for k in range(2):
        at = 16 + 4 * k
        spread(k, rim_ref[2 * k : 2 * k + 2, :], low_ref[at : at + 2, :])
        spread(ROWS + 2 + k, rim_ref[4 + 2 * k : 6 + 2 * k, :], high_ref[at : at + 2, :])
    rows_loop(0, ROWS, 5, lambda row: spread(row + 2, ahead_ref[row], wind_ref[row]))
    rows_ref[2 : ROWS + 2] = own_ref[...]
    for k in range(2):
        rows_ref[k] = low_ref[8 * k : 8 * k + 8, :]
        rows_ref[ROWS + 2 + k] = high_ref[8 * k : 8 * k + 8, :]

    def sweep(source, target, begin, end, unroll):
        def parts(row):
            return adjoint_parts(source[row], east_ref[row], north_ref[row])

        def step(group, carry):
            pending, from_below = carry
            for k in range(unroll):
                row = begin + 1 + group * unroll + k
                kept, to_south, to_north = parts(row)
                target[row - 1] = pending + to_south
                pending, from_below = kept + from_below, to_north
            return pending, from_below

        kept, _, to_north = parts(begin)
        lax.fori_loop(0, (end - begin - 1) // unroll, step, (kept, to_north))

    sweep(rows_ref, step_ref, 0, ROWS + 4, 4)
    sweep(step_ref, back_ref, 1, ROWS + 3, 2)

    here = place().astype(F32)
    inner = jnp.minimum(here, 1.0)
    is_first = place() % 2 == 0

    def each(row):
        returned = back_ref[row + 2]
        before = inner * returned[0:4]
        dual_first, dual_second = own_ref[row, 0:4], own_ref[row, 4:8]
        third_first, third_second = third_ref[row, 0], third_ref[row, 1]
        base = third_first - returned[4:8] + third_second
        base_ref[row, 0] = base
        base_ref[row, 1] = third_second
        sums = dual_first + (2.0 * here) * before - (2.0 * here + 1.0) * base
        total = sums + dual_second - third_second
        sums_ref[row, 0] = sums
        sums_ref[row, 1] = total
        later = base - before
        keep_ref[row] = jnp.where(is_first, later, total)
        send_ref[row] = jnp.where(is_first, total, later)

    rows_loop(0, ROWS, GROUP, each)


def spread_kernel(
    base_ref,
    sums_ref,
    deviation_ref,
    carry_ref,
    received_ref,
    other_ref,
    total_ref,
    total_received_ref,
    dual_ref,
    column_ref,
    model_ref,
):
    here = place().astype(F32)
    is_first = place() % 2 == 0

    def each(row):
        own, other = carry_ref[row] + received_ref[row], other_ref[row]
        later = jnp.where(is_first, own, other)
        earlier = jnp.where(is_first, other, own)
        deviation = deviation_ref[row]
        for sub in range(SUBS):
            dual_ref[row, sub] = base_ref[row, sub] + later
            sums = earlier + sums_ref[row, sub] - (2.0 * here + (1.0 + sub)) * later
            scaled = deviation * sums
            for pair in range(2):
                for tile in range(TILES):
                    column_ref[sub * 16 + pair * 8 + tile, row] = scaled[
                        2 * pair : 2 * pair + 2, tile * LANES : (tile + 1) * LANES
                    ]
        model_ref[row] = total_ref[row] + total_received_ref[row]

    rows_loop(0, ROWS, GROUP, each)


def obs_kernel(
    obs_far, inc_far, weight_far, error_far, out_far, obs, inc, weight, error, out, done, sent
):
    def copies(group):
        rows = group_rows(group)
        return [
            pltpu.make_async_copy(far.at[rows], near.at[rows], done.at[k, group])
            for k, (far, near) in enumerate(
                ((obs_far, obs), (inc_far, inc), (weight_far, weight), (error_far, error))
            )
        ]

    def sending(group):
        rows = group_rows(group)
        return pltpu.make_async_copy(out.at[rows], out_far.at[rows], sent.at[group])

    for group in range(GROUPS):
        for copy in copies(group):
            copy.start()

    @pl.loop(0, GROUPS)
    def _(group):
        for copy in copies(group):
            copy.wait()
        for k in range(GROUP):
            row = group * GROUP + k
            scale = error[row]
            out[row] = (scale * obs[row] + weight[row] * inc[row]) / scale
        sending(group).start()

    @pl.loop(0, GROUPS)
    def _(group):
        sending(group).wait()


def sum_kernel(*refs):
    def each(row):
        total = refs[0][row]
        for ref in refs[1:-1]:
            total = total + ref[row]
        refs[-1][row] = total

    rows_loop(0, ROWS, GROUP, each)


def finish_kernel(
    column_ref,
    base_ref,
    deviation_ref,
    own_ref,
    other_ref,
    received_ref,
    out_ref,
    out_rows,
    done,
):
    is_first = place() % 2 == 0

    def each(row):
        received = received_ref[row]
        earlier = own_ref[row] + other_ref[row]
        earlier = earlier + jnp.where(is_first, jnp.zeros_like(received), received)
        deviation = deviation_ref[row]
        for sub in range(SUBS):
            filtered = jnp.concatenate(
                [
                    jnp.concatenate(
                        [column_ref[sub * 16 + pair * 8 + tile, row] for tile in range(TILES)],
                        axis=1,
                    )
                    for pair in range(2)
                ],
                axis=0,
            )
            out_rows[row, sub] = deviation * filtered + (base_ref[row, sub] + earlier)

    def copy(group):
        rows = group_rows(group)
        return pltpu.make_async_copy(out_rows.at[rows], out_ref.at[rows], done.at[group])

    rows_loop(0, ROWS, GROUP, each, lambda group: copy(group).start())

    @pl.loop(0, GROUPS)
    def _(group):
        copy(group).wait()


def body(
    dual_state,
    obs_dual,
    increment,
    wind_east,
    wind_north,
    deviation,
    merid_filter,
    obs_weight,
    obs_error,
):
    size = lax.axis_size("space")
    upward = [(i, i + 1) for i in range(size - 1)]
    downward = [(i + 1, i) for i in range(size - 1)]
    following = [(i, i + 1) for i in range(2 * CHIPS - 1)]
    swap = [(i, i ^ 1) for i in range(2 * CHIPS)]

    def by_core(first, second):
        return [(2 * a, 2 * b) for a, b in first] + [(2 * a + 1, 2 * b + 1) for a, b in second]

    rise = [(c, c + 1) for c in range(CHIPS - 1)]
    fall = [(c + 1, c) for c in range(CHIPS - 1)]
    ends = (0, CHIPS - 1)
    whole, half = field(ROWS, SUBS, FIELDS, LON), field(ROWS, FIELDS, LON)

    to_north, to_south, winds, ahead, _ = edges(increment, dual_state, wind_east, wind_north)
    low = lax.ppermute(to_north, "space", upward)
    high = lax.ppermute(to_south, "space", downward)
    ahead = lax.ppermute(ahead, "tm", following)
    extended = pltpu.VMEM((ROWS + 4, 8, LON), F32)
    whole_rows = pltpu.VMEM((ROWS, SUBS, FIELDS, LON), F32)
    own_rows, third, token = call(
        third_kernel,
        [field(ROWS, 8, LON), whole],
        [dual_state, obs_dual, obs_weight],
        flops=4 * ROWS * 8 * LON,
    )
    rim, _ = call(rim_kernel, [field(8, LON)], [low, high], after=[token])
    rim = lax.ppermute(rim, "tm", following)
    model_base, model_total, token = call(
        tangent_kernel,
        [whole, half],
        [increment, low, high, winds],
        [extended] * 4,
        flops=40 * ROWS * 8 * LON,
    )
    dual_base, dual_sums, keep, send, _ = call(
        adjoint_kernel,
        [whole, whole, half, half],
        [own_rows, third, winds, low, high, ahead, rim],
        [extended] * 5,
        after=[token],
        flops=60 * ROWS * 8 * LON,
    )

    received = lax.ppermute(send, "tm", swap)
    chip_total, token = call(sum_kernel, [half], [keep, received], flops=ROWS * 4 * LON)
    near = lax.ppermute(chip_total, "tm", by_core(fall, rise))
    wrapped = lax.ppermute(chip_total, "tm", by_core([ends[::-1]], [ends]))

    square = pltpu.VMEM((LAT, LAT), BF16)

    def square_half(begin, after):
        return call(
            functools.partial(square_kernel, begin),
            [jax.ShapeDtypeStruct((BLOCK, LAT), BF16)] * 2,
            [merid_filter],
            [square] * 2,
            after=after,
            flops=3 * LAT**3,
        )

    first_high, first_low, token = square_half(0, [token])
    near = hold(near, [token])
    on = lax.ppermute(near, "tm", by_core(fall[:2], rise[1:]))
    second_high, second_low, token = square_half(BLOCK, [near])
    model_received = lax.ppermute(model_total, "tm", swap)

    carry, _ = call(
        sum_kernel, [half], [near, wrapped, on], after=[token], flops=2 * ROWS * 4 * LON
    )
    other = lax.ppermute(carry, "tm", swap)

    precond_dual, columns, model_chip, token = call(
        spread_kernel,
        [whole, field(SPACE, ROWS, 2, LANES), half],
        [
            dual_base,
            dual_sums,
            deviation,
            carry,
            received,
            other,
            model_total,
            model_received,
        ],
        flops=10 * ROWS * 8 * LON,
    )

    columns = lax.all_to_all(columns, "space", split_axis=0, concat_axis=0, tiled=True)
    model_near = lax.ppermute(model_chip, "tm", by_core([ends], rise))

    columns, token = call(
        filter_kernel,
        [field(2 * LAT, LANES)],
        [first_high, first_low, second_high, second_low, columns.reshape(2 * LAT, LANES)],
        [square] * 2
        + [pltpu.VMEM((2 * LAT, LANES), F32)]
        + [pltpu.VMEM((LAT, 2 * LANES), BF16)] * 2
        + [pltpu.VMEM((2 * LAT, LANES), F32), pltpu.SemaphoreType.DMA((3, LAT // BLOCK))]
        + [pltpu.SemaphoreType.DMA((LAT // BLOCK,))],
        after=[model_near],
        flops=6 * LAT * LAT * 2 * LANES,
        far_ins=(0, 1, 2, 3, 4),
        far_outs=(0,),
        limit=63 * 1024 * 1024,
    )
    columns = lax.all_to_all(
        columns.reshape(SPACE, ROWS, 2, LANES), "space", split_axis=0, concat_axis=0, tiled=True
    )

    precond_obs, token = call(
        obs_kernel,
        [whole],
        [obs_dual, increment, obs_weight, obs_error],
        [whole_rows] * 5
        + [pltpu.SemaphoreType.DMA((4, GROUPS)), pltpu.SemaphoreType.DMA((GROUPS,))],
        after=[token],
        flops=OBS_FLOPS,
        far_ins=(0, 1, 2, 3),
        far_outs=(0,),
        limit=WHOLE_VMEM,
    )

    model_on = lax.ppermute(model_near, "tm", by_core([], rise[1:]))
    model_carry, _ = call(
        sum_kernel, [half], [model_near, model_on], after=[token], flops=SUM_FLOPS
    )
    model_other = lax.ppermute(model_carry, "tm", swap)

    precond_increment, _ = call(
        finish_kernel,
        [whole],
        [columns, model_base, deviation, model_carry, model_other, model_received],
        [whole_rows, pltpu.SemaphoreType.DMA((GROUPS,))],
        flops=4 * ROWS * 8 * LON,
        far_outs=(0,),
    )
    return (precond_dual, precond_obs, precond_increment)


def solution(mesh):
    banded = P("space", "tm", None, None)
    placed = (
        banded,
        banded,
        banded,
        P("space", "tm", None),
        P("space", "tm", None),
        P("space", None, None),
        P(),
        banded,
        banded,
    )
    return jax.shard_map(
        body,
        mesh=mesh,
        in_specs=placed,
        out_specs=(banded, banded, banded),
        check_vma=False,
    )
```

```python
import functools

import jax
import jax.numpy as jnp
from jax import lax
from jax.experimental import pallas as pl
from jax.experimental.pallas import tpu as pltpu
from jax.sharding import PartitionSpec as P

ROWS, SUBS, FIELDS, LON = 25, 2, 4, 1024
LAT = 800
SPACE = 32
CHIPS = 4
BLOCK = 400
LANES = 128
TILES = LON // LANES
VMEM_LIMIT = 16 * 1024 * 1024
WHOLE_VMEM = 61 * 1024 * 1024
OBS_FLOPS = 10**11
SUM_FLOPS = 10**11

F32 = jnp.float32
BF16 = jnp.bfloat16
TOKEN = jax.ShapeDtypeStruct((8, LANES), F32)


HBM = pl.BlockSpec(memory_space=pltpu.HBM)
VMEM = pl.BlockSpec(memory_space=pltpu.VMEM)


def call(
    kernel, outs, operands, scratch=(), after=(), flops=0, far_ins=(), far_outs=(),
    limit=VMEM_LIMIT,
):
    count, made = len(operands), len(outs)

    def run(*refs):
        begin = count + len(after)
        kernel(*refs[:count], *refs[begin : begin + made], *refs[begin + made + 1 :])

    size = sum(4 * a.size for a in operands) + sum(4 * o.size for o in outs)
    return pl.pallas_call(
        run,
        out_shape=(*outs, TOKEN),
        in_specs=[HBM if k in far_ins else VMEM for k in range(count)] + [HBM] * len(after),
        out_specs=(*(HBM if k in far_outs else VMEM for k in range(made)), HBM),
        scratch_shapes=list(scratch),
        compiler_params=pltpu.CompilerParams(vmem_limit_bytes=limit),
        cost_estimate=pl.CostEstimate(flops=flops, bytes_accessed=size, transcendentals=0),
    )(*operands, *after)


def hold(array, after=(), flops=0):
    def run(*refs):
        pass

    return pl.pallas_call(
        run,
        out_shape=field(*array.shape),
        in_specs=[pl.BlockSpec(memory_space=pl.ANY)] * (1 + len(after)),
        out_specs=pl.BlockSpec(memory_space=pl.ANY),
        input_output_aliases={0: 0},
        compiler_params=pltpu.CompilerParams(vmem_limit_bytes=1024 * 1024),
        cost_estimate=pl.CostEstimate(flops=flops, bytes_accessed=0, transcendentals=0),
    )(array, *after)


def place():
    return lax.axis_index("tm")


def rows_loop(begin, end, unroll, each, then=None):
    @pl.loop(0, (end - begin) // unroll)
    def _(group):
        for k in range(unroll):
            each(begin + group * unroll + k)
        if then is not None:
            then(group)

    for row in range(end - (end - begin) % unroll, end):
        each(row)


GROUP = 5
GROUPS = ROWS // GROUP


def group_rows(group):
    return pl.ds(group * GROUP, GROUP)


def field(*shape):
    return jax.ShapeDtypeStruct(shape, F32)


def split(x):
    high = x.astype(BF16)
    return high, (x - high.astype(F32)).astype(BF16)


def dot3(a_high, a_low, b_high, b_low, dims):
    def one(a, b):
        return lax.dot_general(a, b, (dims, ((), ())), preferred_element_type=F32)

    return one(a_high, b_high) + (one(a_high, b_low) + one(a_low, b_high))


def edge_kernel(
    inc_ref,
    dual_ref,
    east_ref,
    north_ref,
    up_ref,
    down_ref,
    wind_ref,
    ahead_ref,
    inc_rows,
    dual_rows,
    east_rows,
    north_rows,
    done,
):
    copies = [
        pltpu.make_async_copy(east_ref, east_rows, done.at[2, 0]),
        pltpu.make_async_copy(north_ref, north_rows, done.at[2, 1]),
    ]
    for k, rows in enumerate((pl.ds(0, 2), pl.ds(ROWS - 2, 2))):
        copies += [
            pltpu.make_async_copy(inc_ref.at[rows], inc_rows.at[k], done.at[k, 0]),
            pltpu.make_async_copy(dual_ref.at[rows], dual_rows.at[k], done.at[k, 1]),
        ]
    for copy in copies:
        copy.start()
    for copy in copies:
        copy.wait()

    for side, (target, begin) in enumerate(((down_ref, 0), (up_ref, ROWS - 2))):
        for k in range(2):
            for sub in range(SUBS):
                start = 8 * k + FIELDS * sub
                target[start : start + FIELDS, :] = dual_rows[side, k, sub]
                target[24 + start : 24 + start + FIELDS, :] = inc_rows[side, k, sub]
                at = 16 + 4 * k + 2 * sub
                target[at : at + 1, :] = east_rows[begin + k, sub : sub + 1]
                target[at + 1 : at + 2, :] = north_rows[begin + k, sub : sub + 1]

    def each(row):
        east, north = east_rows[row], north_rows[row]
        wind_ref[row, 0:1] = east[0:1]
        wind_ref[row, 1:2] = north[0:1]
        wind_ref[row, 2:3] = east[1:2]
        wind_ref[row, 3:4] = north[1:2]
        ahead_ref[row, 0:1] = east[1:2]
        ahead_ref[row, 1:2] = north[1:2]

    rows_loop(0, ROWS, GROUP, each)


def edges(increment, dual_state, wind_east, wind_north):
    ends = pltpu.VMEM((2, 2, SUBS, FIELDS, LON), F32)
    wind = pltpu.VMEM((ROWS, SUBS, LON), F32)
    return call(
        edge_kernel,
        [field(40, LON)] * 2 + [field(ROWS, 4, LON), field(ROWS, 2, LON)],
        [increment, dual_state, wind_east, wind_north],
        [ends, ends, wind, wind, pltpu.SemaphoreType.DMA((3, 2))],
        far_ins=(0, 1, 2, 3),
        limit=WHOLE_VMEM,
    )


def rim_kernel(low_ref, high_ref, rim_ref):
    for k in range(2):
        rim_ref[2 * k : 2 * k + 2, :] = low_ref[18 + 4 * k : 20 + 4 * k, :]
        rim_ref[4 + 2 * k : 6 + 2 * k, :] = high_ref[18 + 4 * k : 20 + 4 * k, :]


def square_kernel(begin, w_ref, high_ref, low_ref, w_high, w_low):
    high, low = split(w_ref[...])
    w_high[...] = high
    w_low[...] = low
    rows = slice(begin, begin + BLOCK)
    product = dot3(w_high[rows, :], w_low[rows, :], w_high[...], w_low[...], ((1,), (1,)))
    product_high, product_low = split(product)
    high_ref[...] = product_high
    low_ref[...] = product_low


def filter_kernel(
    first_high, first_low, second_high, second_low, x_ref, y_ref, high, low, x_rows, x_high,
    x_low, y_rows, done, sent,
):
    copies = [
        pltpu.make_async_copy(source, target.at[pl.ds(block * BLOCK, BLOCK)], done.at[k, block])
        for block, pair in enumerate(((first_high, first_low), (second_high, second_low)))
        for k, (source, target) in enumerate(zip(pair, (high, low)))
    ]
    arrival = pltpu.make_async_copy(x_ref, x_rows, done.at[2, 0])
    arrival.start()
    for copy in copies:
        copy.start()
    arrival.wait()
    for part in range(2):
        part_high, part_low = split(x_rows[pl.ds(part, LAT, stride=2), :])
        x_high[:, part * LANES : (part + 1) * LANES] = part_high
        x_low[:, part * LANES : (part + 1) * LANES] = part_low
    for copy in copies:
        copy.wait()

    def sending(block):
        rows = pl.ds(pl.multiple_of(2 * block * BLOCK, 2 * BLOCK), 2 * BLOCK)
        return pltpu.make_async_copy(y_rows.at[rows], y_ref.at[rows], sent.at[block])

    @pl.loop(0, LAT // BLOCK)
    def _(block):
        rows = pl.ds(pl.multiple_of(block * BLOCK, BLOCK), BLOCK)
        product = dot3(high[rows, :], low[rows, :], x_high[...], x_low[...], ((1,), (0,)))
        for part in range(2):
            y_rows[pl.ds(2 * block * BLOCK + part, BLOCK, stride=2), :] = product[
                :, part * LANES : (part + 1) * LANES
            ]
        sending(block).start()

    @pl.loop(0, LAT // BLOCK)
    def _(block):
        sending(block).wait()


def paired(first, second):
    lower = lax.broadcasted_iota(jnp.int32, (2 * FIELDS, LON), 0) < FIELDS
    shape = (2 * FIELDS, LON)
    return jnp.where(lower, jnp.broadcast_to(first, shape), jnp.broadcast_to(second, shape))


def tangent_row(below, here, above, east, north):
    east_size, north_size = jnp.abs(east), jnp.abs(north)
    along = jnp.where(east > 0, pltpu.roll(here, 1, 1), pltpu.roll(here, LON - 1, 1))
    across = jnp.where(north > 0, below, above)
    return (1.0 - east_size - north_size) * here + east_size * along + north_size * across


def halo_rows(target, source, low, high):
    for k in range(2):
        target[k] = low[24 + 8 * k : 32 + 8 * k, :]
        target[ROWS + 2 + k] = high[24 + 8 * k : 32 + 8 * k, :]

    def each(row):
        target[row + 2] = jnp.concatenate([source[row, 0], source[row, 1]], axis=0)

    rows_loop(0, ROWS, 5, each)


def tangent_kernel(
    inc_ref,
    low_ref,
    high_ref,
    wind_ref,
    base_ref,
    total_ref,
    rows_ref,
    step_ref,
    east_ref,
    north_ref,
):
    halo_rows(rows_ref, inc_ref, low_ref, high_ref)

    def spread(row, block):
        east_ref[row] = paired(block[0:1], block[2:3])
        north_ref[row] = paired(block[1:2], block[3:4])

    spread(1, low_ref[20:24, :])
    spread(ROWS + 2, high_ref[16:20, :])
    rows_loop(0, ROWS, 5, lambda row: spread(row + 2, wind_ref[row]))

    def first_step(row):
        step_ref[row] = tangent_row(
            rows_ref[row - 1], rows_ref[row], rows_ref[row + 1], east_ref[row], north_ref[row]
        )

    rows_loop(1, ROWS + 3, 3, first_step)

    def second_step(row):
        advanced = tangent_row(
            step_ref[row + 1], step_ref[row + 2], step_ref[row + 3],
            east_ref[row + 2], north_ref[row + 2],
        )
        first = inc_ref[row, 0]
        second = first + inc_ref[row, 1] - advanced[0:4]
        base_ref[row, 0] = first
        base_ref[row, 1] = second
        total_ref[row] = second - advanced[4:8]

    rows_loop(0, ROWS, 5, second_step)


def adjoint_parts(here, east, north):
    along, across = east * here, north * here
    zero = jnp.zeros_like(here)
    kept = (1.0 - jnp.abs(east) - jnp.abs(north)) * here
    kept = kept + pltpu.roll(jnp.where(east > 0, along, zero), LON - 1, 1)
    kept = kept + pltpu.roll(jnp.where(east > 0, zero, -along), 1, 1)
    to_south = jnp.where(north > 0, across, zero)
    to_north = jnp.where(north > 0, zero, -across)
    return kept, to_south, to_north


def third_kernel(dual_ref, obs_ref, weight_ref, rows_ref, third_ref):
    def each(row):
        first, second = dual_ref[row, 0], dual_ref[row, 1]
        rows_ref[row] = jnp.concatenate([first, second], axis=0)
        third_ref[row, 0] = first + weight_ref[row, 0] * obs_ref[row, 0]
        third_ref[row, 1] = second + weight_ref[row, 1] * obs_ref[row, 1]

    rows_loop(0, ROWS, GROUP, each)


def adjoint_kernel(
    own_ref,
    third_ref,
    wind_ref,
    low_ref,
    high_ref,
    ahead_ref,
    rim_ref,
    base_ref,
    sums_ref,
    keep_ref,
    send_ref,
    rows_ref,
    step_ref,
    back_ref,
    east_ref,
    north_ref,
):
    def spread(row, early, block):
        east_ref[row] = paired(early[0:1], block[0:1])
        north_ref[row] = paired(early[1:2], block[1:2])

    for k in range(2):
        at = 16 + 4 * k
        spread(k, rim_ref[2 * k : 2 * k + 2, :], low_ref[at : at + 2, :])
        spread(ROWS + 2 + k, rim_ref[4 + 2 * k : 6 + 2 * k, :], high_ref[at : at + 2, :])
    rows_loop(0, ROWS, 5, lambda row: spread(row + 2, ahead_ref[row], wind_ref[row]))
    rows_ref[2 : ROWS + 2] = own_ref[...]
    for k in range(2):
        rows_ref[k] = low_ref[8 * k : 8 * k + 8, :]
        rows_ref[ROWS + 2 + k] = high_ref[8 * k : 8 * k + 8, :]

    def sweep(source, target, begin, end, unroll):
        def parts(row):
            return adjoint_parts(source[row], east_ref[row], north_ref[row])

        def step(group, carry):
            pending, from_below = carry
            for k in range(unroll):
                row = begin + 1 + group * unroll + k
                kept, to_south, to_north = parts(row)
                target[row - 1] = pending + to_south
                pending, from_below = kept + from_below, to_north
            return pending, from_below

        kept, _, to_north = parts(begin)
        lax.fori_loop(0, (end - begin - 1) // unroll, step, (kept, to_north))

    sweep(rows_ref, step_ref, 0, ROWS + 4, 4)
    sweep(step_ref, back_ref, 1, ROWS + 3, 2)

    here = place().astype(F32)
    inner = jnp.minimum(here, 1.0)
    is_first = place() % 2 == 0

    def each(row):
        returned = back_ref[row + 2]
        before = inner * returned[0:4]
        dual_first, dual_second = own_ref[row, 0:4], own_ref[row, 4:8]
        third_first, third_second = third_ref[row, 0], third_ref[row, 1]
        base = third_first - returned[4:8] + third_second
        base_ref[row, 0] = base
        base_ref[row, 1] = third_second
        sums = dual_first + (2.0 * here) * before - (2.0 * here + 1.0) * base
        total = sums + dual_second - third_second
        sums_ref[row, 0] = sums
        sums_ref[row, 1] = total
        later = base - before
        keep_ref[row] = jnp.where(is_first, later, total)
        send_ref[row] = jnp.where(is_first, total, later)

    rows_loop(0, ROWS, GROUP, each)


def spread_kernel(
    base_ref,
    sums_ref,
    deviation_ref,
    carry_ref,
    received_ref,
    other_ref,
    dual_ref,
    column_ref,
):
    here = place().astype(F32)
    is_first = place() % 2 == 0

    def each(row):
        own, other = carry_ref[row] + received_ref[row], other_ref[row]
        later = jnp.where(is_first, own, other)
        earlier = jnp.where(is_first, other, own)
        deviation = deviation_ref[row]
        for sub in range(SUBS):
            dual_ref[row, sub] = base_ref[row, sub] + later
            sums = earlier + sums_ref[row, sub] - (2.0 * here + (1.0 + sub)) * later
            scaled = deviation * sums
            for pair in range(2):
                for tile in range(TILES):
                    column_ref[sub * 16 + pair * 8 + tile, row] = scaled[
                        2 * pair : 2 * pair + 2, tile * LANES : (tile + 1) * LANES
                    ]

    rows_loop(0, ROWS, GROUP, each)


def obs_kernel(
    obs_far, inc_far, weight_far, error_far, out_far, obs, inc, weight, error, out, done, sent
):
    def copies(group):
        rows = group_rows(group)
        return [
            pltpu.make_async_copy(far.at[rows], near.at[rows], done.at[k, group])
            for k, (far, near) in enumerate(
                ((obs_far, obs), (inc_far, inc), (weight_far, weight), (error_far, error))
            )
        ]

    def sending(group):
        rows = group_rows(group)
        return pltpu.make_async_copy(out.at[rows], out_far.at[rows], sent.at[group])

    for group in range(GROUPS):
        for copy in copies(group):
            copy.start()

    @pl.loop(0, GROUPS)
    def _(group):
        for copy in copies(group):
            copy.wait()
        for k in range(GROUP):
            row = group * GROUP + k
            scale = error[row]
            out[row] = (scale * obs[row] + weight[row] * inc[row]) / scale
        sending(group).start()

    @pl.loop(0, GROUPS)
    def _(group):
        sending(group).wait()


def sum_kernel(*refs):
    def each(row):
        total = refs[0][row]
        for ref in refs[1:-1]:
            total = total + ref[row]
        refs[-1][row] = total

    rows_loop(0, ROWS, GROUP, each)


def finish_kernel(
    column_ref,
    base_ref,
    deviation_ref,
    own_ref,
    other_ref,
    received_ref,
    out_ref,
    out_rows,
    done,
):
    is_first = place() % 2 == 0

    def each(row):
        received = received_ref[row]
        earlier = own_ref[row] + other_ref[row]
        earlier = earlier + jnp.where(is_first, jnp.zeros_like(received), received)
        deviation = deviation_ref[row]
        for sub in range(SUBS):
            filtered = jnp.concatenate(
                [
                    jnp.concatenate(
                        [column_ref[sub * 16 + pair * 8 + tile, row] for tile in range(TILES)],
                        axis=1,
                    )
                    for pair in range(2)
                ],
                axis=0,
            )
            out_rows[row, sub] = deviation * filtered + (base_ref[row, sub] + earlier)

    def copy(group):
        rows = group_rows(group)
        return pltpu.make_async_copy(out_rows.at[rows], out_ref.at[rows], done.at[group])

    rows_loop(0, ROWS, GROUP, each, lambda group: copy(group).start())

    @pl.loop(0, GROUPS)
    def _(group):
        copy(group).wait()


def body(
    dual_state,
    obs_dual,
    increment,
    wind_east,
    wind_north,
    deviation,
    merid_filter,
    obs_weight,
    obs_error,
):
    size = lax.axis_size("space")
    upward = [(i, i + 1) for i in range(size - 1)]
    downward = [(i + 1, i) for i in range(size - 1)]
    following = [(i, i + 1) for i in range(2 * CHIPS - 1)]
    swap = [(i, i ^ 1) for i in range(2 * CHIPS)]

    def by_core(first, second):
        return [(2 * a, 2 * b) for a, b in first] + [(2 * a + 1, 2 * b + 1) for a, b in second]

    rise = [(c, c + 1) for c in range(CHIPS - 1)]
    fall = [(c + 1, c) for c in range(CHIPS - 1)]
    ends = (0, CHIPS - 1)
    whole, half = field(ROWS, SUBS, FIELDS, LON), field(ROWS, FIELDS, LON)

    to_north, to_south, winds, ahead, _ = edges(increment, dual_state, wind_east, wind_north)
    low = lax.ppermute(to_north, "space", upward)
    high = lax.ppermute(to_south, "space", downward)
    ahead = lax.ppermute(ahead, "tm", following)
    extended = pltpu.VMEM((ROWS + 4, 8, LON), F32)
    whole_rows = pltpu.VMEM((ROWS, SUBS, FIELDS, LON), F32)
    own_rows, third, token = call(
        third_kernel,
        [field(ROWS, 8, LON), whole],
        [dual_state, obs_dual, obs_weight],
        flops=4 * ROWS * 8 * LON,
    )
    rim, _ = call(rim_kernel, [field(8, LON)], [low, high], after=[token])
    rim = lax.ppermute(rim, "tm", following)
    model_base, model_total, token = call(
        tangent_kernel,
        [whole, half],
        [increment, low, high, winds],
        [extended] * 4,
        flops=40 * ROWS * 8 * LON,
    )
    dual_base, dual_sums, keep, send, _ = call(
        adjoint_kernel,
        [whole, whole, half, half],
        [own_rows, third, winds, low, high, ahead, rim],
        [extended] * 5,
        after=[token],
        flops=60 * ROWS * 8 * LON,
    )

    received = lax.ppermute(send, "tm", swap)
    chip_total, token = call(sum_kernel, [half], [keep, received], flops=ROWS * 4 * LON)
    near = lax.ppermute(chip_total, "tm", by_core(fall, rise))
    wrapped = lax.ppermute(chip_total, "tm", by_core([ends[::-1]], [ends]))

    square = pltpu.VMEM((LAT, LAT), BF16)

    def square_half(begin, after):
        return call(
            functools.partial(square_kernel, begin),
            [jax.ShapeDtypeStruct((BLOCK, LAT), BF16)] * 2,
            [merid_filter],
            [square] * 2,
            after=after,
            flops=3 * LAT**3,
        )

    first_high, first_low, token = square_half(0, [token])
    near = hold(near, [token])
    on = lax.ppermute(near, "tm", by_core(fall[:2], rise[1:]))
    second_high, second_low, token = square_half(BLOCK, [near])
    model_received = lax.ppermute(model_total, "tm", swap)

    model_chip, token = call(
        sum_kernel, [half], [model_total, model_received], after=[token], flops=ROWS * 4 * LON
    )
    model_near = lax.ppermute(model_chip, "tm", by_core([ends], rise))

    carry, _ = call(
        sum_kernel, [half], [near, wrapped, on], after=[token], flops=2 * ROWS * 4 * LON
    )
    other = lax.ppermute(carry, "tm", swap)

    precond_dual, columns, spread_token = call(
        spread_kernel,
        [whole, field(SPACE, ROWS, 2, LANES)],
        [
            dual_base,
            dual_sums,
            deviation,
            carry,
            received,
            other,
        ],
        flops=10 * ROWS * 8 * LON,
    )

    columns = lax.all_to_all(columns, "space", split_axis=0, concat_axis=0, tiled=True)

    precond_obs, token = call(
        obs_kernel,
        [whole],
        [obs_dual, increment, obs_weight, obs_error],
        [whole_rows] * 5
        + [pltpu.SemaphoreType.DMA((4, GROUPS)), pltpu.SemaphoreType.DMA((GROUPS,))],
        after=[precond_dual],
        flops=OBS_FLOPS,
        far_ins=(0, 1, 2, 3),
        far_outs=(0,),
        limit=WHOLE_VMEM,
    )

    model_near = hold(model_near, [spread_token])
    model_on = lax.ppermute(model_near, "tm", by_core([], rise[1:]))
    columns, token = call(
        filter_kernel,
        [field(2 * LAT, LANES)],
        [first_high, first_low, second_high, second_low, columns.reshape(2 * LAT, LANES)],
        [square] * 2
        + [pltpu.VMEM((2 * LAT, LANES), F32)]
        + [pltpu.VMEM((LAT, 2 * LANES), BF16)] * 2
        + [pltpu.VMEM((2 * LAT, LANES), F32), pltpu.SemaphoreType.DMA((3, LAT // BLOCK))]
        + [pltpu.SemaphoreType.DMA((LAT // BLOCK,))],
        after=[token],
        flops=6 * LAT * LAT * 2 * LANES,
        far_ins=(0, 1, 2, 3, 4),
        far_outs=(0,),
        limit=63 * 1024 * 1024,
    )
    columns = lax.all_to_all(
        columns.reshape(SPACE, ROWS, 2, LANES), "space", split_axis=0, concat_axis=0, tiled=True
    )

    model_carry, _ = call(
        sum_kernel, [half], [model_near, model_on], after=[token], flops=SUM_FLOPS
    )
    model_other = lax.ppermute(model_carry, "tm", swap)

    precond_increment, _ = call(
        finish_kernel,
        [whole],
        [columns, model_base, deviation, model_carry, model_other, model_received],
        [whole_rows, pltpu.SemaphoreType.DMA((GROUPS,))],
        flops=4 * ROWS * 8 * LON,
        far_outs=(0,),
    )
    return (precond_dual, precond_obs, precond_increment)


def solution(mesh):
    banded = P("space", "tm", None, None)
    placed = (
        banded,
        banded,
        banded,
        P("space", "tm", None),
        P("space", "tm", None),
        P("space", None, None),
        P(),
        banded,
        banded,
    )
    return jax.shard_map(
        body,
        mesh=mesh,
        in_specs=placed,
        out_specs=(banded, banded, banded),
        check_vma=False,
    )
```

```python
import functools

import jax
import jax.numpy as jnp
from jax import lax
from jax.experimental import pallas as pl
from jax.experimental.pallas import tpu as pltpu
from jax.sharding import PartitionSpec as P

ROWS, SUBS, FIELDS, LON = 25, 2, 4, 1024
LAT = 800
SPACE = 32
CHIPS = 4
BLOCK = 400
LANES = 128
TILES = LON // LANES
VMEM_LIMIT = 16 * 1024 * 1024
WHOLE_VMEM = 61 * 1024 * 1024
OBS_FLOPS = 10**11
SUM_FLOPS = 10**11

F32 = jnp.float32
BF16 = jnp.bfloat16
TOKEN = jax.ShapeDtypeStruct((8, LANES), F32)


HBM = pl.BlockSpec(memory_space=pltpu.HBM)
VMEM = pl.BlockSpec(memory_space=pltpu.VMEM)


def call(
    kernel, outs, operands, scratch=(), after=(), flops=0, far_ins=(), far_outs=(),
    limit=VMEM_LIMIT,
):
    count, made = len(operands), len(outs)

    def run(*refs):
        begin = count + len(after)
        kernel(*refs[:count], *refs[begin : begin + made], *refs[begin + made + 1 :])

    size = sum(4 * a.size for a in operands) + sum(4 * o.size for o in outs)
    return pl.pallas_call(
        run,
        out_shape=(*outs, TOKEN),
        in_specs=[HBM if k in far_ins else VMEM for k in range(count)] + [HBM] * len(after),
        out_specs=(*(HBM if k in far_outs else VMEM for k in range(made)), HBM),
        scratch_shapes=list(scratch),
        compiler_params=pltpu.CompilerParams(vmem_limit_bytes=limit),
        cost_estimate=pl.CostEstimate(flops=flops, bytes_accessed=size, transcendentals=0),
    )(*operands, *after)


def hold(array, after=(), flops=0):
    def run(*refs):
        pass

    return pl.pallas_call(
        run,
        out_shape=field(*array.shape),
        in_specs=[pl.BlockSpec(memory_space=pl.ANY)] * (1 + len(after)),
        out_specs=pl.BlockSpec(memory_space=pl.ANY),
        input_output_aliases={0: 0},
        compiler_params=pltpu.CompilerParams(vmem_limit_bytes=1024 * 1024),
        cost_estimate=pl.CostEstimate(flops=flops, bytes_accessed=0, transcendentals=0),
    )(array, *after)


def place():
    return lax.axis_index("tm")


def rows_loop(begin, end, unroll, each, then=None):
    @pl.loop(0, (end - begin) // unroll)
    def _(group):
        for k in range(unroll):
            each(begin + group * unroll + k)
        if then is not None:
            then(group)

    for row in range(end - (end - begin) % unroll, end):
        each(row)


GROUP = 5
GROUPS = ROWS // GROUP


def group_rows(group):
    return pl.ds(group * GROUP, GROUP)


def field(*shape):
    return jax.ShapeDtypeStruct(shape, F32)


def split(x):
    high = x.astype(BF16)
    return high, (x - high.astype(F32)).astype(BF16)


def dot3(a_high, a_low, b_high, b_low, dims):
    def one(a, b):
        return lax.dot_general(a, b, (dims, ((), ())), preferred_element_type=F32)

    return one(a_high, b_high) + (one(a_high, b_low) + one(a_low, b_high))


def edge_kernel(
    inc_ref,
    dual_ref,
    east_ref,
    north_ref,
    up_ref,
    down_ref,
    wind_ref,
    ahead_ref,
    inc_rows,
    dual_rows,
    east_rows,
    north_rows,
    done,
):
    copies = [
        pltpu.make_async_copy(east_ref, east_rows, done.at[2, 0]),
        pltpu.make_async_copy(north_ref, north_rows, done.at[2, 1]),
    ]
    for k, rows in enumerate((pl.ds(0, 2), pl.ds(ROWS - 2, 2))):
        copies += [
            pltpu.make_async_copy(inc_ref.at[rows], inc_rows.at[k], done.at[k, 0]),
            pltpu.make_async_copy(dual_ref.at[rows], dual_rows.at[k], done.at[k, 1]),
        ]
    for copy in copies:
        copy.start()
    for copy in copies:
        copy.wait()

    for side, (target, begin) in enumerate(((down_ref, 0), (up_ref, ROWS - 2))):
        for k in range(2):
            for sub in range(SUBS):
                start = 8 * k + FIELDS * sub
                target[start : start + FIELDS, :] = dual_rows[side, k, sub]
                target[24 + start : 24 + start + FIELDS, :] = inc_rows[side, k, sub]
                at = 16 + 4 * k + 2 * sub
                target[at : at + 1, :] = east_rows[begin + k, sub : sub + 1]
                target[at + 1 : at + 2, :] = north_rows[begin + k, sub : sub + 1]

    def each(row):
        east, north = east_rows[row], north_rows[row]
        wind_ref[row, 0:1] = east[0:1]
        wind_ref[row, 1:2] = north[0:1]
        wind_ref[row, 2:3] = east[1:2]
        wind_ref[row, 3:4] = north[1:2]
        ahead_ref[row, 0:1] = east[1:2]
        ahead_ref[row, 1:2] = north[1:2]

    rows_loop(0, ROWS, GROUP, each)


def edges(increment, dual_state, wind_east, wind_north):
    ends = pltpu.VMEM((2, 2, SUBS, FIELDS, LON), F32)
    wind = pltpu.VMEM((ROWS, SUBS, LON), F32)
    return call(
        edge_kernel,
        [field(40, LON)] * 2 + [field(ROWS, 4, LON), field(ROWS, 2, LON)],
        [increment, dual_state, wind_east, wind_north],
        [ends, ends, wind, wind, pltpu.SemaphoreType.DMA((3, 2))],
        far_ins=(0, 1, 2, 3),
        limit=WHOLE_VMEM,
    )


def rim_kernel(low_ref, high_ref, rim_ref):
    for k in range(2):
        rim_ref[2 * k : 2 * k + 2, :] = low_ref[18 + 4 * k : 20 + 4 * k, :]
        rim_ref[4 + 2 * k : 6 + 2 * k, :] = high_ref[18 + 4 * k : 20 + 4 * k, :]


def square_kernel(begin, w_ref, high_ref, low_ref, w_high, w_low):
    high, low = split(w_ref[...])
    w_high[...] = high
    w_low[...] = low
    rows = slice(begin, begin + BLOCK)
    product = dot3(w_high[rows, :], w_low[rows, :], w_high[...], w_low[...], ((1,), (1,)))
    product_high, product_low = split(product)
    high_ref[...] = product_high
    low_ref[...] = product_low


def filter_kernel(
    first_high, first_low, second_high, second_low, x_ref, y_ref, high, low, x_rows, x_high,
    x_low, y_rows, done, sent,
):
    copies = [
        pltpu.make_async_copy(source, target.at[pl.ds(block * BLOCK, BLOCK)], done.at[k, block])
        for block, pair in enumerate(((first_high, first_low), (second_high, second_low)))
        for k, (source, target) in enumerate(zip(pair, (high, low)))
    ]
    arrival = pltpu.make_async_copy(x_ref, x_rows, done.at[2, 0])
    arrival.start()
    for copy in copies:
        copy.start()
    arrival.wait()
    for part in range(2):
        part_high, part_low = split(x_rows[pl.ds(part, LAT, stride=2), :])
        x_high[:, part * LANES : (part + 1) * LANES] = part_high
        x_low[:, part * LANES : (part + 1) * LANES] = part_low
    for copy in copies:
        copy.wait()

    def sending(block):
        rows = pl.ds(pl.multiple_of(2 * block * BLOCK, 2 * BLOCK), 2 * BLOCK)
        return pltpu.make_async_copy(y_rows.at[rows], y_ref.at[rows], sent.at[block])

    @pl.loop(0, LAT // BLOCK)
    def _(block):
        rows = pl.ds(pl.multiple_of(block * BLOCK, BLOCK), BLOCK)
        product = dot3(high[rows, :], low[rows, :], x_high[...], x_low[...], ((1,), (0,)))
        for part in range(2):
            y_rows[pl.ds(2 * block * BLOCK + part, BLOCK, stride=2), :] = product[
                :, part * LANES : (part + 1) * LANES
            ]
        sending(block).start()

    @pl.loop(0, LAT // BLOCK)
    def _(block):
        sending(block).wait()


def paired(first, second):
    lower = lax.broadcasted_iota(jnp.int32, (2 * FIELDS, LON), 0) < FIELDS
    shape = (2 * FIELDS, LON)
    return jnp.where(lower, jnp.broadcast_to(first, shape), jnp.broadcast_to(second, shape))


def tangent_row(below, here, above, east, north):
    east_size, north_size = jnp.abs(east), jnp.abs(north)
    along = jnp.where(east > 0, pltpu.roll(here, 1, 1), pltpu.roll(here, LON - 1, 1))
    across = jnp.where(north > 0, below, above)
    return (1.0 - east_size - north_size) * here + east_size * along + north_size * across


def halo_rows(target, source, low, high):
    for k in range(2):
        target[k] = low[24 + 8 * k : 32 + 8 * k, :]
        target[ROWS + 2 + k] = high[24 + 8 * k : 32 + 8 * k, :]

    def each(row):
        target[row + 2] = jnp.concatenate([source[row, 0], source[row, 1]], axis=0)

    rows_loop(0, ROWS, 5, each)


def tangent_kernel(
    inc_ref,
    low_ref,
    high_ref,
    wind_ref,
    base_ref,
    total_ref,
    rows_ref,
    step_ref,
    east_ref,
    north_ref,
):
    halo_rows(rows_ref, inc_ref, low_ref, high_ref)

    def spread(row, block):
        east_ref[row] = paired(block[0:1], block[2:3])
        north_ref[row] = paired(block[1:2], block[3:4])

    spread(1, low_ref[20:24, :])
    spread(ROWS + 2, high_ref[16:20, :])
    rows_loop(0, ROWS, 5, lambda row: spread(row + 2, wind_ref[row]))

    def first_step(row):
        step_ref[row] = tangent_row(
            rows_ref[row - 1], rows_ref[row], rows_ref[row + 1], east_ref[row], north_ref[row]
        )

    rows_loop(1, ROWS + 3, 3, first_step)

    def second_step(row):
        advanced = tangent_row(
            step_ref[row + 1], step_ref[row + 2], step_ref[row + 3],
            east_ref[row + 2], north_ref[row + 2],
        )
        first = inc_ref[row, 0]
        second = first + inc_ref[row, 1] - advanced[0:4]
        base_ref[row, 0] = first
        base_ref[row, 1] = second
        total_ref[row] = second - advanced[4:8]

    rows_loop(0, ROWS, 5, second_step)


def adjoint_parts(here, east, north):
    along, across = east * here, north * here
    zero = jnp.zeros_like(here)
    kept = (1.0 - jnp.abs(east) - jnp.abs(north)) * here
    kept = kept + pltpu.roll(jnp.where(east > 0, along, zero), LON - 1, 1)
    kept = kept + pltpu.roll(jnp.where(east > 0, zero, -along), 1, 1)
    to_south = jnp.where(north > 0, across, zero)
    to_north = jnp.where(north > 0, zero, -across)
    return kept, to_south, to_north


def third_kernel(dual_ref, obs_ref, weight_ref, rows_ref, third_ref):
    def each(row):
        first, second = dual_ref[row, 0], dual_ref[row, 1]
        rows_ref[row] = jnp.concatenate([first, second], axis=0)
        third_ref[row, 0] = first + weight_ref[row, 0] * obs_ref[row, 0]
        third_ref[row, 1] = second + weight_ref[row, 1] * obs_ref[row, 1]

    rows_loop(0, ROWS, GROUP, each)


def adjoint_kernel(
    own_ref,
    third_ref,
    wind_ref,
    low_ref,
    high_ref,
    ahead_ref,
    rim_ref,
    base_ref,
    sums_ref,
    keep_ref,
    send_ref,
    rows_ref,
    step_ref,
    back_ref,
    east_ref,
    north_ref,
):
    def spread(row, early, block):
        east_ref[row] = paired(early[0:1], block[0:1])
        north_ref[row] = paired(early[1:2], block[1:2])

    for k in range(2):
        at = 16 + 4 * k
        spread(k, rim_ref[2 * k : 2 * k + 2, :], low_ref[at : at + 2, :])
        spread(ROWS + 2 + k, rim_ref[4 + 2 * k : 6 + 2 * k, :], high_ref[at : at + 2, :])
    rows_loop(0, ROWS, 5, lambda row: spread(row + 2, ahead_ref[row], wind_ref[row]))
    rows_ref[2 : ROWS + 2] = own_ref[...]
    for k in range(2):
        rows_ref[k] = low_ref[8 * k : 8 * k + 8, :]
        rows_ref[ROWS + 2 + k] = high_ref[8 * k : 8 * k + 8, :]

    def sweep(source, target, begin, end, unroll):
        def parts(row):
            return adjoint_parts(source[row], east_ref[row], north_ref[row])

        def step(group, carry):
            pending, from_below = carry
            for k in range(unroll):
                row = begin + 1 + group * unroll + k
                kept, to_south, to_north = parts(row)
                target[row - 1] = pending + to_south
                pending, from_below = kept + from_below, to_north
            return pending, from_below

        kept, _, to_north = parts(begin)
        lax.fori_loop(0, (end - begin - 1) // unroll, step, (kept, to_north))

    sweep(rows_ref, step_ref, 0, ROWS + 4, 4)
    sweep(step_ref, back_ref, 1, ROWS + 3, 2)

    here = place().astype(F32)
    inner = jnp.minimum(here, 1.0)
    is_first = place() % 2 == 0

    def each(row):
        returned = back_ref[row + 2]
        before = inner * returned[0:4]
        dual_first, dual_second = own_ref[row, 0:4], own_ref[row, 4:8]
        third_first, third_second = third_ref[row, 0], third_ref[row, 1]
        base = third_first - returned[4:8] + third_second
        base_ref[row, 0] = base
        base_ref[row, 1] = third_second
        sums = dual_first + (2.0 * here) * before - (2.0 * here + 1.0) * base
        total = sums + dual_second - third_second
        sums_ref[row, 0] = sums
        sums_ref[row, 1] = total
        later = base - before
        keep_ref[row] = jnp.where(is_first, later, total)
        send_ref[row] = jnp.where(is_first, total, later)

    rows_loop(0, ROWS, GROUP, each)


def spread_kernel(
    base_ref,
    sums_ref,
    deviation_ref,
    carry_ref,
    received_ref,
    other_ref,
    total_ref,
    total_received_ref,
    dual_ref,
    column_ref,
    model_ref,
):
    here = place().astype(F32)
    is_first = place() % 2 == 0

    def each(row):
        own, other = carry_ref[row] + received_ref[row], other_ref[row]
        later = jnp.where(is_first, own, other)
        earlier = jnp.where(is_first, other, own)
        deviation = deviation_ref[row]
        for sub in range(SUBS):
            dual_ref[row, sub] = base_ref[row, sub] + later
            sums = earlier + sums_ref[row, sub] - (2.0 * here + (1.0 + sub)) * later
            scaled = deviation * sums
            for pair in range(2):
                for tile in range(TILES):
                    column_ref[sub * 16 + pair * 8 + tile, row] = scaled[
                        2 * pair : 2 * pair + 2, tile * LANES : (tile + 1) * LANES
                    ]
        model_ref[row] = total_ref[row] + total_received_ref[row]

    rows_loop(0, ROWS, GROUP, each)


def obs_kernel(
    obs_far, inc_far, weight_far, error_far, out_far, obs, inc, weight, error, out, done, sent
):
    def copies(group):
        rows = group_rows(group)
        return [
            pltpu.make_async_copy(far.at[rows], near.at[rows], done.at[k, group])
            for k, (far, near) in enumerate(
                ((obs_far, obs), (inc_far, inc), (weight_far, weight), (error_far, error))
            )
        ]

    def sending(group):
        rows = group_rows(group)
        return pltpu.make_async_copy(out.at[rows], out_far.at[rows], sent.at[group])

    for group in range(GROUPS):
        for copy in copies(group):
            copy.start()

    @pl.loop(0, GROUPS)
    def _(group):
        for copy in copies(group):
            copy.wait()
        for k in range(GROUP):
            row = group * GROUP + k
            scale = error[row]
            out[row] = (scale * obs[row] + weight[row] * inc[row]) / scale
        sending(group).start()

    @pl.loop(0, GROUPS)
    def _(group):
        sending(group).wait()


def sum_kernel(*refs):
    def each(row):
        total = refs[0][row]
        for ref in refs[1:-1]:
            total = total + ref[row]
        refs[-1][row] = total

    rows_loop(0, ROWS, GROUP, each)


def finish_kernel(
    column_ref,
    base_ref,
    deviation_ref,
    own_ref,
    other_ref,
    received_ref,
    out_ref,
    out_rows,
    done,
):
    is_first = place() % 2 == 0

    def each(row):
        received = received_ref[row]
        earlier = own_ref[row] + other_ref[row]
        earlier = earlier + jnp.where(is_first, jnp.zeros_like(received), received)
        deviation = deviation_ref[row]
        for sub in range(SUBS):
            filtered = jnp.concatenate(
                [
                    jnp.concatenate(
                        [column_ref[sub * 16 + pair * 8 + tile, row] for tile in range(TILES)],
                        axis=1,
                    )
                    for pair in range(2)
                ],
                axis=0,
            )
            out_rows[row, sub] = deviation * filtered + (base_ref[row, sub] + earlier)

    def copy(group):
        rows = group_rows(group)
        return pltpu.make_async_copy(out_rows.at[rows], out_ref.at[rows], done.at[group])

    rows_loop(0, ROWS, GROUP, each, lambda group: copy(group).start())

    @pl.loop(0, GROUPS)
    def _(group):
        copy(group).wait()


def body(
    dual_state,
    obs_dual,
    increment,
    wind_east,
    wind_north,
    deviation,
    merid_filter,
    obs_weight,
    obs_error,
):
    size = lax.axis_size("space")
    upward = [(i, i + 1) for i in range(size - 1)]
    downward = [(i + 1, i) for i in range(size - 1)]
    following = [(i, i + 1) for i in range(2 * CHIPS - 1)]
    swap = [(i, i ^ 1) for i in range(2 * CHIPS)]

    def by_core(first, second):
        return [(2 * a, 2 * b) for a, b in first] + [(2 * a + 1, 2 * b + 1) for a, b in second]

    rise = [(c, c + 1) for c in range(CHIPS - 1)]
    fall = [(c + 1, c) for c in range(CHIPS - 1)]
    ends = (0, CHIPS - 1)
    whole, half = field(ROWS, SUBS, FIELDS, LON), field(ROWS, FIELDS, LON)

    to_north, to_south, winds, ahead, _ = edges(increment, dual_state, wind_east, wind_north)
    low = lax.ppermute(to_north, "space", upward)
    high = lax.ppermute(to_south, "space", downward)
    ahead = lax.ppermute(ahead, "tm", following)
    extended = pltpu.VMEM((ROWS + 4, 8, LON), F32)
    whole_rows = pltpu.VMEM((ROWS, SUBS, FIELDS, LON), F32)
    own_rows, third, token = call(
        third_kernel,
        [field(ROWS, 8, LON), whole],
        [dual_state, obs_dual, obs_weight],
        flops=4 * ROWS * 8 * LON,
    )
    rim, _ = call(rim_kernel, [field(8, LON)], [low, high], after=[token])
    rim = lax.ppermute(rim, "tm", following)
    dual_base, dual_sums, keep, send, _ = call(
        adjoint_kernel,
        [whole, whole, half, half],
        [own_rows, third, winds, low, high, ahead, rim],
        [extended] * 5,
        flops=60 * ROWS * 8 * LON,
    )

    received = lax.ppermute(send, "tm", swap)
    chip_total, token = call(sum_kernel, [half], [keep, received], flops=ROWS * 4 * LON)
    near = lax.ppermute(chip_total, "tm", by_core(fall, rise))
    wrapped = lax.ppermute(chip_total, "tm", by_core([ends[::-1]], [ends]))

    square = pltpu.VMEM((LAT, LAT), BF16)

    def square_half(begin, after):
        return call(
            functools.partial(square_kernel, begin),
            [jax.ShapeDtypeStruct((BLOCK, LAT), BF16)] * 2,
            [merid_filter],
            [square] * 2,
            after=after,
            flops=3 * LAT**3,
        )

    first_high, first_low, token = square_half(0, [token])
    model_base, model_total, token = call(
        tangent_kernel,
        [whole, half],
        [increment, low, high, winds],
        [extended] * 4,
        after=[token],
        flops=40 * ROWS * 8 * LON,
    )
    near = hold(near, [token])
    on = lax.ppermute(near, "tm", by_core(fall[:2], rise[1:]))
    second_high, second_low, token = square_half(BLOCK, [near])
    model_received = lax.ppermute(model_total, "tm", swap)

    carry, _ = call(
        sum_kernel, [half], [near, wrapped, on], after=[token], flops=2 * ROWS * 4 * LON
    )
    other = lax.ppermute(carry, "tm", swap)

    precond_dual, columns, model_chip, token = call(
        spread_kernel,
        [whole, field(SPACE, ROWS, 2, LANES), half],
        [
            dual_base,
            dual_sums,
            deviation,
            carry,
            received,
            other,
            model_total,
            model_received,
        ],
        flops=10 * ROWS * 8 * LON,
    )

    columns = lax.all_to_all(columns, "space", split_axis=0, concat_axis=0, tiled=True)
    model_near = lax.ppermute(model_chip, "tm", by_core([ends], rise))

    precond_obs, token = call(
        obs_kernel,
        [whole],
        [obs_dual, increment, obs_weight, obs_error],
        [whole_rows] * 5
        + [pltpu.SemaphoreType.DMA((4, GROUPS)), pltpu.SemaphoreType.DMA((GROUPS,))],
        after=[precond_dual],
        flops=OBS_FLOPS,
        far_ins=(0, 1, 2, 3),
        far_outs=(0,),
        limit=WHOLE_VMEM,
    )

    columns, token = call(
        filter_kernel,
        [field(2 * LAT, LANES)],
        [first_high, first_low, second_high, second_low, columns.reshape(2 * LAT, LANES)],
        [square] * 2
        + [pltpu.VMEM((2 * LAT, LANES), F32)]
        + [pltpu.VMEM((LAT, 2 * LANES), BF16)] * 2
        + [pltpu.VMEM((2 * LAT, LANES), F32), pltpu.SemaphoreType.DMA((3, LAT // BLOCK))]
        + [pltpu.SemaphoreType.DMA((LAT // BLOCK,))],
        after=[token, model_near],
        flops=6 * LAT * LAT * 2 * LANES,
        far_ins=(0, 1, 2, 3, 4),
        far_outs=(0,),
        limit=63 * 1024 * 1024,
    )
    columns = lax.all_to_all(
        columns.reshape(SPACE, ROWS, 2, LANES), "space", split_axis=0, concat_axis=0, tiled=True
    )

    model_on = lax.ppermute(model_near, "tm", by_core([], rise[1:]))
    model_carry, _ = call(
        sum_kernel, [half], [model_near, model_on], after=[token], flops=SUM_FLOPS
    )
    model_other = lax.ppermute(model_carry, "tm", swap)

    precond_increment, _ = call(
        finish_kernel,
        [whole],
        [columns, model_base, deviation, model_carry, model_other, model_received],
        [whole_rows, pltpu.SemaphoreType.DMA((GROUPS,))],
        flops=4 * ROWS * 8 * LON,
        far_outs=(0,),
    )
    return (precond_dual, precond_obs, precond_increment)


def solution(mesh):
    banded = P("space", "tm", None, None)
    placed = (
        banded,
        banded,
        banded,
        P("space", "tm", None),
        P("space", "tm", None),
        P("space", None, None),
        P(),
        banded,
        banded,
    )
    return jax.shard_map(
        body,
        mesh=mesh,
        in_specs=placed,
        out_specs=(banded, banded, banded),
        check_vma=False,
    )
```

```python
import functools

import jax
import jax.numpy as jnp
from jax import lax
from jax.experimental import pallas as pl
from jax.experimental.pallas import tpu as pltpu
from jax.sharding import PartitionSpec as P

ROWS, SUBS, FIELDS, LON = 25, 2, 4, 1024
LAT = 800
SPACE = 32
CHIPS = 4
BLOCK = 400
LANES = 128
TILES = LON // LANES
VMEM_LIMIT = 16 * 1024 * 1024
WHOLE_VMEM = 61 * 1024 * 1024
OBS_FLOPS = 10**11
SUM_FLOPS = 10**11

F32 = jnp.float32
BF16 = jnp.bfloat16
TOKEN = jax.ShapeDtypeStruct((8, LANES), F32)


HBM = pl.BlockSpec(memory_space=pltpu.HBM)
VMEM = pl.BlockSpec(memory_space=pltpu.VMEM)


def call(
    kernel, outs, operands, scratch=(), after=(), flops=0, far_ins=(), far_outs=(),
    limit=VMEM_LIMIT, size=None,
):
    count, made = len(operands), len(outs)

    def run(*refs):
        begin = count + len(after)
        kernel(*refs[:count], *refs[begin : begin + made], *refs[begin + made + 1 :])

    if size is None:
        size = sum(4 * a.size for a in operands) + sum(4 * o.size for o in outs)
    return pl.pallas_call(
        run,
        out_shape=(*outs, TOKEN),
        in_specs=[HBM if k in far_ins else VMEM for k in range(count)] + [HBM] * len(after),
        out_specs=(*(HBM if k in far_outs else VMEM for k in range(made)), HBM),
        scratch_shapes=list(scratch),
        compiler_params=pltpu.CompilerParams(vmem_limit_bytes=limit),
        cost_estimate=pl.CostEstimate(flops=flops, bytes_accessed=size, transcendentals=0),
    )(*operands, *after)


def hold(array, after=(), flops=0):
    def run(*refs):
        pass

    return pl.pallas_call(
        run,
        out_shape=field(*array.shape),
        in_specs=[pl.BlockSpec(memory_space=pl.ANY)] * (1 + len(after)),
        out_specs=pl.BlockSpec(memory_space=pl.ANY),
        input_output_aliases={0: 0},
        compiler_params=pltpu.CompilerParams(vmem_limit_bytes=1024 * 1024),
        cost_estimate=pl.CostEstimate(flops=flops, bytes_accessed=0, transcendentals=0),
    )(array, *after)


def place():
    return lax.axis_index("tm")


def rows_loop(begin, end, unroll, each, then=None):
    @pl.loop(0, (end - begin) // unroll)
    def _(group):
        for k in range(unroll):
            each(begin + group * unroll + k)
        if then is not None:
            then(group)

    for row in range(end - (end - begin) % unroll, end):
        each(row)


GROUP = 5
CUT = 13
GROUPS = ROWS // GROUP


def group_rows(group):
    return pl.ds(group * GROUP, GROUP)


def field(*shape):
    return jax.ShapeDtypeStruct(shape, F32)


def split(x):
    high = x.astype(BF16)
    return high, (x - high.astype(F32)).astype(BF16)


def dot3(a_high, a_low, b_high, b_low, dims):
    def one(a, b):
        return lax.dot_general(a, b, (dims, ((), ())), preferred_element_type=F32)

    return one(a_high, b_high) + (one(a_high, b_low) + one(a_low, b_high))


def edge_kernel(
    inc_ref,
    dual_ref,
    east_ref,
    north_ref,
    up_ref,
    down_ref,
    wind_ref,
    ahead_ref,
    inc_rows,
    dual_rows,
    east_rows,
    north_rows,
    done,
):
    copies = [
        pltpu.make_async_copy(east_ref, east_rows, done.at[2, 0]),
        pltpu.make_async_copy(north_ref, north_rows, done.at[2, 1]),
    ]
    for k, rows in enumerate((pl.ds(0, 2), pl.ds(ROWS - 2, 2))):
        copies += [
            pltpu.make_async_copy(inc_ref.at[rows], inc_rows.at[k], done.at[k, 0]),
            pltpu.make_async_copy(dual_ref.at[rows], dual_rows.at[k], done.at[k, 1]),
        ]
    for copy in copies:
        copy.start()
    for copy in copies:
        copy.wait()

    for side, (target, begin) in enumerate(((down_ref, 0), (up_ref, ROWS - 2))):
        for k in range(2):
            for sub in range(SUBS):
                start = 8 * k + FIELDS * sub
                target[start : start + FIELDS, :] = dual_rows[side, k, sub]
                target[24 + start : 24 + start + FIELDS, :] = inc_rows[side, k, sub]
                at = 16 + 4 * k + 2 * sub
                target[at : at + 1, :] = east_rows[begin + k, sub : sub + 1]
                target[at + 1 : at + 2, :] = north_rows[begin + k, sub : sub + 1]

    def each(row):
        east, north = east_rows[row], north_rows[row]
        wind_ref[row, 0:1] = east[0:1]
        wind_ref[row, 1:2] = north[0:1]
        wind_ref[row, 2:3] = east[1:2]
        wind_ref[row, 3:4] = north[1:2]
        ahead_ref[row, 0:1] = east[1:2]
        ahead_ref[row, 1:2] = north[1:2]

    rows_loop(0, ROWS, GROUP, each)


def edges(increment, dual_state, wind_east, wind_north):
    ends = pltpu.VMEM((2, 2, SUBS, FIELDS, LON), F32)
    wind = pltpu.VMEM((ROWS, SUBS, LON), F32)
    return call(
        edge_kernel,
        [field(40, LON)] * 2 + [field(ROWS, 4, LON), field(ROWS, 2, LON)],
        [increment, dual_state, wind_east, wind_north],
        [ends, ends, wind, wind, pltpu.SemaphoreType.DMA((3, 2))],
        far_ins=(0, 1, 2, 3),
        limit=WHOLE_VMEM,
    )


def rim_kernel(low_ref, high_ref, rim_ref):
    for k in range(2):
        rim_ref[2 * k : 2 * k + 2, :] = low_ref[18 + 4 * k : 20 + 4 * k, :]
        rim_ref[4 + 2 * k : 6 + 2 * k, :] = high_ref[18 + 4 * k : 20 + 4 * k, :]


def square_kernel(begin, w_ref, high_ref, low_ref, w_high, w_low):
    high, low = split(w_ref[...])
    w_high[...] = high
    w_low[...] = low
    rows = slice(begin, begin + BLOCK)
    product = dot3(w_high[rows, :], w_low[rows, :], w_high[...], w_low[...], ((1,), (1,)))
    product_high, product_low = split(product)
    high_ref[...] = product_high
    low_ref[...] = product_low


def filter_kernel(
    first_high, first_low, second_high, second_low, x_ref, y_ref, high, low, x_rows, x_high,
    x_low, y_rows, done, sent,
):
    copies = [
        pltpu.make_async_copy(source, target.at[pl.ds(block * BLOCK, BLOCK)], done.at[k, block])
        for block, pair in enumerate(((first_high, first_low), (second_high, second_low)))
        for k, (source, target) in enumerate(zip(pair, (high, low)))
    ]
    arrival = pltpu.make_async_copy(x_ref, x_rows, done.at[2, 0])
    arrival.start()
    for copy in copies:
        copy.start()
    arrival.wait()
    for part in range(2):
        part_high, part_low = split(x_rows[pl.ds(part, LAT, stride=2), :])
        x_high[:, part * LANES : (part + 1) * LANES] = part_high
        x_low[:, part * LANES : (part + 1) * LANES] = part_low
    for copy in copies:
        copy.wait()

    def sending(block):
        rows = pl.ds(pl.multiple_of(2 * block * BLOCK, 2 * BLOCK), 2 * BLOCK)
        return pltpu.make_async_copy(y_rows.at[rows], y_ref.at[rows], sent.at[block])

    @pl.loop(0, LAT // BLOCK)
    def _(block):
        rows = pl.ds(pl.multiple_of(block * BLOCK, BLOCK), BLOCK)
        product = dot3(high[rows, :], low[rows, :], x_high[...], x_low[...], ((1,), (0,)))
        for part in range(2):
            y_rows[pl.ds(2 * block * BLOCK + part, BLOCK, stride=2), :] = product[
                :, part * LANES : (part + 1) * LANES
            ]
        sending(block).start()

    @pl.loop(0, LAT // BLOCK)
    def _(block):
        sending(block).wait()


def paired(first, second):
    lower = lax.broadcasted_iota(jnp.int32, (2 * FIELDS, LON), 0) < FIELDS
    shape = (2 * FIELDS, LON)
    return jnp.where(lower, jnp.broadcast_to(first, shape), jnp.broadcast_to(second, shape))


def tangent_row(below, here, above, east, north):
    east_size, north_size = jnp.abs(east), jnp.abs(north)
    along = jnp.where(east > 0, pltpu.roll(here, 1, 1), pltpu.roll(here, LON - 1, 1))
    across = jnp.where(north > 0, below, above)
    return (1.0 - east_size - north_size) * here + east_size * along + north_size * across


def halo_rows(target, source, low, high):
    for k in range(2):
        target[k] = low[24 + 8 * k : 32 + 8 * k, :]
        target[ROWS + 2 + k] = high[24 + 8 * k : 32 + 8 * k, :]

    def each(row):
        target[row + 2] = jnp.concatenate([source[row, 0], source[row, 1]], axis=0)

    rows_loop(0, ROWS, 5, each)


def tangent_kernel(
    inc_ref,
    low_ref,
    high_ref,
    wind_ref,
    base_ref,
    total_ref,
    rows_ref,
    step_ref,
    east_ref,
    north_ref,
):
    halo_rows(rows_ref, inc_ref, low_ref, high_ref)

    def spread(row, block):
        east_ref[row] = paired(block[0:1], block[2:3])
        north_ref[row] = paired(block[1:2], block[3:4])

    spread(1, low_ref[20:24, :])
    spread(ROWS + 2, high_ref[16:20, :])
    rows_loop(0, ROWS, 5, lambda row: spread(row + 2, wind_ref[row]))

    def first_step(row):
        step_ref[row] = tangent_row(
            rows_ref[row - 1], rows_ref[row], rows_ref[row + 1], east_ref[row], north_ref[row]
        )

    rows_loop(1, ROWS + 3, 3, first_step)

    def second_step(row):
        advanced = tangent_row(
            step_ref[row + 1], step_ref[row + 2], step_ref[row + 3],
            east_ref[row + 2], north_ref[row + 2],
        )
        first = inc_ref[row, 0]
        second = first + inc_ref[row, 1] - advanced[0:4]
        base_ref[row, 0] = first
        base_ref[row, 1] = second
        total_ref[row] = second - advanced[4:8]

    rows_loop(0, ROWS, 5, second_step)


def adjoint_parts(here, east, north):
    along, across = east * here, north * here
    zero = jnp.zeros_like(here)
    kept = (1.0 - jnp.abs(east) - jnp.abs(north)) * here
    kept = kept + pltpu.roll(jnp.where(east > 0, along, zero), LON - 1, 1)
    kept = kept + pltpu.roll(jnp.where(east > 0, zero, -along), 1, 1)
    to_south = jnp.where(north > 0, across, zero)
    to_north = jnp.where(north > 0, zero, -across)
    return kept, to_south, to_north


def third_kernel(dual_ref, obs_ref, weight_ref, rows_ref, third_ref):
    def each(row):
        first, second = dual_ref[row, 0], dual_ref[row, 1]
        rows_ref[row] = jnp.concatenate([first, second], axis=0)
        third_ref[row, 0] = first + weight_ref[row, 0] * obs_ref[row, 0]
        third_ref[row, 1] = second + weight_ref[row, 1] * obs_ref[row, 1]

    rows_loop(0, ROWS, GROUP, each)


def adjoint_kernel(
    own_ref,
    third_ref,
    wind_ref,
    low_ref,
    high_ref,
    ahead_ref,
    rim_ref,
    base_ref,
    sums_ref,
    keep_ref,
    send_ref,
    rows_ref,
    step_ref,
    back_ref,
    east_ref,
    north_ref,
):
    def spread(row, early, block):
        east_ref[row] = paired(early[0:1], block[0:1])
        north_ref[row] = paired(early[1:2], block[1:2])

    for k in range(2):
        at = 16 + 4 * k
        spread(k, rim_ref[2 * k : 2 * k + 2, :], low_ref[at : at + 2, :])
        spread(ROWS + 2 + k, rim_ref[4 + 2 * k : 6 + 2 * k, :], high_ref[at : at + 2, :])
    rows_loop(0, ROWS, 5, lambda row: spread(row + 2, ahead_ref[row], wind_ref[row]))
    rows_ref[2 : ROWS + 2] = own_ref[...]
    for k in range(2):
        rows_ref[k] = low_ref[8 * k : 8 * k + 8, :]
        rows_ref[ROWS + 2 + k] = high_ref[8 * k : 8 * k + 8, :]

    def sweep(source, target, begin, end, unroll):
        def parts(row):
            return adjoint_parts(source[row], east_ref[row], north_ref[row])

        def step(group, carry):
            pending, from_below = carry
            for k in range(unroll):
                row = begin + 1 + group * unroll + k
                kept, to_south, to_north = parts(row)
                target[row - 1] = pending + to_south
                pending, from_below = kept + from_below, to_north
            return pending, from_below

        kept, _, to_north = parts(begin)
        lax.fori_loop(0, (end - begin - 1) // unroll, step, (kept, to_north))

    sweep(rows_ref, step_ref, 0, ROWS + 4, 4)
    sweep(step_ref, back_ref, 1, ROWS + 3, 2)

    here = place().astype(F32)
    inner = jnp.minimum(here, 1.0)
    is_first = place() % 2 == 0

    def each(row):
        returned = back_ref[row + 2]
        before = inner * returned[0:4]
        dual_first, dual_second = own_ref[row, 0:4], own_ref[row, 4:8]
        third_first, third_second = third_ref[row, 0], third_ref[row, 1]
        base = third_first - returned[4:8] + third_second
        base_ref[row, 0] = base
        base_ref[row, 1] = third_second
        sums = dual_first + (2.0 * here) * before - (2.0 * here + 1.0) * base
        total = sums + dual_second - third_second
        sums_ref[row, 0] = sums
        sums_ref[row, 1] = total
        later = base - before
        keep_ref[row] = jnp.where(is_first, later, total)
        send_ref[row] = jnp.where(is_first, total, later)

    rows_loop(0, ROWS, GROUP, each)


def spread_kernel(
    base_ref,
    sums_ref,
    deviation_ref,
    carry_ref,
    received_ref,
    other_ref,
    total_ref,
    total_received_ref,
    dual_ref,
    column_ref,
    model_ref,
):
    here = place().astype(F32)
    is_first = place() % 2 == 0

    def each(row):
        own, other = carry_ref[row] + received_ref[row], other_ref[row]
        later = jnp.where(is_first, own, other)
        earlier = jnp.where(is_first, other, own)
        deviation = deviation_ref[row]
        for sub in range(SUBS):
            dual_ref[row, sub] = base_ref[row, sub] + later
            sums = earlier + sums_ref[row, sub] - (2.0 * here + (1.0 + sub)) * later
            scaled = deviation * sums
            for pair in range(2):
                for tile in range(TILES):
                    column_ref[sub * 16 + pair * 8 + tile, row] = scaled[
                        2 * pair : 2 * pair + 2, tile * LANES : (tile + 1) * LANES
                    ]
        model_ref[row] = total_ref[row] + total_received_ref[row]

    rows_loop(0, ROWS, GROUP, each)


def obs_kernel(
    obs_far, inc_far, weight_far, error_far, out_far, obs, inc, weight, error, out, done, sent
):
    def copies(group):
        rows = group_rows(group)
        return [
            pltpu.make_async_copy(far.at[rows], near.at[rows], done.at[k, group])
            for k, (far, near) in enumerate(
                ((obs_far, obs), (inc_far, inc), (weight_far, weight), (error_far, error))
            )
        ]

    def sending(group):
        rows = group_rows(group)
        return pltpu.make_async_copy(out.at[rows], out_far.at[rows], sent.at[group])

    for group in range(GROUPS):
        for copy in copies(group):
            copy.start()

    @pl.loop(0, GROUPS)
    def _(group):
        for copy in copies(group):
            copy.wait()
        for k in range(GROUP):
            row = group * GROUP + k
            scale = error[row]
            out[row] = (scale * obs[row] + weight[row] * inc[row]) / scale
        sending(group).start()

    @pl.loop(0, GROUPS)
    def _(group):
        sending(group).wait()


def total_kernel(keep_ref, received_ref, first_ref, second_ref):
    def first(row):
        first_ref[row] = keep_ref[row] + received_ref[row]

    def second(row):
        second_ref[row] = keep_ref[row + CUT] + received_ref[row + CUT]

    rows_loop(0, CUT, 4, first)
    rows_loop(0, ROWS - CUT, 4, second)


def carry_kernel(
    near_first, near_second, wrap_first, wrap_second, on_first, on_second, carry_ref
):
    def first(row):
        carry_ref[row] = near_first[row] + wrap_first[row] + on_first[row]

    def second(row):
        carry_ref[row + CUT] = near_second[row] + wrap_second[row] + on_second[row]

    rows_loop(0, CUT, 4, first)
    rows_loop(0, ROWS - CUT, 4, second)


def sum_kernel(*refs):
    def each(row):
        total = refs[0][row]
        for ref in refs[1:-1]:
            total = total + ref[row]
        refs[-1][row] = total

    rows_loop(0, ROWS, GROUP, each)


def finish_kernel(
    column_ref,
    base_ref,
    deviation_ref,
    own_ref,
    other_ref,
    received_ref,
    out_ref,
    out_rows,
    done,
):
    is_first = place() % 2 == 0

    def each(row):
        received = received_ref[row]
        earlier = own_ref[row] + other_ref[row]
        earlier = earlier + jnp.where(is_first, jnp.zeros_like(received), received)
        deviation = deviation_ref[row]
        for sub in range(SUBS):
            filtered = jnp.concatenate(
                [
                    jnp.concatenate(
                        [column_ref[sub * 16 + pair * 8 + tile, row] for tile in range(TILES)],
                        axis=1,
                    )
                    for pair in range(2)
                ],
                axis=0,
            )
            out_rows[row, sub] = deviation * filtered + (base_ref[row, sub] + earlier)

    def copy(group):
        rows = group_rows(group)
        return pltpu.make_async_copy(out_rows.at[rows], out_ref.at[rows], done.at[group])

    rows_loop(0, ROWS, GROUP, each, lambda group: copy(group).start())

    @pl.loop(0, GROUPS)
    def _(group):
        copy(group).wait()


def body(
    dual_state,
    obs_dual,
    increment,
    wind_east,
    wind_north,
    deviation,
    merid_filter,
    obs_weight,
    obs_error,
):
    size = lax.axis_size("space")
    upward = [(i, i + 1) for i in range(size - 1)]
    downward = [(i + 1, i) for i in range(size - 1)]
    following = [(i, i + 1) for i in range(2 * CHIPS - 1)]
    swap = [(i, i ^ 1) for i in range(2 * CHIPS)]

    def by_core(first, second):
        return [(2 * a, 2 * b) for a, b in first] + [(2 * a + 1, 2 * b + 1) for a, b in second]

    rise = [(c, c + 1) for c in range(CHIPS - 1)]
    fall = [(c + 1, c) for c in range(CHIPS - 1)]
    ends = (0, CHIPS - 1)
    whole, half = field(ROWS, SUBS, FIELDS, LON), field(ROWS, FIELDS, LON)

    to_north, to_south, winds, ahead, _ = edges(increment, dual_state, wind_east, wind_north)
    low = lax.ppermute(to_north, "space", upward)
    high = lax.ppermute(to_south, "space", downward)
    ahead = lax.ppermute(ahead, "tm", following)
    extended = pltpu.VMEM((ROWS + 4, 8, LON), F32)
    whole_rows = pltpu.VMEM((ROWS, SUBS, FIELDS, LON), F32)
    own_rows, third, token = call(
        third_kernel,
        [field(ROWS, 8, LON), whole],
        [dual_state, obs_dual, obs_weight],
        flops=4 * ROWS * 8 * LON,
    )
    rim, _ = call(rim_kernel, [field(8, LON)], [low, high], after=[token])
    rim = lax.ppermute(rim, "tm", following)
    dual_base, dual_sums, keep, send, _ = call(
        adjoint_kernel,
        [whole, whole, half, half],
        [own_rows, third, winds, low, high, ahead, rim],
        [extended] * 5,
        flops=60 * ROWS * 8 * LON,
    )

    received = lax.ppermute(send, "tm", swap)
    total_first, total_second, token = call(
        total_kernel,
        [field(CUT, FIELDS, LON), field(ROWS - CUT, FIELDS, LON)],
        [keep, received],
        flops=ROWS * 4 * LON,
    )
    near_first = lax.ppermute(total_first, "tm", by_core(fall, rise))
    near_second = lax.ppermute(total_second, "tm", by_core(fall, rise))
    wrap_first = lax.ppermute(total_first, "tm", by_core([ends[::-1]], [ends]))
    wrap_second = lax.ppermute(total_second, "tm", by_core([ends[::-1]], [ends]))

    square = pltpu.VMEM((LAT, LAT), BF16)

    def square_half(begin, after):
        return call(
            functools.partial(square_kernel, begin),
            [jax.ShapeDtypeStruct((BLOCK, LAT), BF16)] * 2,
            [merid_filter],
            [square] * 2,
            after=after,
            flops=0,
            size=0,
        )

    first_high, first_low, token = square_half(0, [token])
    near_first = hold(near_first, [token])
    on_first = lax.ppermute(near_first, "tm", by_core(fall[:2], rise[1:]))
    model_base, model_total, token = call(
        tangent_kernel,
        [whole, half],
        [increment, low, high, winds],
        [extended] * 4,
        after=[near_first],
        flops=40 * ROWS * 8 * LON,
    )
    near_second = hold(near_second, [token])
    on_second = lax.ppermute(near_second, "tm", by_core(fall[:2], rise[1:]))
    second_high, second_low, token = square_half(BLOCK, [near_second])
    model_received = lax.ppermute(model_total, "tm", swap)

    carry, _ = call(
        carry_kernel,
        [half],
        [near_first, near_second, wrap_first, wrap_second, on_first, on_second],
        after=[token],
        flops=2 * ROWS * 4 * LON,
    )
    other = lax.ppermute(carry, "tm", swap)

    precond_dual, columns, model_chip, token = call(
        spread_kernel,
        [whole, field(SPACE, ROWS, 2, LANES), half],
        [
            dual_base,
            dual_sums,
            deviation,
            carry,
            received,
            other,
            model_total,
            model_received,
        ],
        flops=10 * ROWS * 8 * LON,
    )

    columns = lax.all_to_all(columns, "space", split_axis=0, concat_axis=0, tiled=True)
    model_near = lax.ppermute(model_chip, "tm", by_core([ends], rise))

    precond_obs, token = call(
        obs_kernel,
        [whole],
        [obs_dual, increment, obs_weight, obs_error],
        [whole_rows] * 5
        + [pltpu.SemaphoreType.DMA((4, GROUPS)), pltpu.SemaphoreType.DMA((GROUPS,))],
        after=[precond_dual],
        flops=OBS_FLOPS,
        far_ins=(0, 1, 2, 3),
        far_outs=(0,),
        limit=WHOLE_VMEM,
    )

    columns, token = call(
        filter_kernel,
        [field(2 * LAT, LANES)],
        [first_high, first_low, second_high, second_low, columns.reshape(2 * LAT, LANES)],
        [square] * 2
        + [pltpu.VMEM((2 * LAT, LANES), F32)]
        + [pltpu.VMEM((LAT, 2 * LANES), BF16)] * 2
        + [pltpu.VMEM((2 * LAT, LANES), F32), pltpu.SemaphoreType.DMA((3, LAT // BLOCK))]
        + [pltpu.SemaphoreType.DMA((LAT // BLOCK,))],
        after=[token, model_near],
        flops=6 * LAT * LAT * 2 * LANES,
        far_ins=(0, 1, 2, 3, 4),
        far_outs=(0,),
        limit=63 * 1024 * 1024,
    )
    columns = lax.all_to_all(
        columns.reshape(SPACE, ROWS, 2, LANES), "space", split_axis=0, concat_axis=0, tiled=True
    )

    model_on = lax.ppermute(model_near, "tm", by_core([], rise[1:]))
    model_carry, _ = call(
        sum_kernel, [half], [model_near, model_on], after=[token], flops=SUM_FLOPS
    )
    model_other = lax.ppermute(model_carry, "tm", swap)

    precond_increment, _ = call(
        finish_kernel,
        [whole],
        [columns, model_base, deviation, model_carry, model_other, model_received],
        [whole_rows, pltpu.SemaphoreType.DMA((GROUPS,))],
        flops=4 * ROWS * 8 * LON,
        far_outs=(0,),
    )
    return (precond_dual, precond_obs, precond_increment)


def solution(mesh):
    banded = P("space", "tm", None, None)
    placed = (
        banded,
        banded,
        banded,
        P("space", "tm", None),
        P("space", "tm", None),
        P("space", None, None),
        P(),
        banded,
        banded,
    )
    return jax.shard_map(
        body,
        mesh=mesh,
        in_specs=placed,
        out_specs=(banded, banded, banded),
        check_vma=False,
    )
```
